32 devices in a mesh: dp: 8 (over z, y), expert: 4 (over x, core).
Axes of the slice: x: 2, y: 2, z: 4, core: 2. Of those that a mesh axis runs over, the one named last changes fastest.
Arguments:
- model_predictions: bfloat16 [4, 4096, 4416], P('expert', 'dp'), may hold values from -18 to 18
- member_tile_presence: int32 [4, 4096], P('expert', 'dp'), may hold values 0 or 1
- piece_usable_flags: int32 [4096], P(('dp', 'expert')), may hold values from 0 to 1, as said below
- horizon_positions: int32 [8], P('dp'), may hold values from 0 to 7, as said below
- result_adjoint: bfloat16 [4096, 4416], P(('dp', 'expert')), may hold values from -6 to 6
- tile_lift_matrix: bfloat16 [4416, 768], replicated, may hold values from -0.09375 to 0.09375
- tile_lift_offset: bfloat16 [768], replicated, may hold values from -3 to 3
- horizon_lookup: bfloat16 [8, 768], replicated, may hold values from -3 to 3
- normalizer_scales: bfloat16 [3, 768], replicated, may hold values from 0.5 to 1.5
- normalizer_offsets: bfloat16 [3, 768], replicated, may hold values from -1.25 to 1.25
- query_key_value_matrix: bfloat16 [768, 2304], replicated, may hold values from -0.21875 to 0.21875
- attend_result_matrix: bfloat16 [768, 768], replicated, may hold values from -3 to 3
- attend_offset_vector: bfloat16 [768], replicated, may hold values from -1.75 to 1.75
- expand_matrix: bfloat16 [768, 3072], replicated, may hold values from -0.21875 to 0.21875
- expand_offset: bfloat16 [3072], replicated, may hold values from -1.75 to 1.75
- contract_matrix: bfloat16 [3072, 768], replicated, may hold values from -0.21875 to 0.21875
- contract_offset: bfloat16 [768], replicated, may hold values from -1.75 to 1.75
- mixing_head_matrix: bfloat16 [768, 276], replicated, may hold values from -0.15625 to 0.15625
- mixing_head_offset: bfloat16 [276], replicated, may hold values from -0.625 to 0.625
Outputs:
- combined_prediction: bfloat16 [4096, 4416], P(('dp', 'expert'))
- model_predictions_slope: bfloat16 [4, 4096, 4416], P('expert', 'dp')
- sublevel_magnitudes: float32 [4], replicated
- tile_lift_matrix_slope: float32 [4416, 768], P('dp')
- tile_lift_offset_slope: float32 [768], replicated
- horizon_lookup_slope: float32 [8, 768], replicated
- normalizer_scales_slope: float32 [3, 768], replicated
- normalizer_offsets_slope: float32 [3, 768], replicated
- query_key_value_slope: float32 [768, 2304], P('dp')
- attend_result_slope: float32 [768, 768], P('dp')
- attend_offset_slope: float32 [768], replicated
- expand_matrix_slope: float32 [768, 3072], P('dp')
- expand_offset_slope: float32 [3072], replicated
- contract_matrix_slope: float32 [3072, 768], P('dp')
- contract_offset_slope: float32 [768], replicated
- mixing_head_matrix_slope: float32 [768, 276], P('dp')
- mixing_head_offset_slope: float32 [276], replicated
The draws below stay inside these ranges and needn't reach their ends.
Inputs may be any that keep to these rules, and one draw needn't show every extreme that they name: `piece_usable_flags`: the first patch of every frame is valid. `horizon_positions`: some frame has lead 0 and some frame has lead 8 - 1.
All inputs are finite; a program needn't handle non-finite values. No bound on the sum of `member_tile_presence` on one device may be relied on, other than what follows from the above.
Results may differ from the reference program's by a relative error of at most 0.015.
Values may be sent and summed in bfloat16 or wider, within the bound.
No kernel may reach another device: no remote copies, remote signals or barrier semaphores. Data moves between devices by JAX's collectives and lax.ppermute only.
A program may use at most 192 MiB of HBM per device.

```python
import jax
import jax.numpy as jnp
from jax import lax

D = 768
HEADS = 12
HEAD_DIM = 64
FF = 3072
MODEL_TALLY = 3
CHANNELS = 69
PIXELS = 64
LEADS = 8
SNAPSHOT_TILES = 512
SNAPSHOTS = 8
GROUP_PIECES = 4096
TILE_ENTRIES = 4416
HEAD_OUT = 276


def draw_model_predictions(key, part):
    frame_pos = jnp.arange(GROUP_PIECES) // SNAPSHOT_TILES
    rising = frame_pos.astype(jnp.float32) / max(SNAPSHOTS - 1, 1)
    random_part = jnp.clip(jax.random.normal(key, (MODEL_TALLY + 1, GROUP_PIECES, TILE_ENTRIES), jnp.float32), -6.0, 6.0)
    spread = 1.0 + 2.0 * rising
    return (random_part * spread[None, :, None]).astype(jnp.bfloat16)


def draw_piece_usable_flags(key, part):
    positions = jnp.arange(GROUP_PIECES)
    frame_pos = positions // SNAPSHOT_TILES
    widest = max(SNAPSHOTS - 1, 1)
    drawn_ints = jax.random.randint(key, (GROUP_PIECES,), 0, 3 * widest)
    chosen = drawn_ints < widest + 2 * frame_pos
    leading = positions % SNAPSHOT_TILES == 0
    return jnp.where(chosen | leading, 1, 0).astype(jnp.int32)


def draw_horizon_positions(key, part):
    picked = jax.random.randint(jax.random.fold_in(key, 1), (SNAPSHOTS,), 0, LEADS)
    places = jax.random.permutation(jax.random.fold_in(key, 2), SNAPSHOTS)
    picked = picked.at[places[0]].set(0)
    picked = picked.at[places[1]].set(LEADS - 1)
    return picked.astype(jnp.int32)


def with_ends(entries, rng, low, largest):
    shape = entries.shape
    place = [jax.random.randint(jax.random.fold_in(rng, axis), (), 0, shape[axis]) for axis in range(len(shape))]
    entries = entries.at[tuple(place)].set(low)
    longest = shape.index(max(shape))
    place[longest] = (place[longest] + 1) % shape[longest]
    return entries.at[tuple(place)].set(largest)


def levels(key, extent, cuts, low, largest):
    factor_of, own = 1.0, jax.random.fold_in(key, 6)
    for dim, parts in cuts:
        draws = jnp.exp(jax.random.uniform(jax.random.fold_in(own, dim), (parts,), jnp.float32, low / len(cuts), largest / len(cuts)))
        factor_of = factor_of * jnp.repeat(draws, extent[dim] // parts).reshape([-1 if axis == dim else 1 for axis in range(len(extent))])
    return factor_of


def noise(rng, extent, width, reach, split=(), held_as=jnp.bfloat16):
    entries = width * jax.random.normal(rng, extent, jnp.float32)
    if split:
        entries = entries * levels(rng, extent, split, -0.22, 0.18)
    return jnp.clip(entries, -reach, reach).astype(held_as)


def setup_inputs(seed: int = 0) -> dict:
    keys = jax.random.split(jax.random.key(seed), 20)
    model_predictions = draw_model_predictions(jax.random.fold_in(keys[19], 71), 0)
    member_tile_presence = with_ends((jax.random.randint(keys[1], (MODEL_TALLY + 1, GROUP_PIECES), 0, 8) < 7).astype(jnp.int32), jax.random.fold_in(keys[1], 1), 0, 1)
    piece_usable_flags = draw_piece_usable_flags(jax.random.fold_in(keys[19], 71), 0)
    horizon_positions = draw_horizon_positions(jax.random.fold_in(keys[19], 71), 0)
    result_adjoint = noise(keys[4], (GROUP_PIECES, TILE_ENTRIES), 1.0, 6.0, ((0, 32),))
    tile_lift_matrix = noise(keys[5], (TILE_ENTRIES, D), TILE_ENTRIES ** -0.5, 0.09375)
    tile_lift_offset = noise(keys[6], (D,), 0.5, 3.0)
    horizon_lookup = noise(keys[7], (LEADS, D), 0.5, 3.0)
    normalizer_scales = jnp.clip(1.0 + 0.1 * jax.random.normal(keys[8], (3, D), jnp.float32), 0.5, 1.5).astype(jnp.bfloat16)
    normalizer_offsets = noise(keys[9], (3, D), 0.2, 1.25)
    query_key_value_matrix = noise(keys[10], (D, 3 * D), D ** -0.5, 0.21875)
    attend_result_matrix = noise(keys[11], (D, D), (max(D // 192, 1)) ** -0.5, 3.0)
    attend_offset_vector = noise(keys[12], (D,), 0.3, 1.75)
    expand_matrix = noise(keys[13], (D, FF), D ** -0.5, 0.21875)
    expand_offset = noise(keys[14], (FF,), 0.3, 1.75)
    contract_matrix = noise(keys[15], (FF, D), (FF // 4) ** -0.5, 0.21875)
    contract_offset = noise(keys[16], (D,), 0.3, 1.75)
    mixing_head_matrix = noise(keys[17], (D, HEAD_OUT), (2 * D) ** -0.5, 0.15625)
    mixing_head_offset = noise(keys[18], (HEAD_OUT,), 0.1, 0.625)
    return dict(model_predictions=model_predictions, member_tile_presence=member_tile_presence, piece_usable_flags=piece_usable_flags, horizon_positions=horizon_positions, result_adjoint=result_adjoint, tile_lift_matrix=tile_lift_matrix, tile_lift_offset=tile_lift_offset, horizon_lookup=horizon_lookup, normalizer_scales=normalizer_scales, normalizer_offsets=normalizer_offsets, query_key_value_matrix=query_key_value_matrix, attend_result_matrix=attend_result_matrix, attend_offset_vector=attend_offset_vector, expand_matrix=expand_matrix, expand_offset=expand_offset, contract_matrix=contract_matrix, contract_offset=contract_offset, mixing_head_matrix=mixing_head_matrix, mixing_head_offset=mixing_head_offset)


NORM_EPSILON = 1e-05
SQUARE_EPSILON = 1e-06
MASKED_SCORE = -1e+30
HIGHEST_PRECISION = lax.Precision.HIGHEST

@jax.custom_vjp
def low(v):
    return lax.optimization_barrier(v.astype(jnp.bfloat16)).astype(jnp.float32)

@jax.custom_vjp
def low_back(v):
    return v

def low_keep(v):
    return (low(v), None)

def low_pass(kept, grad):
    return (grad,)

def back_keep(v):
    return (v, None)

def back_low(kept, grad):
    return (low(grad),)
low.defvjp(low_keep, low_pass)
low_back.defvjp(back_keep, back_low)

def layer_norm(values, gain_row, offset_row):
    center = values - lax.optimization_barrier(jnp.mean(values, axis=-1, keepdims=True))
    inverse = lax.rsqrt(lax.optimization_barrier(jnp.mean(center * center, axis=-1, keepdims=True)) + NORM_EPSILON)
    return center * inverse * gain_row + offset_row

def matmul(former, latter):
    return jnp.dot(former, latter, precision=HIGHEST_PRECISION)

def softmax_over(values, axis_index):
    maxima = lax.optimization_barrier(jnp.max(values, axis=axis_index, keepdims=True))
    powers = jnp.exp(values - maxima)
    return powers / lax.optimization_barrier(jnp.sum(powers, axis=axis_index, keepdims=True))

def square_sum(values, usable_snapshot):
    return jnp.sum(lax.optimization_barrier(jnp.sum(values * values, axis=-1)) * usable_snapshot)

def snapshot_primal(parameter_set, prediction_snapshot, presence_snapshot, usable_snapshot, horizon_position):
    tile_lift_matrix, tile_lift_offset, horizon_lookup, normalizer_scales, normalizer_offsets, query_key_value_matrix, attend_result_matrix, attend_offset_vector, expand_matrix, expand_offset, contract_matrix, contract_offset, mixing_head_matrix, mixing_head_offset = parameter_set
    tiles_present = prediction_snapshot.shape[1]
    present_prediction = prediction_snapshot[:MODEL_TALLY]
    embed_parts = jnp.einsum('epf,fd->epd', present_prediction, tile_lift_matrix, precision=HIGHEST_PRECISION)
    embedded = low_back(lax.optimization_barrier(jnp.sum(embed_parts * presence_snapshot[:MODEL_TALLY, :, None], axis=0)))
    stream_in = embedded + tile_lift_offset
    normed_one = low(layer_norm(stream_in, normalizer_scales[0], normalizer_offsets[0]) + horizon_lookup[horizon_position])
    triple = low_back(low(matmul(normed_one, query_key_value_matrix)))
    queries = triple[:, :D].reshape(tiles_present, HEADS, HEAD_DIM)
    keys_all = triple[:, D:2 * D].reshape(tiles_present, HEADS, HEAD_DIM)
    values_all = triple[:, 2 * D:].reshape(tiles_present, HEADS, HEAD_DIM)
    raw_scores = low_back(jnp.einsum('qhd,khd->hqk', queries, keys_all, precision=HIGHEST_PRECISION))
    scores = jnp.where(usable_snapshot[None, None, :] > 0, raw_scores * HEAD_DIM ** (-0.5), MASKED_SCORE)
    chance = low(softmax_over(scores, 2))
    mixed = jnp.einsum('hqk,khd->qhd', chance, values_all, precision=HIGHEST_PRECISION)
    mixed = low_back(low(mixed)).reshape(tiles_present, D)
    attend_out = low_back(matmul(mixed, attend_result_matrix)) + attend_offset_vector
    stream_mid = stream_in + attend_out
    normed_two = low(layer_norm(stream_mid, normalizer_scales[1], normalizer_offsets[1]))
    hidden = low_back(matmul(normed_two, expand_matrix)) + expand_offset
    activated = low(jax.nn.gelu(hidden))
    feed_out = low_back(matmul(activated, contract_matrix)) + contract_offset
    stream_out = stream_mid + feed_out
    normed_three = low(layer_norm(stream_out, normalizer_scales[2], normalizer_offsets[2]))
    head_vals = low_back(matmul(normed_three, mixing_head_matrix)) + mixing_head_offset
    logits = head_vals[:, :MODEL_TALLY * CHANNELS].reshape(tiles_present, MODEL_TALLY, CHANNELS)
    shift_out = head_vals[:, MODEL_TALLY * CHANNELS:]
    blend_weights = softmax_over(logits, 1)
    wide_weights = jnp.repeat(jnp.transpose(blend_weights, (1, 0, 2)), PIXELS, axis=2)
    combined_prediction = lax.optimization_barrier(jnp.sum(wide_weights * present_prediction, axis=0)) + jnp.repeat(shift_out, PIXELS, axis=1)
    snapshot_moments = jnp.stack([square_sum(stream_in, usable_snapshot), square_sum(attend_out, usable_snapshot), square_sum(feed_out, usable_snapshot), square_sum(stream_out, usable_snapshot), jnp.sum(usable_snapshot)])
    return (combined_prediction, snapshot_moments)

def reference(model_predictions, member_tile_presence, piece_usable_flags, horizon_positions, result_adjoint, tile_lift_matrix, tile_lift_offset, horizon_lookup, normalizer_scales, normalizer_offsets, query_key_value_matrix, attend_result_matrix, attend_offset_vector, expand_matrix, expand_offset, contract_matrix, contract_offset, mixing_head_matrix, mixing_head_offset):
    parameter_set = (tile_lift_matrix.astype(jnp.float32), tile_lift_offset.astype(jnp.float32), horizon_lookup.astype(jnp.float32), normalizer_scales.astype(jnp.float32), normalizer_offsets.astype(jnp.float32), query_key_value_matrix.astype(jnp.float32), attend_result_matrix.astype(jnp.float32), attend_offset_vector.astype(jnp.float32), expand_matrix.astype(jnp.float32), expand_offset.astype(jnp.float32), contract_matrix.astype(jnp.float32), contract_offset.astype(jnp.float32), mixing_head_matrix.astype(jnp.float32), mixing_head_offset.astype(jnp.float32))

    def snapshot_advance(running, frame_index):
        derivative_total, moment_total = running
        first_piece = (frame_index * SNAPSHOT_TILES).astype(jnp.int32)
        prediction_snapshot = lax.dynamic_slice_in_dim(model_predictions, first_piece, SNAPSHOT_TILES, 1).astype(jnp.float32)
        presence_snapshot = lax.dynamic_slice_in_dim(member_tile_presence, first_piece, SNAPSHOT_TILES, 1).astype(jnp.float32)
        usable_snapshot = lax.dynamic_slice_in_dim(piece_usable_flags, first_piece, SNAPSHOT_TILES, 0).astype(jnp.float32)
        cotangent = lax.dynamic_slice_in_dim(result_adjoint, first_piece, SNAPSHOT_TILES, 0).astype(jnp.float32)
        horizon_position = lax.dynamic_index_in_dim(horizon_positions, frame_index, 0, keepdims=False)

        def primal_pass(params_in, fore_in):
            return snapshot_primal(params_in, fore_in, presence_snapshot, usable_snapshot, horizon_position)
        combined_prediction, adjoint_map, snapshot_moments = jax.vjp(primal_pass, parameter_set, prediction_snapshot, has_aux=True)
        grad_params, grad_fore = adjoint_map(cotangent)
        derivative_total = jax.tree.map(lambda summed, addend: summed + addend, derivative_total, grad_params)
        return ((derivative_total, moment_total + snapshot_moments), (combined_prediction.astype(jnp.bfloat16), grad_fore.astype(jnp.bfloat16)))
    initial_carry = (jax.tree.map(jnp.zeros_like, parameter_set), jnp.zeros((5,), jnp.float32))
    (derivative_total, moment_total), (mixture_snapshots, prediction_slopes) = lax.scan(snapshot_advance, initial_carry, jnp.arange(SNAPSHOTS, dtype=jnp.int32))
    combined_prediction = mixture_snapshots.reshape(GROUP_PIECES, TILE_ENTRIES)
    model_predictions_slope = jnp.transpose(prediction_slopes, (1, 0, 2, 3)).reshape(MODEL_TALLY + 1, GROUP_PIECES, TILE_ENTRIES)
    sublevel_magnitudes = jnp.sqrt(moment_total[:4] / (moment_total[4] * D) + SQUARE_EPSILON)
    tile_lift_matrix_slope, tile_lift_offset_slope, horizon_lookup_slope, normalizer_scales_slope, normalizer_offsets_slope, query_key_value_slope, attend_result_slope, attend_offset_slope, expand_matrix_slope, expand_offset_slope, contract_matrix_slope, contract_offset_slope, mixing_head_matrix_slope, mixing_head_offset_slope = derivative_total
    return (combined_prediction, model_predictions_slope, sublevel_magnitudes, tile_lift_matrix_slope, tile_lift_offset_slope, horizon_lookup_slope, normalizer_scales_slope, normalizer_offsets_slope, query_key_value_slope, attend_result_slope, attend_offset_slope, expand_matrix_slope, expand_offset_slope, contract_matrix_slope, contract_offset_slope, mixing_head_matrix_slope, mixing_head_offset_slope)
```

```python
import jax
import jax.numpy as jnp
from jax import lax
from jax.sharding import PartitionSpec as P

D = 768
HEADS = 12
HEAD_DIM = 64
MODEL_TALLY = 3
CHANNELS = 69
PIXELS = 64
TILE_ENTRIES = 4416

NORM_EPSILON = 1e-05
SQUARE_EPSILON = 1e-06
MASKED_SCORE = -1e30
F32 = jnp.float32
BF16 = jnp.bfloat16


def normalize(values, gain_row, offset_row):
    center = values - jnp.mean(values, axis=-1, keepdims=True)
    inverse = lax.rsqrt(jnp.mean(center * center, axis=-1, keepdims=True) + NORM_EPSILON)
    unit_rows = center * inverse
    return (unit_rows * gain_row + offset_row, unit_rows, inverse)


def normalize_back(grad_out, unit_rows, inverse, gain_row):
    scaled = grad_out * gain_row
    grad_in = inverse * (
        scaled
        - jnp.mean(scaled, axis=-1, keepdims=True)
        - unit_rows * jnp.mean(scaled * unit_rows, axis=-1, keepdims=True)
    )
    return (grad_in, jnp.sum(grad_out * unit_rows, axis=0), jnp.sum(grad_out, axis=0))


def dot_nn(a, b):
    return jnp.dot(a, b, preferred_element_type=F32)


def dot_tn(a, b):
    return lax.dot_general(a, b, (((0,), (0,)), ((), ())), preferred_element_type=F32)


def dot_nt(a, b):
    return lax.dot_general(a, b, (((1,), (1,)), ((), ())), preferred_element_type=F32)


def expert_swap(v, k):
    size = lax.axis_size("expert")
    return lax.ppermute(v, "expert", [(i, i ^ k) for i in range(size)])


def frame_swap(v, k):
    size = lax.axis_size("dp")
    return lax.ppermute(v, "dp", [(i, i ^ k) for i in range(size)])


def gather_four(v):
    across = expert_swap(v, 2)
    pair = jnp.stack([v, across])
    other = expert_swap(pair, 1)
    return [v, other[0], across, other[1]]


def in_order(parts, e):
    odd = (e & 1) == 1
    high = (e & 2) == 2
    a, b, c, d = parts
    a, b, c, d = (
        jnp.where(odd, b, a),
        jnp.where(odd, a, b),
        jnp.where(odd, d, c),
        jnp.where(odd, c, d),
    )
    return [jnp.where(high, c, a), jnp.where(high, d, b), jnp.where(high, a, c), jnp.where(high, b, d)]


def frame_scatter(blocks):
    n, rows, cols = blocks.shape
    steps = n.bit_length() - 1
    me = lax.axis_index("dp")
    now = blocks.reshape((2,) * steps + (rows, cols))
    for i in range(steps):
        bit = (me >> i) & 1
        axis = steps - 1 - i
        send = lax.dynamic_index_in_dim(now, 1 - bit, axis, keepdims=False)
        keep = lax.dynamic_index_in_dim(now, bit, axis, keepdims=False)
        got = frame_swap(send, 1 << i)
        now = (keep.astype(F32) + got.astype(F32)).astype(BF16)
    return now


def frame_sum(v):
    steps = lax.axis_size("dp").bit_length() - 1
    for i in range(steps):
        v = v + frame_swap(v, 1 << i)
    return v


def square_sum(values, valid_rows):
    return jnp.sum(jnp.sum(values * values, axis=-1) * valid_rows)


def local(
    model_predictions,
    member_tile_presence,
    piece_usable_flags,
    horizon_positions,
    result_adjoint,
    tile_lift_matrix,
    tile_lift_offset,
    horizon_lookup,
    normalizer_scales,
    normalizer_offsets,
    query_key_value_matrix,
    attend_result_matrix,
    attend_offset_vector,
    expand_matrix,
    expand_offset,
    contract_matrix,
    contract_offset,
    mixing_head_matrix,
    mixing_head_offset,
):
    n = lax.axis_size("dp")
    e = lax.axis_index("expert")
    core = e & 1
    active = (e < MODEL_TALLY).astype(F32)
    pred = model_predictions[0]
    tokens = pred.shape[0]
    own = result_adjoint.shape[0]
    half = tokens // 2
    block_rows = TILE_ENTRIES // n
    step = block_rows // 4 // 8 * 8 if block_rows % 8 == 0 else block_rows // 4
    width = block_rows - 3 * step

    mask = member_tile_presence[0].astype(F32) * active
    info = jnp.concatenate([mask, piece_usable_flags.astype(F32)])[None]
    infos = in_order(gather_four(info), e)
    masks = [v[0, :tokens] for v in infos]
    valid = jnp.concatenate([v[0, tokens:] for v in infos])

    adjoints = in_order(gather_four(result_adjoint), e)
    adjoint = jnp.concatenate(adjoints, axis=0)

    part = (dot_nn(pred, tile_lift_matrix) * mask[:, None]).astype(BF16)
    other = expert_swap(part, 1)
    pair_sum = (part.astype(F32) + other.astype(F32)).astype(BF16)
    across = expert_swap(lax.dynamic_slice_in_dim(pair_sum, core * half, half, 0), 2)
    across_other = expert_swap(across, 1)
    far = jnp.where(
        core == 0,
        jnp.concatenate([across, across_other], axis=0),
        jnp.concatenate([across_other, across], axis=0),
    )
    stream_in = pair_sum.astype(F32) + far.astype(F32) + tile_lift_offset.astype(F32)

    blocked = pred.reshape(tokens, n, block_rows)
    pieces = [
        blocked[:, :, q * step : q * step + width].reshape(tokens, n * width) for q in range(4)
    ]
    pieces = in_order(pieces, e)
    columns = [pieces[0]] + [expert_swap(pieces[k], k) for k in (1, 2, 3)]
    columns = in_order(columns, e)[:MODEL_TALLY]

    gain_rows = normalizer_scales.astype(F32)
    shift_rows = normalizer_offsets.astype(F32)
    lead_hot = (jnp.arange(horizon_lookup.shape[0]) == horizon_positions[0]).astype(BF16)
    lead_vector = dot_nn(lead_hot, horizon_lookup)
    normed, unit_one, inverse_one = normalize(stream_in, gain_rows[0], shift_rows[0])
    normed_one = (normed + lead_vector).astype(BF16)
    triple = dot_nn(normed_one, query_key_value_matrix).astype(BF16)
    queries = triple[:, :D].reshape(tokens, HEADS, HEAD_DIM)
    keys_all = triple[:, D : 2 * D].reshape(tokens, HEADS, HEAD_DIM)
    values_all = triple[:, 2 * D :].reshape(tokens, HEADS, HEAD_DIM)

    def masked_scores():
        raw = jnp.einsum("qhd,khd->hqk", queries, keys_all, preferred_element_type=F32)
        return jnp.where(valid[None, None, :] > 0, raw * HEAD_DIM ** (-0.5), MASKED_SCORE)

    scores = masked_scores()
    maxima = jnp.max(scores, axis=-1, keepdims=True)
    log_norm = maxima + jnp.log(jnp.sum(jnp.exp(scores - maxima), axis=-1, keepdims=True))
    chance = jnp.exp(scores - log_norm)
    mixed = jnp.einsum("hqk,khd->qhd", chance.astype(BF16), values_all, preferred_element_type=F32)
    mixed = mixed.astype(BF16).reshape(tokens, D)
    attend_out = dot_nn(mixed, attend_result_matrix) + attend_offset_vector.astype(F32)
    stream_mid = stream_in + attend_out
    normed, unit_two, inverse_two = normalize(stream_mid, gain_rows[1], shift_rows[1])
    normed_two = normed.astype(BF16)
    hidden = dot_nn(normed_two, expand_matrix) + expand_offset.astype(F32)
    activated = jax.nn.gelu(hidden).astype(BF16)
    feed_out = dot_nn(activated, contract_matrix) + contract_offset.astype(F32)
    stream_out = stream_mid + feed_out
    normed, unit_three, inverse_three = normalize(stream_out, gain_rows[2], shift_rows[2])
    normed_three = normed.astype(BF16)
    head_vals = dot_nn(normed_three, mixing_head_matrix) + mixing_head_offset.astype(F32)
    logits = head_vals[:, : MODEL_TALLY * CHANNELS].reshape(tokens, MODEL_TALLY, CHANNELS)
    shift_out = head_vals[:, MODEL_TALLY * CHANNELS :]
    powers = jnp.exp(logits - jnp.max(logits, axis=1, keepdims=True))
    blend = powers / jnp.sum(powers, axis=1, keepdims=True)

    place = jnp.arange(n * width)
    channel = ((place // width) * block_rows + e * step + place % width) // PIXELS
    spread = (jnp.arange(CHANNELS)[:, None] == channel[None, :]).astype(F32)

    def wide(v, spread):
        return jnp.dot(v, spread, precision=lax.Precision.HIGHEST)

    combined = wide(shift_out, spread)
    for q in range(MODEL_TALLY):
        combined = combined + wide(blend[:, q], spread) * columns[q].astype(F32)
    combined = combined.astype(BF16).reshape(4, own, n * width)
    outgoing = in_order([combined[k] for k in range(4)], e)
    arrived = [outgoing[0]] + [expert_swap(outgoing[k], k) for k in (1, 2, 3)]
    arrived = [v.reshape(own, n, width) for v in in_order(arrived, e)]
    combined_prediction = jnp.concatenate(
        [v[:, :, :step] for v in arrived[:3]] + [arrived[3]], axis=2
    ).reshape(own, TILE_ENTRIES)

    adjoint_wide = adjoint.astype(F32)
    mine = jnp.sum(
        (adjoint_wide * pred.astype(F32)).reshape(tokens, CHANNELS, PIXELS), axis=-1
    )
    grad_weights = jnp.stack(in_order(gather_four(mine), e)[:MODEL_TALLY], axis=1)
    grad_shift = jnp.sum(adjoint_wide.reshape(tokens, CHANNELS, PIXELS), axis=-1)
    grad_logits = blend * (grad_weights - jnp.sum(blend * grad_weights, axis=1, keepdims=True))
    grad_head = jnp.concatenate([grad_logits.reshape(tokens, MODEL_TALLY * CHANNELS), grad_shift], axis=1)
    head_bias_grad = jnp.sum(grad_head, axis=0)
    head_low = grad_head.astype(BF16)

    def quarter(v):
        cols = v.shape[1] // 4
        return lax.dynamic_slice_in_dim(v, e * cols, cols, 1)

    def by_frame(g):
        return g.astype(BF16).reshape(n, g.shape[0] // n, g.shape[1])

    head_share = by_frame(dot_tn(normed_three, quarter(head_low)))
    grad_normed_three = dot_nt(head_low, mixing_head_matrix)
    grad_stream_out, gain_three, shift_three = normalize_back(
        grad_normed_three, unit_three, inverse_three, gain_rows[2]
    )
    contract_bias_grad = jnp.sum(grad_stream_out, axis=0)
    feed_low = grad_stream_out.astype(BF16)
    contract_share = by_frame(dot_tn(activated, quarter(feed_low)))
    grad_activated = dot_nt(feed_low, contract_matrix)
    _, gelu_back = jax.vjp(jax.nn.gelu, hidden)
    grad_hidden = gelu_back(grad_activated)[0]
    expand_bias_grad = jnp.sum(grad_hidden, axis=0)
    hidden_low = grad_hidden.astype(BF16)
    expand_share = by_frame(dot_tn(normed_two, quarter(hidden_low)))
    grad_normed_two = dot_nt(hidden_low, expand_matrix)
    grad_mid_norm, gain_two, shift_two = normalize_back(
        grad_normed_two, unit_two, inverse_two, gain_rows[1]
    )
    grad_stream_mid = grad_stream_out + grad_mid_norm
    attend_bias_grad = jnp.sum(grad_stream_mid, axis=0)
    attend_low = grad_stream_mid.astype(BF16)
    result_share = by_frame(dot_tn(mixed, quarter(attend_low)))
    grad_mixed = dot_nt(attend_low, attend_result_matrix).astype(BF16).reshape(tokens, HEADS, HEAD_DIM)
    grad_values = jnp.einsum("hqk,qhd->khd", chance.astype(BF16), grad_mixed, preferred_element_type=F32)
    grad_chance = jnp.einsum("qhd,khd->hqk", grad_mixed, values_all, preferred_element_type=F32)
    delta_rows = jnp.sum(chance * grad_chance, axis=-1, keepdims=True)
    grad_scores = (chance * (grad_chance - delta_rows) * HEAD_DIM ** (-0.5)).astype(BF16)
    grad_queries = jnp.einsum("hqk,khd->qhd", grad_scores, keys_all, preferred_element_type=F32)
    grad_keys = jnp.einsum("hqk,qhd->khd", grad_scores, queries, preferred_element_type=F32)
    grad_triple = jnp.concatenate(
        [v.reshape(tokens, D) for v in (grad_queries, grad_keys, grad_values)], axis=1
    ).astype(BF16)
    triple_share = by_frame(dot_tn(normed_one, quarter(grad_triple)))
    grad_normed_one = dot_nt(grad_triple, query_key_value_matrix)
    lead_grad = lead_hot.astype(F32)[:, None] * jnp.sum(grad_normed_one, axis=0)[None, :]
    grad_in_norm, gain_one, shift_one = normalize_back(
        grad_normed_one, unit_one, inverse_one, gain_rows[0]
    )
    grad_stream_in = grad_stream_mid + grad_in_norm
    lift_bias_grad = jnp.sum(grad_stream_in, axis=0)
    embed_low = grad_stream_in.astype(BF16)

    lift_part = 0.0
    for q in range(MODEL_TALLY):
        lift_part = lift_part + dot_tn(columns[q], embed_low * masks[q].astype(BF16)[:, None])
    lift_share = lift_part.astype(BF16).reshape(n, width, D)

    own_blend = jnp.where(e == 0, blend[:, 0], jnp.where(e == 1, blend[:, 1], blend[:, 2])) * active
    natural = (
        jnp.arange(CHANNELS)[:, None] == (jnp.arange(TILE_ENTRIES) // PIXELS)[None, :]
    ).astype(F32)
    predictions_slope = (
        dot_nt(embed_low * mask.astype(BF16)[:, None], tile_lift_matrix)
        + wide(own_blend, natural) * adjoint_wide
    ).astype(BF16)[None]

    def finish(share):
        return in_order(gather_four(frame_scatter(share)), e)

    def columns_of(share):
        return jnp.concatenate(finish(share), axis=1).astype(F32)

    head_slope = columns_of(head_share)
    contract_slope = columns_of(contract_share)
    expand_slope = columns_of(expand_share)
    result_slope = columns_of(result_share)
    triple_slope = columns_of(triple_share)
    lift_rows = finish(lift_share)
    lift_slope = jnp.concatenate([v[:step] for v in lift_rows[:3]] + [lift_rows[3]], axis=0).astype(F32)

    stats = jnp.stack(
        [square_sum(v, valid) for v in (stream_in, attend_out, feed_out, stream_out)] + [jnp.sum(valid)]
    )
    flat = [
        lift_bias_grad,
        lead_grad,
        jnp.stack([gain_one, gain_two, gain_three]),
        jnp.stack([shift_one, shift_two, shift_three]),
        attend_bias_grad,
        expand_bias_grad,
        contract_bias_grad,
        head_bias_grad,
        stats,
    ]
    sizes = [v.size for v in flat]
    packed = jnp.concatenate([v.reshape(-1) for v in flat])
    packed = jnp.pad(packed, (0, -packed.size % 1024)).reshape(-1, 128)
    packed = frame_sum(packed).reshape(-1)
    back, at = [], 0
    for v, size in zip(flat, sizes):
        back.append(packed[at : at + size].reshape(v.shape))
        at += size
    total = back[8]
    magnitudes = jnp.sqrt(total[:4] / (total[4] * D) + SQUARE_EPSILON)
    return (
        combined_prediction,
        predictions_slope,
        magnitudes,
        lift_slope,
        back[0],
        back[1],
        back[2],
        back[3],
        triple_slope,
        result_slope,
        back[4],
        expand_slope,
        back[5],
        contract_slope,
        back[6],
        head_slope,
        back[7],
    )


def solution(mesh):
    rows = P(("dp", "expert"), None)
    placed = (
        P("expert", "dp", None),
        P("expert", "dp"),
        P(("dp", "expert")),
        P("dp"),
        rows,
    ) + (P(),) * 14
    given = (
        rows,
        P("expert", "dp", None),
        P(),
        P("dp", None),
        P(),
        P(),
        P(),
        P(),
        P("dp", None),
        P("dp", None),
        P(),
        P("dp", None),
        P(),
        P("dp", None),
        P(),
        P("dp", None),
        P(),
    )
    return jax.shard_map(local, mesh=mesh, in_specs=placed, out_specs=given, check_vma=False)
```

```python
import functools

import jax
import jax.numpy as jnp
from jax import lax
from jax.experimental import pallas as pl
from jax.experimental.pallas import tpu as pltpu
from jax.sharding import PartitionSpec as P

D = 768
HEADS = 12
HEAD_DIM = 64
FF = 3072
MODEL_TALLY = 3
CHANNELS = 69
PIXELS = 64
TILE_ENTRIES = 4416
LANES = 128
PAIRS = HEADS // 2

NORM_EPSILON = 1e-05
SQUARE_EPSILON = 1e-06
MASKED_SCORE = -1e30
GELU_A = 0.7978845608028654
GELU_B = 0.044715
F32 = jnp.float32
BF16 = jnp.bfloat16

ROW_LIFT, ROW_GAIN, ROW_SHIFT, ROW_ATTEND, ROW_CONTRACT, ROW_EXPAND, ROW_LEAD, ROW_HEAD = 0, 1, 4, 7, 8, 9, 13, 14
PARAM_ROWS = 16
HEAD_ROWS = 72
VMEM_MIB = 20
VMEM_SMALL = 12

VMEM = pltpu.VMEM
SMEM = pltpu.SMEM


def whole():
    return pl.BlockSpec(memory_space=VMEM)


def scalars():
    return pl.BlockSpec(memory_space=SMEM)


def in_hbm():
    return pl.BlockSpec(memory_space=pl.ANY)


def shaped(shape, dtype):
    return jax.ShapeDtypeStruct(shape, dtype)


def dot_nn(a, b):
    return jnp.dot(a, b, preferred_element_type=F32)


def dot_tn(a, b):
    return lax.dot_general(a, b, (((0,), (0,)), ((), ())), preferred_element_type=F32)


def dot_nt(a, b):
    return lax.dot_general(a, b, (((1,), (1,)), ((), ())), preferred_element_type=F32)


def unit_of(values):
    center = values - jnp.mean(values, axis=-1, keepdims=True)
    inverse = lax.rsqrt(jnp.mean(center * center, axis=-1, keepdims=True) + NORM_EPSILON)
    return center * inverse, inverse


def norm_back(grad_out, unit, inverse, gain):
    scaled = grad_out * gain
    return inverse * (
        scaled
        - jnp.mean(scaled, axis=-1, keepdims=True)
        - unit * jnp.mean(scaled * unit, axis=-1, keepdims=True)
    )


def column_sum(v):
    return jnp.sum(v, axis=0, keepdims=True)


def taking(us):
    return pl.CostEstimate(flops=int(us*1e9), bytes_accessed=1000, transcendentals=0)


def call(
    body, inputs, in_specs, outs, scratch=(), vmem=VMEM_MIB, grid=None, out_specs=None, name=None, deps=(), us=1.0
):
    kwargs = {}
    if grid is not None:
        kwargs["grid"] = grid
    count = len(inputs)

    def kernel(*refs):
        body(*refs[:count], *refs[count + len(deps) :])

    return pl.pallas_call(
        kernel,
        out_shape=outs,
        in_specs=list(in_specs) + [in_hbm() for _ in deps],
        out_specs=out_specs if out_specs is not None else jax.tree.map(lambda _: whole(), outs),
        scratch_shapes=list(scratch),
        compiler_params=pltpu.CompilerParams(vmem_limit_bytes=vmem * 1024 * 1024),
        cost_estimate=taking(us),
        name=name,
        **kwargs,
    )(*inputs, *deps)


def hold_kernel(*refs):
    count = len(refs) // 2
    for i in range(count):
        refs[count + i][...] = refs[i][...]


def hold(arrays, deps):
    return call(
        hold_kernel,
        arrays,
        [whole() for _ in arrays],
        [shaped(v.shape, v.dtype) for v in arrays],
        vmem=VMEM_SMALL,
        name="hold",
        us=1,
        deps=deps,
    )


def embed_kernel(place_ref, mask_ref, pred_hbm, lift_hbm, own_ref, other_ref, pred, lift, acc, sems, *, cuts):
    copies = []
    for i, (a, b) in enumerate(cuts):
        one = pltpu.make_async_copy(pred_hbm.at[a:b], pred.at[a:b], sems.at[0, i])
        two = pltpu.make_async_copy(lift_hbm.at[a:b], lift.at[a:b], sems.at[1, i])
        one.start()
        two.start()
        copies.append((one, two))
    for i, (a, b) in enumerate(cuts):
        for copy in copies[i]:
            copy.wait()
        part = dot_tn(pred[a:b], lift[a:b])
        if i == 0:
            acc[...] = part
        elif i < len(cuts) - 1:
            acc[...] += part
        else:
            mask = jnp.transpose(jnp.broadcast_to(mask_ref[...], (8, mask_ref.shape[1])))[:, :1]
            acc[...] = (acc[...] + part) * mask
            half = own_ref.shape[0]
            core = place_ref[0] & 1
            own_ref[...] = acc[pl.ds(pl.multiple_of(core * half, half), half)].astype(BF16)
            other_ref[...] = acc[pl.ds(pl.multiple_of((1 - core) * half, half), half)].astype(BF16)


def embed(place, mask, pred, lift):
    tokens = pred.shape[1]
    cuts = [(0, 768), (768, 1536), (1536, 2560), (2560, 3584), (3584, TILE_ENTRIES)]
    return call(
        functools.partial(embed_kernel, cuts=cuts),
        (place, mask, pred, lift),
        [scalars(), whole(), in_hbm(), in_hbm()],
        [shaped((tokens // 2, D), BF16)] * 2,
        scratch=[
            VMEM((TILE_ENTRIES, tokens), BF16),
            VMEM((TILE_ENTRIES, D), BF16),
            VMEM((tokens, D), F32),
            pltpu.SemaphoreType.DMA((2, len(cuts))),
        ],
        name="embed",
        us=7.5,
    )


def pack_kernel(place_ref, pred_ref, *outs, n, step, width, padded):
    e = place_ref[0]
    tokens = pred_ref.shape[1]
    block = TILE_ENTRIES // n
    for here in range(4):

        @pl.when(e == here)
        def _():
            for k in range(4):
                q = here ^ k
                for d in range(n):
                    start = d * block + q * step
                    outs[k][d * padded : d * padded + width] = pred_ref[start : start + width]
                    if padded > width:
                        outs[k][d * padded + width : (d + 1) * padded] = jnp.zeros((padded - width, tokens), BF16)


def pack(place, pred, n, step, width, padded, deps=()):
    tokens = pred.shape[1]
    return call(
        functools.partial(pack_kernel, n=n, step=step, width=width, padded=padded),
        (place, pred),
        [scalars(), whole()],
        [shaped((n * padded, tokens), BF16)] * 4,
        name="pack",
        us=5,
        deps=deps,
    )


def unpack_kernel(place_ref, *refs, n, step, width, padded):
    parts, out = refs[:4], refs[4]
    e = place_ref[0]
    block = TILE_ENTRIES // n
    for here in range(4):

        @pl.when(e == here)
        def _():
            for q in range(4):
                take = step if q < 3 else width
                for d in range(n):
                    start = d * block + q * step
                    out[start : start + take] = parts[here ^ q][d * padded : d * padded + take]


def unpack(place, parts, n, step, width, padded, deps=()):
    rows = parts[0].shape[1]
    return call(
        functools.partial(unpack_kernel, n=n, step=step, width=width, padded=padded),
        (place, *parts),
        [scalars()] + [whole()] * 4,
        shaped((TILE_ENTRIES, rows), BF16),
        name="unpack",
        us=2,
        deps=deps,
    )


def lane_side(shape):
    return lax.broadcasted_iota(jnp.int32, shape, 1) // HEAD_DIM


GROUPS = 3
WIDTH = D // GROUPS


def attend_kernel(
    place_ref, own_ref, mine_ref, other_ref, across_ref, across_other_ref, bias_ref, par_ref,
    wq_ref, wk_ref, wv_ref, wo_ref,
    sin_ref, n1_ref, q_ref, k_ref, v_ref, mixed_ref, smid_ref, lse_ref, stat_ref,
):
    j = pl.program_id(0)
    core = place_ref[0] & 1
    tokens = bias_ref.shape[0]
    half = tokens // 2

    @pl.when(j == 0)
    def _():
        gain = par_ref[ROW_GAIN : ROW_GAIN + 1]
        shift = par_ref[ROW_SHIFT : ROW_SHIFT + 1] + par_ref[ROW_LEAD : ROW_LEAD + 1]
        offset = par_ref[ROW_LIFT : ROW_LIFT + 1]
        other = (mine_ref[...].astype(F32) + other_ref[...].astype(F32)).astype(BF16)
        for side, near, far in ((core, own_ref[...], across_ref), (1 - core, other, across_other_ref)):
            rows = pl.ds(pl.multiple_of(side * half, half), half)
            s = near.astype(F32) + far[...].astype(F32) + offset
            sin_ref[rows] = s
            smid_ref[rows] = s + par_ref[ROW_ATTEND : ROW_ATTEND + 1]
            unit, _ = unit_of(s)
            n1_ref[rows] = (unit * gain + shift).astype(BF16)

    n1 = n1_ref[...]
    q_ref[...] = dot_nn(n1, wq_ref[...]).astype(BF16)
    k_ref[...] = dot_nn(n1, wk_ref[...]).astype(BF16)
    v_ref[...] = dot_nn(n1, wv_ref[...]).astype(BF16)
    side_of = lane_side((tokens, LANES))
    one = (lax.broadcasted_iota(jnp.int32, (tokens, LANES), 1) == 0).astype(BF16)
    bias = bias_ref[...]
    for pair in range(WIDTH // LANES):
        at = slice(pair * LANES, (pair + 1) * LANES)
        q = q_ref[:, at] * BF16(HEAD_DIM ** -0.5)
        keys = jnp.concatenate([k_ref[:, at], bias], axis=1)
        vt = jnp.transpose(v_ref[:, at])
        outs = []
        for a in range(2):
            qa = jnp.concatenate([jnp.where(side_of == a, q, BF16(0)), one], axis=1)
            s = dot_nt(keys, qa)
            top = jnp.max(s, axis=0, keepdims=True)
            p = jnp.exp(s - top)
            total = jnp.sum(p, axis=0, keepdims=True)
            lse_ref[pair, a : a + 1, :] = top + jnp.log(total)
            o = dot_nn(vt[a * HEAD_DIM : (a + 1) * HEAD_DIM], p.astype(BF16))
            outs.append(o * (1.0 / total))
        mixed_ref[:, at] = jnp.transpose(jnp.concatenate(outs, axis=0)).astype(BF16)
    smid_ref[...] += dot_nn(mixed_ref[...], wo_ref[...])

    @pl.when(j == GROUPS - 1)
    def _():
        s = sin_ref[...]
        attend_out = smid_ref[...] - s
        valid = (bias[:, :1].astype(F32) == 0.0).astype(F32)
        stat_ref[0:1] = column_sum(s * s * valid)
        stat_ref[1:2] = column_sum(attend_out * attend_out * valid)
        stat_ref[2:8] = jnp.zeros((6, D), F32)


def fixed(shape):
    return pl.BlockSpec(shape, lambda *_: (0,) * len(shape))


def by_column(rows, cols, first=0):
    return pl.BlockSpec((rows, cols), lambda j: (0, first + j))


def by_row(rows, cols):
    return pl.BlockSpec((rows, cols), lambda j: (j, 0))


def attend(place, own, mine, other, across, across_other, bias, par, wqkv, wo, deps=()):
    tokens = bias.shape[0]
    half = tokens // 2
    return call(
        attend_kernel,
        (place, own, mine, other, across, across_other, bias, par, wqkv, wqkv, wqkv, wo),
        [scalars()] + [fixed((half, D))] * 5 + [fixed((tokens, LANES)), fixed(par.shape)]
        + [by_column(D, WIDTH, first) for first in (0, GROUPS, 2 * GROUPS)]
        + [by_row(WIDTH, D)],
        [shaped((tokens, D), F32)]
        + [shaped((tokens, D), BF16)] * 5
        + [shaped((tokens, D), F32), shaped((PAIRS, 8, tokens), F32), shaped((8, D), F32)],
        out_specs=[fixed((tokens, D)), fixed((tokens, D))]
        + [by_column(tokens, WIDTH)] * 4
        + [fixed((tokens, D)), pl.BlockSpec((PAIRS // GROUPS, 8, tokens), lambda j: (j, 0, 0)), fixed((8, D))],
        grid=(GROUPS,),
        vmem=VMEM_MIB,
        name="attend",
        us=14.0,
        deps=deps,
    )


def stages_of(n):
    return [[b] for b in range(n.bit_length() - 1)]


def bits_at(x, bits):
    place = 0
    for b in bits:
        place = place * 2 + ((x >> b) & 1)
    return place


def peer_of(part, bits):
    return sum(1 << b for j, b in enumerate(reversed(bits)) if (part >> j) & 1)


def store_block(refs, me, d, stages, rows, cols, value):
    part = bits_at(me ^ d, stages[0])
    place = bits_at(me ^ d, sum(stages[1:], []))
    for i, ref in enumerate(refs):

        @pl.when(part == i)
        def _():
            ref[place, rows, cols] = value.astype(BF16)


def store_blocks(g_ref, me, n, refs, stages, cols, at):
    rows = g_ref.shape[0] // n
    for d in range(n):
        store_block(
            refs, me, d, stages, slice(0, rows), slice(at, at + cols), g_ref[d * rows : (d + 1) * rows, :cols]
        )


def share_shapes(n, stages, rows, cols):
    parts = 1 << len(stages[0])
    return [shaped((n // parts, rows, cols), BF16) for _ in range(parts)]


def clear_spare(refs, rows):
    for ref in refs:
        if ref.shape[1] > rows:
            ref[...] = jnp.zeros_like(ref)


def attend_back_kernel(
    place_ref, gmid_ref, wo_ref, q_ref, k_ref, v_ref, lse_ref, bias_ref, n1_ref, mixed_ref, sin_ref, par_ref,
    wq_ref, wk_ref, wv_ref,
    low_ref, vec_ref, *rest, n, stages,
):
    shares, (gtri, alow, quarter, grad, gn) = rest[:-5], rest[-5:]
    j = pl.program_id(0)
    e, me = place_ref[0], place_ref[1]
    tokens = gmid_ref.shape[0]

    @pl.when(j == 0)
    def _():
        alow[...] = gmid_ref[...].astype(BF16)

    gmix = dot_nt(alow[...], wo_ref[...]).astype(BF16)
    side_of = lane_side((tokens, LANES))
    one = (lax.broadcasted_iota(jnp.int32, (tokens, LANES), 1) == 0).astype(BF16)
    bias = bias_ref[...]
    scale = HEAD_DIM ** -0.5
    for pair in range(WIDTH // LANES):
        at = slice(pair * LANES, (pair + 1) * LANES)
        q, k, v, do = q_ref[:, at], k_ref[:, at], v_ref[:, at], gmix[:, at]
        keys = jnp.concatenate([k, bias], axis=1)
        kt = jnp.transpose(k)
        dq, dk, dv = [], 0.0, 0.0
        for a in range(2):
            qm = jnp.where(side_of == a, q, BF16(0))
            dom = jnp.where(side_of == a, do, BF16(0))
            s = dot_nt(keys, jnp.concatenate([qm * BF16(scale), one], axis=1))
            p = jnp.exp(s - lse_ref[pair, a : a + 1, :])
            dv = dv + dot_nn(p.astype(BF16), dom)
            dp = dot_nt(v, dom)
            delta = jnp.sum(p * dp, axis=0, keepdims=True)
            ds = (p * (dp - delta) * scale).astype(BF16)
            dk = dk + dot_nn(ds, qm)
            dq.append(dot_nn(kt[a * HEAD_DIM : (a + 1) * HEAD_DIM], ds))
        here = pl.ds(pl.multiple_of(j * WIDTH + pair * LANES, LANES), LANES)
        gtri[0, :, here] = jnp.transpose(jnp.concatenate(dq, axis=0)).astype(BF16)
        gtri[1, :, here] = dk.astype(BF16)
        gtri[2, :, here] = dv.astype(BF16)
    here = pl.ds(pl.multiple_of(j * WIDTH, WIDTH), WIDTH)
    part = (
        dot_nt(gtri[0, :, here], wq_ref[...])
        + dot_nt(gtri[1, :, here], wk_ref[...])
        + dot_nt(gtri[2, :, here], wv_ref[...])
    )

    @pl.when(j == 0)
    def _():
        gn[...] = part

    @pl.when(j > 0)
    def _():
        gn[...] += part

    @pl.when(j == GROUPS - 1)
    def _():
        wide, thin = 3 * D // 4, D // 4
        for mine in range(4):

            @pl.when(e == mine)
            def _():
                at = 0
                for b in range(3):
                    first, last = max(mine * wide, b * D), min((mine + 1) * wide, (b + 1) * D)
                    if first < last:
                        quarter[:, at : at + last - first] = gtri[b, :, first - b * D : last - b * D]
                        at += last - first
                quarter[:, wide:] = alow[:, mine * thin : (mine + 1) * thin]

        grad[:, :wide] = dot_tn(n1_ref[...], quarter[:, :wide])
        grad[:, wide:] = dot_tn(mixed_ref[...], quarter[:, wide:])
        clear_spare(shares, D // n)
        store_blocks(grad, me, n, shares, stages, D, 0)
        g = gn[...]
        unit, inverse = unit_of(sin_ref[...])
        gin = gmid_ref[...] + norm_back(g, unit, inverse, par_ref[ROW_GAIN : ROW_GAIN + 1])
        low_ref[...] = gin.astype(BF16)
        vec_ref[0:1] = column_sum(gin)
        vec_ref[1:2] = column_sum(g)
        vec_ref[2:3] = column_sum(g * unit)
        vec_ref[3:4] = column_sum(gmid_ref[...])
        vec_ref[4:8] = jnp.zeros((4, D), F32)


def padded_rows(rows):
    return -(-rows // 16) * 16


def attend_back(place, gmid, wo, q, k, v, lse, bias, n1, mixed, sin, par, wqkv, n, stages, deps=()):
    tokens = gmid.shape[0]
    rows = padded_rows(D // n)
    outs = [shaped((tokens, D), BF16), shaped((8, D), F32)] + share_shapes(n, stages, rows, D)
    return call(
        functools.partial(attend_back_kernel, n=n, stages=stages),
        (place, gmid, wo, q, k, v, lse, bias, n1, mixed, sin, par, wqkv, wqkv, wqkv),
        [scalars(), fixed((tokens, D)), by_row(WIDTH, D)]
        + [by_column(tokens, WIDTH)] * 3
        + [pl.BlockSpec((PAIRS // GROUPS, 8, tokens), lambda j: (j, 0, 0)), fixed((tokens, LANES))]
        + [fixed((tokens, D))] * 3
        + [fixed(par.shape)]
        + [by_column(D, WIDTH, first) for first in (0, GROUPS, 2 * GROUPS)],
        outs,
        out_specs=[fixed(v.shape) for v in outs],
        grid=(GROUPS,),
        scratch=[
            VMEM((3, tokens, D), BF16),
            VMEM((tokens, D), BF16),
            VMEM((tokens, D), BF16),
            VMEM((D, D), F32),
            VMEM((tokens, D), F32),
        ],
        vmem=VMEM_MIB,
        name="attend_back",
        us=19.0,
        deps=deps,
    )


STEPS = FF // D


def feed_kernel(
    smid_ref, bias_ref, par_ref, w1_ref, w2_ref, wh_ref, ho_ref,
    n2_ref, act_ref, slope_ref, sout_ref, n3_ref, blend_ref, stat_ref, feed,
):
    j = pl.program_id(0)

    @pl.when(j == 0)
    def _():
        unit, _ = unit_of(smid_ref[...])
        n2_ref[...] = (
            unit * par_ref[ROW_GAIN + 1 : ROW_GAIN + 2] + par_ref[ROW_SHIFT + 1 : ROW_SHIFT + 2]
        ).astype(BF16)
        feed[...] = jnp.broadcast_to(par_ref[ROW_CONTRACT : ROW_CONTRACT + 1], feed.shape)

    row = par_ref[ROW_EXPAND : ROW_EXPAND + 1]
    for i in range(1, STEPS):
        row = jnp.where(j == i, par_ref[ROW_EXPAND + i : ROW_EXPAND + i + 1], row)
    h = dot_nn(n2_ref[...], w1_ref[...]) + row
    sq = h * h
    t = jnp.tanh(h * (GELU_A + (GELU_A * GELU_B) * sq))
    side = 0.5 + 0.5 * t
    act_ref[...] = (h * side).astype(BF16)
    slope_ref[...] = (
        side + (h * (0.5 - 0.5 * t * t)) * (GELU_A + (3.0 * GELU_A * GELU_B) * sq)
    ).astype(BF16)
    feed[...] += dot_nn(act_ref[...], w2_ref[...])

    @pl.when(j == STEPS - 1)
    def _():
        feed_out = feed[...]
        sout = smid_ref[...] + feed_out
        sout_ref[...] = sout
        unit, _ = unit_of(sout)
        n3_ref[...] = (
            unit * par_ref[ROW_GAIN + 2 : ROW_GAIN + 3] + par_ref[ROW_SHIFT + 2 : ROW_SHIFT + 3]
        ).astype(BF16)
        vals = dot_nt(n3_ref[...], wh_ref[...]) + ho_ref[0:1]
        l = [vals[:, q * LANES : (q + 1) * LANES] for q in range(MODEL_TALLY)]
        top = jnp.maximum(jnp.maximum(l[0], l[1]), l[2])
        p = [jnp.exp(v - top) for v in l]
        total = p[0] + p[1] + p[2]
        for q in range(MODEL_TALLY):
            blend_ref[q] = p[q] / total
        blend_ref[MODEL_TALLY] = vals[:, MODEL_TALLY * LANES :]
        valid = (bias_ref[:, :1].astype(F32) == 0.0).astype(F32)
        stat_ref[0:1] = column_sum(feed_out * feed_out * valid)
        stat_ref[1:2] = column_sum(sout * sout * valid)
        stat_ref[2:3] = jnp.broadcast_to(column_sum(valid), (1, D)) * (1.0 / D)
        stat_ref[3:8] = jnp.zeros((5, D), F32)


def feed(smid, bias, par, w1, w2, wh, ho, deps=()):
    tokens = smid.shape[0]
    outs = [
        shaped((tokens, D), BF16),
        shaped((tokens, FF), BF16),
        shaped((tokens, FF), BF16),
        shaped((tokens, D), F32),
        shaped((tokens, D), BF16),
        shaped((4, tokens, LANES), F32),
        shaped((8, D), F32),
    ]
    out_specs = [fixed(v.shape) for v in outs]
    out_specs[1] = out_specs[2] = by_column(tokens, D)
    return call(
        feed_kernel,
        (smid, bias, par, w1, w2, wh, ho),
        [fixed((tokens, D)), fixed(bias.shape), fixed(par.shape), by_column(D, D), by_row(D, D)]
        + [fixed(wh.shape), fixed(ho.shape)],
        outs,
        out_specs=out_specs,
        grid=(STEPS,),
        scratch=[VMEM((tokens, D), F32)],
        vmem=VMEM_MIB,
        name="feed",
        us=12.0,
        deps=deps,
    )


def head_back_kernel(
    place_ref, blend_ref, gw_ref, gs_ref, wh_ref, sout_ref, par_ref, act_ref,
    hlow_ref, gout_ref, vec_ref, *rest, n, stages,
):
    shares, (flow, quarter, cgrad) = rest[:-3], rest[-3:]
    e, me = place_ref[0], place_ref[1]

    def by_token(v):
        tall = jnp.concatenate([v, jnp.zeros((LANES - HEAD_ROWS, v.shape[1]), F32)], axis=0)
        return jnp.transpose(tall)

    weights = [by_token(gw_ref[q]) for q in range(MODEL_TALLY)]
    inner = 0.0
    for q in range(MODEL_TALLY):
        inner = inner + blend_ref[q] * weights[q]
    vec_ref[...] = jnp.zeros_like(vec_ref)
    for q in range(MODEL_TALLY + 1):
        cols = slice(q * LANES, (q + 1) * LANES)
        g = by_token(gs_ref[...]) if q == MODEL_TALLY else blend_ref[q] * (weights[q] - inner)
        vec_ref[0:1, cols] = column_sum(g)
        hlow_ref[:, cols] = g.astype(BF16)
    gn3 = dot_nn(hlow_ref[...], wh_ref[...])
    unit, inverse = unit_of(sout_ref[...])
    g = norm_back(gn3, unit, inverse, par_ref[ROW_GAIN + 2 : ROW_GAIN + 3])
    gout_ref[...] = g
    flow[...] = g.astype(BF16)
    vec_ref[1:2] = column_sum(gn3 * unit)
    vec_ref[2:3] = column_sum(gn3)
    vec_ref[3:4] = column_sum(g)
    thin = D // 4
    for here in range(4):

        @pl.when(e == here)
        def _():
            quarter[...] = flow[:, here * thin : (here + 1) * thin]

    size, rows = FF // n, D // n
    clear_spare(shares, rows)
    cgrad[...] = dot_tn(quarter[...], act_ref[...])
    for d in range(n):
        for i in range(n // 4):
            part = cgrad[i * rows : (i + 1) * rows, d * size : (d + 1) * size]
            store_block(shares, me, d, stages, slice(0, rows), slice(i * size, (i + 1) * size), part)


def head_back(place, blend, gw, gs, wh, sout, par, act, n, stages, deps=()):
    tokens = sout.shape[0]
    return call(
        functools.partial(head_back_kernel, n=n, stages=stages),
        (place, blend, gw, gs, wh, sout, par, act),
        [scalars()] + [whole()] * 7,
        [shaped((tokens, 4 * LANES), BF16), shaped((tokens, D), F32), shaped((8, D), F32)]
        + share_shapes(n, stages, padded_rows(D // n), D),
        scratch=[VMEM((tokens, D), BF16), VMEM((tokens, D // 4), BF16), VMEM((D // 4, FF), F32)],
        name="head_back",
        us=7,
        deps=deps,
    )


def feed_back_kernel(
    place_ref, hlow_ref, gout_ref, n3_ref, par_ref, slope_ref, n2_ref, smid_ref, w1_ref, w2_ref,
    gmid_ref, vec_ref, *rest, n, stages,
):
    shares, (flow, hid, mine, gn2, grad) = rest[:-5], rest[-5:]
    j = pl.program_id(0)
    e, me = place_ref[0], place_ref[1]

    @pl.when(j == 0)
    def _():
        flow[...] = gout_ref[...].astype(BF16)
        vec_ref[...] = jnp.zeros_like(vec_ref)
        gn2[...] = jnp.zeros_like(gn2)

    h = dot_nt(flow[...], w2_ref[...]) * slope_ref[...].astype(F32)
    sums = column_sum(h)
    for i in range(STEPS):

        @pl.when(j == i)
        def _():
            vec_ref[i : i + 1] = sums

    hid[...] = h.astype(BF16)

    @pl.when(j == e)
    def _():
        mine[...] = hid[...]

    gn2[...] += dot_nt(hid[...], w1_ref[...])

    @pl.when(j == STEPS - 1)
    def _():
        clear_spare(shares, D // n)
        grad[...] = dot_tn(n2_ref[...], mine[...])
        store_blocks(grad, me, n, shares, stages, D, 0)
        grad[:, :LANES] = dot_tn(n3_ref[...], hlow_ref[:, pl.ds(pl.multiple_of(e * LANES, LANES), LANES)])
        store_blocks(grad, me, n, shares, stages, LANES, D)
        unit, inverse = unit_of(smid_ref[...])
        y = gn2[...]
        gmid_ref[...] = gout_ref[...] + norm_back(y, unit, inverse, par_ref[ROW_GAIN + 1 : ROW_GAIN + 2])
        vec_ref[4:5] = column_sum(y * unit)
        vec_ref[5:6] = column_sum(y)


def feed_back(place, hlow, gout, n3, par, slope, n2, smid, w1, w2, n, stages, deps=()):
    tokens = smid.shape[0]
    rows = padded_rows(D // n)
    outs = [shaped((tokens, D), F32), shaped((8, D), F32)] + share_shapes(n, stages, rows, D + LANES)
    return call(
        functools.partial(feed_back_kernel, n=n, stages=stages),
        (place, hlow, gout, n3, par, slope, n2, smid, w1, w2),
        [scalars()]
        + [fixed(v.shape) for v in (hlow, gout, n3, par)]
        + [by_column(tokens, D), fixed(n2.shape), fixed(smid.shape), by_column(D, D), by_row(D, D)],
        outs,
        out_specs=[fixed(v.shape) for v in outs],
        grid=(STEPS,),
        scratch=[
            VMEM((tokens, D), BF16),
            VMEM((tokens, D), BF16),
            VMEM((tokens, D), BF16),
            VMEM((tokens, D), F32),
            VMEM((D, D), F32),
        ],
        vmem=VMEM_MIB,
        name="feed_back",
        us=13.0,
        deps=deps,
    )


def fold_kernel(*refs, counts, parts, axis):
    outs = refs[sum(counts) :]
    ins, at = 0, 0
    for g, count in enumerate(counts):
        total = refs[ins][...].astype(F32)
        for i in range(1, count):
            total = total + refs[ins + i][...].astype(F32)
        ins += count
        size = total.shape[0] // parts
        for p in range(parts):
            piece = total[p * size : (p + 1) * size].astype(outs[p].dtype)
            if axis is None:
                outs[g * parts + p][...] = piece
            elif axis == 1:
                outs[p][:, at : at + piece.shape[1]] = piece
            else:
                outs[p][:, :, at : at + piece.shape[2]] = piece
        if axis is not None:
            at += total.shape[axis]


def fold(groups, parts, axis=None, deps=()):
    shapes = [g[0].shape for g in groups]
    dtype = groups[0][0].dtype
    size = shapes[0][0] // parts
    if axis is None:
        outs = [shaped((size,) + v[1:], dtype) for v in shapes for _ in range(parts)]
    else:
        full = list(shapes[0])
        full[0], full[axis] = size, sum(v[axis] for v in shapes)
        outs = [shaped(tuple(full), dtype)] * parts
    inputs = [v for g in groups for v in g]
    return call(
        functools.partial(fold_kernel, counts=[len(g) for g in groups], parts=parts, axis=axis),
        inputs,
        [whole()] * len(inputs),
        outs,
        name="fold",
        us=1.3,
        deps=deps,
    )


def vectors_kernel(*refs):
    head, feed, attend, stat_a, stat_b, hot, out = refs
    out[0:4] = head[0:4]
    out[4:10] = feed[0:6]
    out[10:14] = attend[0:4]
    out[14:16] = stat_a[0:2]
    out[16:19] = stat_b[0:3]
    out[19:24] = jnp.zeros((5, D), F32)
    out[24:32] = hot[:, :1] * attend[1:2]


def vectors(head, feed, attend, stat_a, stat_b, hot, deps=()):
    return call(
        vectors_kernel,
        (head, feed, attend, stat_a, stat_b, hot),
        [whole()] * 6,
        shaped((32, D), F32),
        name="vectors",
        us=1,
        deps=deps,
    )


def assemble_kernel(place_ref, *refs, n, thin):
    parts = refs[0:4]
    contract, expand, head = refs[4:]
    e = place_ref[0]
    rows, size = D // n, FF // n
    for here in range(4):

        @pl.when(e == here)
        def _():
            for i in range(4):
                part = parts[here ^ i]
                for j in range(n // 4):
                    block = jnp.transpose(part[0, :, j * size : (j + 1) * size].astype(F32))
                    contract[:, i * thin + j * rows : i * thin + (j + 1) * rows] = block[:, :rows]
                expand[:, i * D : (i + 1) * D] = part[0, :rows, D : 2 * D].astype(F32)
                head[:, i * CHANNELS : (i + 1) * CHANNELS] = part[0, :rows, 2 * D : 2 * D + CHANNELS].astype(F32)


def assemble(place, parts, n, deps=()):
    rows = D // n
    return call(
        functools.partial(assemble_kernel, n=n, thin=D // 4),
        (place, *parts),
        [scalars()] + [whole()] * 4,
        [shaped((FF // n, D), F32), shaped((rows, FF), F32), shaped((rows, 4 * CHANNELS), F32)],
        name="assemble",
        us=2.5,
        deps=deps,
    )


def assemble_last_kernel(place_ref, *refs, n, step, width, skip, cut):
    first, last, (triple, result, lift) = refs[0:4], refs[4:8], refs[8:]
    e = place_ref[0]
    rows, thin, wide = D // n, D // 4, 3 * D // 4
    for here in range(4):

        @pl.when(e == here)
        def _():
            for i in range(4):
                k = here ^ i
                triple[:, i * wide : (i + 1) * wide] = first[k][0, :rows, :wide].astype(F32)
                result[:, i * thin : (i + 1) * thin] = first[k][0, :rows, wide:].astype(F32)
                take = step if i < 3 else width
                near = min(take, cut)
                lift[i * step : i * step + near] = first[k][0, skip : skip + near].astype(F32)
                if take > cut:
                    lift[i * step + cut : i * step + take] = last[k][0, : take - cut].astype(F32)


def assemble_last(place, first, last, n, step, width, skip, deps=()):
    cut = first[0].shape[1] - skip
    rows = D // n
    return call(
        functools.partial(assemble_last_kernel, n=n, step=step, width=width, skip=skip, cut=cut),
        (place, *first, *last),
        [scalars()] + [whole()] * 8,
        [shaped((rows, 3 * D), F32), shaped((rows, D), F32), shaped((3 * step + width, D), F32)],
        name="assemble_last",
        us=2.5,
        deps=deps,
    )


CUT_CHANNELS = CHANNELS // 3
CUT = CUT_CHANNELS * PIXELS


def channel_sums(pred_ref, adj_ref, first, channels, at, gw_ref, gs_ref):
    for i in range(channels):
        here = slice((first + i) * PIXELS, (first + i + 1) * PIXELS)
        adj = adj_ref[i * PIXELS : (i + 1) * PIXELS].astype(F32)
        gw_ref[first + i : first + i + 1, at] = column_sum(adj * pred_ref[here, at].astype(F32))
        gs_ref[first + i : first + i + 1, at] = column_sum(adj)


def weigh_near_kernel(place_ref, pred_ref, a0, a1, gw_ref, gs_ref):
    e = place_ref[0]
    rows = a0.shape[1]
    gw_ref[CHANNELS:] = jnp.zeros_like(gw_ref[CHANNELS:])
    gs_ref[CHANNELS:] = jnp.zeros_like(gs_ref[CHANNELS:])
    for k, a in enumerate((a0, a1)):
        at = pl.ds(pl.multiple_of((e ^ k) * rows, rows), rows)
        channel_sums(pred_ref, a, 0, CHANNELS, at, gw_ref, gs_ref)


def weigh_near(place, pred, adjoints, deps=()):
    tokens = pred.shape[1]
    return call(
        weigh_near_kernel,
        (place, pred, *adjoints),
        [scalars()] + [whole()] * 3,
        [shaped((HEAD_ROWS, tokens), F32)] * 2,
        name="weigh_near",
        us=3.6,
        deps=deps,
    )


def weigh_far_kernel(place_ref, pred_hbm, a2, a3, b2, b3, gw_in, gs_in, p2, p3, gw_ref, gs_ref, o2, o3, pred, sem):
    e = place_ref[0]
    rows = a2.shape[1]
    at = pl.ds(pl.multiple_of((e // 2) * 2 * rows, 2 * rows), 2 * rows)
    pair = pl.ds(pl.multiple_of((1 - e // 2) * 2 * rows, 2 * rows), 2 * rows)
    load = pltpu.make_async_copy(pred_hbm.at[:, pair], pred, sem)
    load.start()
    o2[...] = p2[...]
    o3[...] = p3[...]
    gw_ref[:, at] = gw_in[:, at]
    gs_ref[:, at] = gs_in[:, at]
    gw_ref[CHANNELS:, pair] = jnp.zeros((HEAD_ROWS - CHANNELS, 2 * rows), F32)
    gs_ref[CHANNELS:, pair] = jnp.zeros((HEAD_ROWS - CHANNELS, 2 * rows), F32)
    load.wait()
    for k, near, far in ((2, a2, b2), (3, a3, b3)):
        token = e ^ k
        own = pl.ds(pl.multiple_of(token * rows, rows), rows)
        inner = pl.ds(pl.multiple_of((token & 1) * rows, rows), rows)
        for i in range(CHANNELS):
            adj_ref, first = (near, 0) if i < CUT_CHANNELS else (far, CUT_CHANNELS)
            here = slice((i - first) * PIXELS, (i - first + 1) * PIXELS)
            adj = adj_ref[here].astype(F32)
            values = pred[i * PIXELS : (i + 1) * PIXELS, inner].astype(F32)
            gw_ref[i : i + 1, own] = column_sum(adj * values)
            gs_ref[i : i + 1, own] = column_sum(adj)


def weigh_far(place, pred, adjoints, gw, gs, pieces, deps=()):
    tokens = pred.shape[1]
    return call(
        weigh_far_kernel,
        (place, pred, *adjoints, gw, gs, *pieces),
        [scalars(), in_hbm()] + [whole()] * 8,
        [shaped((HEAD_ROWS, tokens), F32)] * 2 + [shaped(v.shape, v.dtype) for v in pieces],
        scratch=[VMEM((TILE_ENTRIES, tokens // 2), BF16), pltpu.SemaphoreType.DMA],
        vmem=VMEM_MIB,
        name="weigh_far",
        us=2.7,
        deps=deps,
    )


def split_two(v):
    hi = v.astype(BF16)
    return jnp.concatenate([hi, (v - hi.astype(F32)).astype(BF16)], axis=0)


def blend_kernel(place_ref, blend_ref, c0, c1, c2, c3, spread_ref, o0, o1, o2, o3, acc):
    e = place_ref[0]
    rows = o0.shape[1]
    spread = jnp.concatenate([spread_ref[...]] * 2, axis=1)
    acc[...] = dot_nn(spread, split_two(jnp.transpose(blend_ref[MODEL_TALLY])))
    for k, c in enumerate((c0, c1, c2, c3)):
        q = e ^ k

        @pl.when(q < MODEL_TALLY)
        def _():
            acc[...] += dot_nn(spread, split_two(jnp.transpose(blend_ref[q]))) * c[...].astype(F32)

    for k, o in enumerate((o0, o1, o2, o3)):
        at = pl.multiple_of((e ^ k) * rows, rows)
        o[...] = acc[:, pl.ds(at, rows)].astype(BF16)


def blend_columns(place, blend, columns, spread, deps=()):
    cols, tokens = columns[0].shape
    rows = tokens // 4
    return call(
        blend_kernel,
        (place, blend, *columns, spread),
        [scalars()] + [whole()] * 6,
        [shaped((cols, rows), BF16)] * 4,
        scratch=[VMEM((cols, tokens), F32)],
        name="blend",
        us=5.3,
        deps=deps,
    )


def lift_grad_kernel(place_ref, low_ref, masks_ref, c0, c1, c2, c3, *rest, n, stages, cut):
    shares, grad = rest[:-1], rest[-1]
    e, me = place_ref[0], place_ref[1]
    masks = jnp.transpose(masks_ref[...])
    low = low_ref[...].astype(F32)
    grad[...] = jnp.zeros_like(grad)
    for k, c in enumerate((c0, c1, c2, c3)):

        @pl.when((e ^ k) < MODEL_TALLY)
        def _():
            grad[...] += dot_nn(c[...], (low * masks[:, k : k + 1]).astype(BF16))

    rows = grad.shape[0] // n
    parts = len(shares) // 2
    for d in range(n):
        near = d * rows
        store_block(shares[:parts], me, d, stages, slice(None), slice(None), grad[near : near + cut])
        store_block(shares[parts:], me, d, stages, slice(None), slice(None), grad[near + cut : near + rows])


def lift_grad(place, low, masks, columns, n, stages, deps=()):
    cols, tokens = columns[0].shape
    rows = cols // n
    cut = padded_rows(rows // 2)
    return call(
        functools.partial(lift_grad_kernel, n=n, stages=stages, cut=cut),
        (place, low, masks, *columns),
        [scalars()] + [whole()] * 6,
        share_shapes(n, stages, cut, D) + share_shapes(n, stages, rows - cut, D),
        scratch=[VMEM((cols, D), F32)],
        name="lift_grad",
        us=7.6,
        deps=deps,
    )


def slope_kernel(place_ref, low_ref, masks_ref, blend_ref, lift_ref, a0, a1, a2, a3, *rest, which):
    out_ref, acc = rest[-2], rest[-1]
    e = place_ref[0]
    rows = a0.shape[1]
    masks = jnp.transpose(masks_ref[...])
    low = (low_ref[...].astype(F32) * masks[:, :1]).astype(BF16)
    active = jnp.where(e < MODEL_TALLY, 1.0, 0.0)
    weights = jnp.transpose(blend_ref[jnp.minimum(e, MODEL_TALLY - 1)] * active)
    acc[...] = dot_nt(lift_ref[...], low)
    first = which * CUT_CHANNELS
    for k, a in enumerate((a0, a1, a2, a3)):
        for b in range(4):

            @pl.when((e ^ k) == b)
            def _():
                at = slice(b * rows, (b + 1) * rows)
                for i in range(CUT_CHANNELS):
                    here = slice(i * PIXELS, (i + 1) * PIXELS)
                    weight = weights[first + i : first + i + 1, at]
                    out_ref[here, at] = (acc[here, at] + weight * a[here].astype(F32)).astype(BF16)


def slope(which, before, place, low, masks, blend, lift, adjoints, deps=()):
    tokens = low.shape[0]
    rows = adjoints[0].shape[1]
    third = lambda cols: pl.BlockSpec((CUT, cols), lambda j: (which, 0))
    far = adjoints[2:4] if which == 0 else adjoints[4:6]
    far_spec = pl.BlockSpec((CUT, rows), lambda j: (max(which - 1, 0), 0))
    inputs = [place, low, masks, blend, lift, *adjoints[:2], *far]
    in_specs = [scalars(), fixed((tokens, D)), fixed(masks.shape), fixed(blend.shape), third(D)]
    in_specs += [third(rows)] * 2 + [far_spec] * 2
    aliases = {}
    if before is not None:
        aliases = {len(inputs): 0}
        inputs.append(before)
        in_specs.append(in_hbm())
    for v in deps:
        inputs.append(v)
        in_specs.append(in_hbm())
    return pl.pallas_call(
        functools.partial(slope_kernel, which=which),
        out_shape=shaped((TILE_ENTRIES, tokens), BF16),
        grid=(1,),
        in_specs=in_specs,
        out_specs=third(tokens),
        scratch_shapes=[VMEM((CUT, tokens), F32)],
        input_output_aliases=aliases,
        compiler_params=pltpu.CompilerParams(vmem_limit_bytes=VMEM_MIB * 1024 * 1024),
        cost_estimate=taking(4.3),
        name="slope",
    )(*inputs)


def expert_swap(v, k):
    size = lax.axis_size("expert")
    return lax.ppermute(v, "expert", [(i, i ^ k) for i in range(size)])


def frame_swap(v, k):
    size = lax.axis_size("dp")
    return lax.ppermute(v, "dp", [(i, i ^ k) for i in range(size)])


def gather_four(v):
    across = expert_swap(v, 2)
    return [v, expert_swap(v, 1), across, expert_swap(across, 1)]


def in_order(parts, e):
    odd = (e & 1) == 1
    high = (e & 2) == 2
    a, b, c, d = parts
    a, b, c, d = (
        jnp.where(odd, b, a),
        jnp.where(odd, a, b),
        jnp.where(odd, d, c),
        jnp.where(odd, c, d),
    )
    return [jnp.where(high, c, a), jnp.where(high, d, b), jnp.where(high, a, c), jnp.where(high, b, d)]


def local(
    model_predictions,
    member_tile_presence,
    piece_usable_flags,
    horizon_positions,
    result_adjoint,
    tile_lift_matrix,
    tile_lift_offset,
    horizon_lookup,
    normalizer_scales,
    normalizer_offsets,
    query_key_value_matrix,
    attend_result_matrix,
    attend_offset_vector,
    expand_matrix,
    expand_offset,
    contract_matrix,
    contract_offset,
    mixing_head_matrix,
    mixing_head_offset,
):
    n = lax.axis_size("dp")
    e = lax.axis_index("expert")
    place = jnp.stack([e, lax.axis_index("dp")]).astype(jnp.int32)
    core = e & 1
    active = (e < MODEL_TALLY).astype(F32)
    pred = jnp.transpose(model_predictions[0])
    tokens = pred.shape[1]
    block = TILE_ENTRIES // n
    step = block // 4 // 8 * 8 if block % 8 == 0 else block // 4
    width = block - 3 * step
    padded = padded_rows(width)

    adjoint = jnp.transpose(result_adjoint)
    near = expert_swap(adjoint, 1)
    far_a = expert_swap(adjoint[:CUT], 2)

    mask = member_tile_presence.astype(F32) * active
    own_part, other_part = embed(place, mask, pred, tile_lift_matrix)

    info = jnp.concatenate([mask, piece_usable_flags.astype(F32)[None]], axis=1)
    infos = [info] + [expert_swap(info, k) for k in (1, 2, 3)]
    masks = jnp.concatenate([v[:, :tokens] for v in infos] + [jnp.zeros((4, tokens), F32)], axis=0)
    valid = jnp.concatenate([v[0, tokens:] for v in in_order(infos, e)])
    first = jnp.arange(LANES) == 0
    bias = jnp.where((valid[:, None] == 0) & first[None, :], MASKED_SCORE, 0.0).astype(BF16)

    lead_hot = (jnp.arange(horizon_lookup.shape[0]) == horizon_positions[0]).astype(F32)
    lead_vector = jnp.sum(lead_hot[:, None] * horizon_lookup.astype(F32), axis=0)
    par = jnp.concatenate(
        [
            tile_lift_offset[None].astype(F32),
            normalizer_scales.astype(F32),
            normalizer_offsets.astype(F32),
            attend_offset_vector[None].astype(F32),
            contract_offset[None].astype(F32),
            expand_offset.reshape(FF // D, D).astype(F32),
            lead_vector[None],
            jnp.zeros((PARAM_ROWS - ROW_HEAD, D), F32),
        ],
        axis=0,
    )
    over = (0, LANES - CHANNELS)
    head = jnp.pad(jnp.transpose(mixing_head_matrix).reshape(4, CHANNELS, D), ((0, 0), over, (0, 0)))
    head = head.reshape(4 * LANES, D)
    head_row = jnp.pad(mixing_head_offset.astype(F32).reshape(1, 4, CHANNELS), ((0, 0), (0, 0), over))
    head_row = head_row.reshape(1, 4 * LANES)
    at = jnp.arange(n * padded)
    channel = ((at // padded) * block + e * step + at % padded) // PIXELS
    spread = (channel[:, None] == jnp.arange(LANES)[None, :]).astype(BF16)

    pair = (own_part.astype(F32) + expert_swap(other_part, 1).astype(F32)).astype(BF16)
    other = expert_swap(own_part, 1)
    across = expert_swap(pair, 2)
    across_other = expert_swap(across, 1)

    pieces = pack(place, pred, n, step, width, padded, deps=[pair, far_a, par, bias, head, head_row, spread, masks])
    far_near_a = expert_swap(far_a, 1)
    mine, grad_shift = weigh_near(place, pred, [adjoint, near], deps=[pieces[0]])
    (rest,) = hold([adjoint[CUT:]], deps=[across, mine, far_near_a])
    far_b = expert_swap(rest, 2)

    sin, n1, queries, keys, values, mixed, smid, lse, stat_a = attend(
        place, pair, other_part, other, across, across_other, bias, par, query_key_value_matrix, attend_result_matrix, deps=[rest]
    )
    (far_b,) = hold([far_b], deps=[smid])
    far_near_b = expert_swap(far_b, 1)
    adjoints = [adjoint, near, far_a, far_near_a, far_b, far_near_b]
    mine, grad_shift, across_x, across_both = weigh_far(
        place, pred, adjoints[2:], mine, grad_shift, pieces[2:], deps=[smid]
    )
    columns = [pieces[0], expert_swap(pieces[1], 1), expert_swap(across_x, 2), expert_swap(across_both, 3)]
    all_mine = [mine] + [expert_swap(mine, k) for k in (1, 2, 3)]
    n2, act, gelu_slope, sout, n3, blend, stat_b = feed(
        smid, bias, par, expand_matrix, contract_matrix, head, head_row, deps=[across_x, columns[1]]
    )
    grad_weights = jnp.stack(in_order(all_mine, e)[:MODEL_TALLY])

    stages = stages_of(n)
    last_bit = len(stages) - 1

    def to_end(keep, got, bit, deps):
        while bit < last_bit:
            keep, send = fold([[keep, got]], 2, deps=deps)
            bit += 1
            got = frame_swap(send, 1 << bit)
        return gather_four(fold([[keep, got]], 1, deps=deps)[0])

    hlow, gout, vec_h, ckeep, csend = head_back(
        place, blend, grad_weights, grad_shift, head, sout, par, act, n, stages
    )
    cgot = frame_swap(csend, 1)
    gmid, vec_f, tkeep, tsend = feed_back(
        place, hlow, gout, n3, par, gelu_slope, n2, smid, expand_matrix, contract_matrix, n, stages
    )
    tgot = frame_swap(tsend, 1)
    low, vec_a, qkeep, qsend = attend_back(
        place, gmid, attend_result_matrix, queries, keys, values, lse, bias, n1, mixed, sin, par, query_key_value_matrix, n, stages,
        deps=[cgot],
    )
    qgot = frame_swap(qsend, 1)
    keep, send = fold([[ckeep, cgot], [tkeep, tgot]], 2, axis=2, deps=[low])
    got = frame_swap(send, 2)
    akeep, asend, bkeep, bsend = lift_grad(place, low, masks, columns, n, stages, deps=[keep])
    agot = frame_swap(asend, 1)
    bgot = frame_swap(bsend, 1)
    slopes = [place, low, masks, blend, tile_lift_matrix, adjoints]
    outgoing = blend_columns(place, blend, columns, spread, deps=[akeep])
    hot = jnp.broadcast_to(lead_hot[:, None], (lead_hot.shape[0], LANES))
    packed = vectors(vec_h, vec_f, vec_a, stat_a, stat_b, hot, deps=[outgoing[0]])
    packed_got = frame_swap(packed, 1)
    part_slope = slope(0, None, *slopes, deps=[packed])
    keep, send = fold([[keep, got]], 2, deps=[part_slope])
    got = frame_swap(send, 4)
    skip = qkeep.shape[1]
    qkeep, qsend = fold([[qkeep, qgot], [akeep, agot]], 2, axis=1, deps=[keep])
    qgot = frame_swap(qsend, 2)
    part_slope = slope(1, part_slope, *slopes, deps=[qkeep])
    (packed,) = fold([[packed, packed_got]], 1, deps=[part_slope])
    packed_got = frame_swap(packed, 2)
    bkeep, bsend = fold([[bkeep, bgot]], 2, deps=[packed])
    bgot = frame_swap(bsend, 2)
    part_slope = slope(2, part_slope, *slopes, deps=[bkeep])
    rows_one = to_end(keep, got, 2, [part_slope])
    arrived = [outgoing[0]] + [expert_swap(outgoing[k], k) for k in (1, 2, 3)]
    qkeep, qsend = fold([[qkeep, qgot]], 2, deps=[rows_one[0]])
    qgot = frame_swap(qsend, 4)
    bkeep, bsend = fold([[bkeep, bgot]], 2, deps=[qkeep])
    bgot = frame_swap(bsend, 4)
    combined = unpack(place, arrived, n, step, width, padded, deps=[bkeep])
    combined_prediction = jnp.transpose(combined)
    for bit in range(2, last_bit + 1):
        (packed,) = fold([[packed, packed_got]], 1, deps=[combined])
        packed_got = frame_swap(packed, 1 << bit)
    rows_two = to_end(qkeep, qgot, 2, [packed])
    contract_slope, expand_slope, head_slope = assemble(place, rows_one, n, deps=[rows_two[0]])
    rows_three = to_end(bkeep, bgot, 2, [contract_slope])
    (packed,) = fold([[packed, packed_got]], 1, deps=[rows_three[0]])
    triple_slope, result_slope, lift_slope = assemble_last(place, rows_two, rows_three, n, step, width, skip)
    predictions_slope = jnp.transpose(part_slope)[None]

    head_off = packed[0, : 4 * LANES].reshape(4, LANES)[:, :CHANNELS].reshape(4 * CHANNELS)
    total = jnp.sum(packed[14:19], axis=1)
    magnitudes = jnp.sqrt(total[:4] / (total[4] * D) + SQUARE_EPSILON)
    gains = jnp.stack([packed[12], packed[8], packed[1]])
    shifts = jnp.stack([packed[11], packed[9], packed[2]])
    return (
        combined_prediction,
        predictions_slope,
        magnitudes,
        lift_slope,
        packed[10],
        packed[24:32],
        gains,
        shifts,
        triple_slope,
        result_slope,
        packed[13],
        expand_slope,
        packed[4:8].reshape(FF),
        contract_slope,
        packed[3],
        head_slope,
        head_off,
    )


def solution(mesh):
    rows = P(("dp", "expert"), None)
    placed = (
        P("expert", "dp", None),
        P("expert", "dp"),
        P(("dp", "expert")),
        P("dp"),
        rows,
    ) + (P(),) * 14
    given = (
        rows,
        P("expert", "dp", None),
        P(),
        P("dp", None),
        P(),
        P(),
        P(),
        P(),
        P("dp", None),
        P("dp", None),
        P(),
        P("dp", None),
        P(),
        P("dp", None),
        P(),
        P("dp", None),
        P(),
    )
    return jax.shard_map(local, mesh=mesh, in_specs=placed, out_specs=given, check_vma=False)
```

```python
import functools

import jax
import jax.numpy as jnp
from jax import lax
from jax.experimental import pallas as pl
from jax.experimental.pallas import tpu as pltpu
from jax.sharding import PartitionSpec as P

D = 768
HEADS = 12
HEAD_DIM = 64
FF = 3072
MODEL_TALLY = 3
CHANNELS = 69
PIXELS = 64
TILE_ENTRIES = 4416
LANES = 128
PAIRS = HEADS // 2

NORM_EPSILON = 1e-05
SQUARE_EPSILON = 1e-06
MASKED_SCORE = -1e30
GELU_A = 0.7978845608028654
GELU_B = 0.044715
F32 = jnp.float32
BF16 = jnp.bfloat16

ROW_LIFT, ROW_GAIN, ROW_SHIFT, ROW_ATTEND, ROW_CONTRACT, ROW_EXPAND, ROW_LEAD, ROW_HEAD = 0, 1, 4, 7, 8, 9, 13, 14
PARAM_ROWS = 16
HEAD_ROWS = 72
VMEM_MIB = 20
VMEM_SMALL = 12
SCALE = 1e8

VMEM = pltpu.VMEM
SMEM = pltpu.SMEM


def whole():
    return pl.BlockSpec(memory_space=VMEM)


def scalars():
    return pl.BlockSpec(memory_space=SMEM)


def in_hbm():
    return pl.BlockSpec(memory_space=pl.ANY)


def shaped(shape, dtype):
    return jax.ShapeDtypeStruct(shape, dtype)


def dot_nn(a, b):
    return jnp.dot(a, b, preferred_element_type=F32)


def dot_tn(a, b):
    return lax.dot_general(a, b, (((0,), (0,)), ((), ())), preferred_element_type=F32)


def dot_nt(a, b):
    return lax.dot_general(a, b, (((1,), (1,)), ((), ())), preferred_element_type=F32)


def unit_of(values):
    center = values - jnp.mean(values, axis=-1, keepdims=True)
    inverse = lax.rsqrt(jnp.mean(center * center, axis=-1, keepdims=True) + NORM_EPSILON)
    return center * inverse, inverse


def norm_back(grad_out, unit, inverse, gain):
    scaled = grad_out * gain
    return inverse * (
        scaled
        - jnp.mean(scaled, axis=-1, keepdims=True)
        - unit * jnp.mean(scaled * unit, axis=-1, keepdims=True)
    )


def column_sum(v):
    return jnp.sum(v, axis=0, keepdims=True)


def room(n):
    return VMEM_MIB if (D // n) % 16 == 0 else VMEM_MIB + 24


def fixed(shape):
    return pl.BlockSpec(shape, lambda *_: (0,) * len(shape))


def taking(us):
    return pl.CostEstimate(flops=int(us * SCALE), bytes_accessed=1000, transcendentals=0)


def call(
    body, inputs, in_specs, outs, scratch=(), vmem=VMEM_MIB, grid=None, out_specs=None, name=None, deps=(), us=1.0,
    aliases=None,
):
    kwargs = {}
    if grid is not None:
        kwargs["grid"] = grid
    if aliases:
        kwargs["input_output_aliases"] = aliases
    outs = list(outs) if isinstance(outs, (list, tuple)) else [outs]
    if out_specs is None:
        out_specs = [whole() for _ in outs]
    out_specs = list(out_specs) if isinstance(out_specs, (list, tuple)) else [out_specs]
    count = len(inputs)

    def kernel(*refs):
        given = count + len(deps)
        body(*refs[:count], *refs[given : given + len(outs)], *refs[given + len(outs) + 1 :])
        token = refs[given + len(outs)]
        token[...] = jnp.zeros_like(token)

    return pl.pallas_call(
        kernel,
        out_shape=outs + [shaped((8, LANES), F32)],
        in_specs=list(in_specs) + [in_hbm() for _ in deps],
        out_specs=out_specs + [whole() if grid is None else fixed((8, LANES))],
        scratch_shapes=list(scratch),
        compiler_params=pltpu.CompilerParams(vmem_limit_bytes=vmem * 1024 * 1024),
        cost_estimate=taking(us),
        name=name,
        **kwargs,
    )(*inputs, *deps)


def embed_kernel(place_ref, mask_ref, pred_hbm, lift_hbm, own_ref, other_ref, pred, lift, acc, sems, *, cuts):
    copies = []
    for i, (a, b) in enumerate(cuts):
        one = pltpu.make_async_copy(pred_hbm.at[a:b], pred.at[a:b], sems.at[0, i])
        two = pltpu.make_async_copy(lift_hbm.at[a:b], lift.at[a:b], sems.at[1, i])
        one.start()
        two.start()
        copies.append((one, two))
    for i, (a, b) in enumerate(cuts):
        for copy in copies[i]:
            copy.wait()
        part = dot_tn(pred[a:b], lift[a:b])
        if i == 0:
            acc[...] = part
        elif i < len(cuts) - 1:
            acc[...] += part
        else:
            mask = jnp.transpose(jnp.broadcast_to(mask_ref[...], (8, mask_ref.shape[1])))[:, :1]
            acc[...] = (acc[...] + part) * mask
            half = own_ref.shape[0]
            core = place_ref[0] & 1
            own_ref[...] = acc[pl.ds(pl.multiple_of(core * half, half), half)].astype(BF16)
            other_ref[...] = acc[pl.ds(pl.multiple_of((1 - core) * half, half), half)].astype(BF16)


def embed(place, mask, pred, lift):
    tokens = pred.shape[1]
    cuts = [(0, 768), (768, 1536), (1536, 2560), (2560, 3584), (3584, TILE_ENTRIES)]
    return call(
        functools.partial(embed_kernel, cuts=cuts),
        (place, mask, pred, lift),
        [scalars(), whole(), in_hbm(), in_hbm()],
        [shaped((tokens // 2, D), BF16)] * 2,
        scratch=[
            VMEM((TILE_ENTRIES, tokens), BF16),
            VMEM((TILE_ENTRIES, D), BF16),
            VMEM((tokens, D), F32),
            pltpu.SemaphoreType.DMA((2, len(cuts))),
        ],
        vmem=60,
        name="embed",
        us=7.5,
    )


def cuts_of(n):
    return [0, n // 8, n // 2, n]


def pack_kernel(place_ref, pred_ref, far_ref, *outs, n, step, width, padded):
    outs[-1][...] = far_ref[...]
    e = place_ref[0]
    tokens = pred_ref.shape[1]
    block = TILE_ENTRIES // n
    cuts = cuts_of(n)
    for here in range(4):

        @pl.when(e == here)
        def _():
            for k in range(4):
                q = here ^ k
                for d in range(n):
                    out, first = outs[min(k, 2)], 0
                    if k >= 2:
                        piece = max(i for i in range(3) if cuts[i] <= d)
                        out, first = outs[2 + 3 * (k - 2) + piece], cuts[piece]
                    at = (d - first) * padded
                    start = d * block + q * step
                    out[at : at + width] = pred_ref[start : start + width]
                    if padded > width:
                        out[at + width : at + padded] = jnp.zeros((padded - width, tokens), BF16)


def pack(place, pred, far, n, step, width, padded, deps=()):
    tokens = pred.shape[1]
    cuts = cuts_of(n)
    thirds = [shaped(((cuts[i + 1] - cuts[i]) * padded, tokens), BF16) for i in range(3)]
    return call(
        functools.partial(pack_kernel, n=n, step=step, width=width, padded=padded),
        (place, pred, far),
        [scalars(), whole(), whole()],
        [shaped((n * padded, tokens), BF16)] * 2 + thirds * 2 + [shaped(far.shape, BF16)],
        name="pack",
        us=2,
        deps=deps,
    )


def unpack_kernel(place_ref, *refs, n, step, width, padded):
    parts, out = refs[:4], refs[4]
    e = place_ref[0]
    block = TILE_ENTRIES // n
    for here in range(4):

        @pl.when(e == here)
        def _():
            for q in range(4):
                take = step if q < 3 else width
                for d in range(n):
                    start = d * block + q * step
                    out[start : start + take] = parts[here ^ q][d * padded : d * padded + take]


def unpack(place, parts, n, step, width, padded, deps=()):
    rows = parts[0].shape[1]
    return call(
        functools.partial(unpack_kernel, n=n, step=step, width=width, padded=padded),
        (place, *parts),
        [scalars()] + [whole()] * 4,
        shaped((TILE_ENTRIES, rows), BF16),
        name="unpack",
        us=2,
        deps=deps,
    )


def lane_side(shape):
    return lax.broadcasted_iota(jnp.int32, shape, 1) // HEAD_DIM


GROUPS = 3
WIDTH = D // GROUPS


def attend_kernel(
    place_ref, own_ref, mine_ref, other_ref, across_ref, across_other_ref, bias_ref, par_ref,
    wq_ref, wk_ref, wv_ref, wo_ref,
    sin_ref, n1_ref, q_ref, k_ref, v_ref, mixed_ref, smid_ref, lse_ref, stat_ref,
):
    j = pl.program_id(0)
    core = place_ref[0] & 1
    tokens = bias_ref.shape[0]
    half = tokens // 2

    @pl.when(j == 0)
    def _():
        gain = par_ref[ROW_GAIN : ROW_GAIN + 1]
        shift = par_ref[ROW_SHIFT : ROW_SHIFT + 1] + par_ref[ROW_LEAD : ROW_LEAD + 1]
        offset = par_ref[ROW_LIFT : ROW_LIFT + 1]
        other = (mine_ref[...].astype(F32) + other_ref[...].astype(F32)).astype(BF16)
        for side, near, far in ((core, own_ref[...], across_ref), (1 - core, other, across_other_ref)):
            rows = pl.ds(pl.multiple_of(side * half, half), half)
            s = near.astype(F32) + far[...].astype(F32) + offset
            sin_ref[rows] = s
            smid_ref[rows] = s + par_ref[ROW_ATTEND : ROW_ATTEND + 1]
            unit, _ = unit_of(s)
            n1_ref[rows] = (unit * gain + shift).astype(BF16)

    n1 = n1_ref[...]
    q_ref[...] = dot_nn(n1, wq_ref[...]).astype(BF16)
    k_ref[...] = dot_nn(n1, wk_ref[...]).astype(BF16)
    v_ref[...] = dot_nn(n1, wv_ref[...]).astype(BF16)
    side_of = lane_side((tokens, LANES))
    one = (lax.broadcasted_iota(jnp.int32, (tokens, LANES), 1) == 0).astype(BF16)
    bias = bias_ref[...]
    for pair in range(WIDTH // LANES):
        at = slice(pair * LANES, (pair + 1) * LANES)
        q = q_ref[:, at] * BF16(HEAD_DIM ** -0.5)
        keys = jnp.concatenate([k_ref[:, at], bias], axis=1)
        vt = jnp.transpose(v_ref[:, at])
        outs = []
        for a in range(2):
            qa = jnp.concatenate([jnp.where(side_of == a, q, BF16(0)), one], axis=1)
            s = dot_nt(keys, qa)
            top = jnp.max(s, axis=0, keepdims=True)
            p = jnp.exp(s - top)
            total = jnp.sum(p, axis=0, keepdims=True)
            lse_ref[pair, a : a + 1, :] = top + jnp.log(total)
            o = dot_nn(vt[a * HEAD_DIM : (a + 1) * HEAD_DIM], p.astype(BF16))
            outs.append(o * (1.0 / total))
        mixed_ref[:, at] = jnp.transpose(jnp.concatenate(outs, axis=0)).astype(BF16)
    smid_ref[...] += dot_nn(mixed_ref[...], wo_ref[...])

    @pl.when(j == GROUPS - 1)
    def _():
        s = sin_ref[...]
        attend_out = smid_ref[...] - s
        valid = (bias[:, :1].astype(F32) == 0.0).astype(F32)
        stat_ref[0:1] = column_sum(s * s * valid)
        stat_ref[1:2] = column_sum(attend_out * attend_out * valid)
        stat_ref[2:8] = jnp.zeros((6, D), F32)


def by_column(rows, cols, first=0):
    return pl.BlockSpec((rows, cols), lambda j: (0, first + j))


def by_row(rows, cols):
    return pl.BlockSpec((rows, cols), lambda j: (j, 0))


def attend(place, own, mine, other, across, across_other, bias, par, wqkv, wo, deps=()):
    tokens = bias.shape[0]
    half = tokens // 2
    return call(
        attend_kernel,
        (place, own, mine, other, across, across_other, bias, par, wqkv, wqkv, wqkv, wo),
        [scalars()] + [fixed((half, D))] * 5 + [fixed((tokens, LANES)), fixed(par.shape)]
        + [by_column(D, WIDTH, first) for first in (0, GROUPS, 2 * GROUPS)]
        + [by_row(WIDTH, D)],
        [shaped((tokens, D), F32)]
        + [shaped((tokens, D), BF16)] * 5
        + [shaped((tokens, D), F32), shaped((PAIRS, 8, tokens), F32), shaped((8, D), F32)],
        out_specs=[fixed((tokens, D)), fixed((tokens, D))]
        + [by_column(tokens, WIDTH)] * 4
        + [fixed((tokens, D)), pl.BlockSpec((PAIRS // GROUPS, 8, tokens), lambda j: (j, 0, 0)), fixed((8, D))],
        grid=(GROUPS,),
        vmem=VMEM_MIB,
        name="attend",
        us=14.0,
        deps=deps,
    )


def stages_of(n):
    return [[b] for b in range(n.bit_length() - 1)]


def bits_at(x, bits):
    place = 0
    for b in bits:
        place = place * 2 + ((x >> b) & 1)
    return place


def peer_of(part, bits):
    return sum(1 << b for j, b in enumerate(reversed(bits)) if (part >> j) & 1)


def store_blocks(g_ref, me, refs, stages, rows, cols, at):
    order = sum(stages, [])
    steps = len(order)
    for part, ref in enumerate(refs):
        for place in range(ref.shape[0]):
            value = part * ref.shape[0] + place
            apart = sum(((value >> (steps - 1 - i)) & 1) << b for i, b in enumerate(order))
            ref[place, :, at : at + cols] = g_ref[me ^ apart, rows, :cols].astype(BF16)


def put_blocks(g_ref, value, n):
    rows = value.shape[0] // n
    for d in range(n):
        g_ref[d, :rows, : value.shape[1]] = value[d * rows : (d + 1) * rows]


def share_shapes(n, stages, rows, cols):
    parts = 1 << len(stages[0])
    return [shaped((n // parts, rows, cols), BF16) for _ in range(parts)]


SUMS = 32


def put_sums(v, refs):
    both = split_two(v, 1)
    count = refs[0].shape[0]
    size = both.shape[1] // count
    for ref in refs:
        for i in range(count):
            ref[i, :, ref.shape[2] - size :] = both[:, i * size : (i + 1) * size]


def get_sums(values):
    both = jnp.concatenate([values[i] for i in range(values.shape[0])], axis=1).astype(F32)
    half = both.shape[1] // 2
    return both[:, :half] + both[:, half:]


def sum_columns(rows, count):
    return 2 * SUMS * D // rows // count


def clear_spare(ref, rows):
    if ref.shape[1] > rows:
        ref[...] = jnp.zeros_like(ref)


def attend_back_kernel(
    place_ref, gmid_ref, wo_ref, q_ref, k_ref, v_ref, lse_ref, bias_ref, n1_ref, mixed_ref, sin_ref, par_ref,
    wq_ref, wk_ref, wv_ref, vec_h, vec_f, stat_a, stat_b, hot_ref,
    low_ref, *rest, n, stages,
):
    shares, (gtri, alow, quarter, flat, grad, gn, vec) = rest[:-7], rest[-7:]
    j = pl.program_id(0)
    e, me = place_ref[0], place_ref[1]
    tokens = gmid_ref.shape[0]

    @pl.when(j == 0)
    def _():
        alow[...] = gmid_ref[...].astype(BF16)

    gmix = dot_nt(alow[...], wo_ref[...]).astype(BF16)
    side_of = lane_side((tokens, LANES))
    one = (lax.broadcasted_iota(jnp.int32, (tokens, LANES), 1) == 0).astype(BF16)
    bias = bias_ref[...]
    scale = HEAD_DIM ** -0.5
    for pair in range(WIDTH // LANES):
        at = slice(pair * LANES, (pair + 1) * LANES)
        q, k, v, do = q_ref[:, at], k_ref[:, at], v_ref[:, at], gmix[:, at]
        keys = jnp.concatenate([k, bias], axis=1)
        kt = jnp.transpose(k)
        dq, dk, dv = [], 0.0, 0.0
        for a in range(2):
            qm = jnp.where(side_of == a, q, BF16(0))
            dom = jnp.where(side_of == a, do, BF16(0))
            s = dot_nt(keys, jnp.concatenate([qm * BF16(scale), one], axis=1))
            p = jnp.exp(s - lse_ref[pair, a : a + 1, :])
            dv = dv + dot_nn(p.astype(BF16), dom)
            dp = dot_nt(v, dom)
            delta = jnp.sum(p * dp, axis=0, keepdims=True)
            ds = (p * (dp - delta) * scale).astype(BF16)
            dk = dk + dot_nn(ds, qm)
            dq.append(dot_nn(kt[a * HEAD_DIM : (a + 1) * HEAD_DIM], ds))
        here = pl.ds(pl.multiple_of(j * WIDTH + pair * LANES, LANES), LANES)
        gtri[0, :, here] = jnp.transpose(jnp.concatenate(dq, axis=0)).astype(BF16)
        gtri[1, :, here] = dk.astype(BF16)
        gtri[2, :, here] = dv.astype(BF16)
    here = pl.ds(pl.multiple_of(j * WIDTH, WIDTH), WIDTH)
    part = (
        dot_nt(gtri[0, :, here], wq_ref[...])
        + dot_nt(gtri[1, :, here], wk_ref[...])
        + dot_nt(gtri[2, :, here], wv_ref[...])
    )

    @pl.when(j == 0)
    def _():
        gn[...] = part

    @pl.when(j > 0)
    def _():
        gn[...] += part

    @pl.when(j == GROUPS - 1)
    def _():
        wide, thin = 3 * D // 4, D // 4
        for mine in range(4):

            @pl.when(e == mine)
            def _():
                at = 0
                for b in range(3):
                    first, last = max(mine * wide, b * D), min((mine + 1) * wide, (b + 1) * D)
                    if first < last:
                        quarter[:, at : at + last - first] = gtri[b, :, first - b * D : last - b * D]
                        at += last - first
                quarter[:, wide:] = alow[:, mine * thin : (mine + 1) * thin]

        flat[:, :wide] = dot_tn(n1_ref[...], quarter[:, :wide])
        flat[:, wide:] = dot_tn(mixed_ref[...], quarter[:, wide:])
        clear_spare(grad, D // n)
        put_blocks(grad, flat[...], n)
        store_blocks(grad, me, shares, stages, slice(None), D, 0)
        g = gn[...]
        unit, inverse = unit_of(sin_ref[...])
        gin = gmid_ref[...] + norm_back(g, unit, inverse, par_ref[ROW_GAIN : ROW_GAIN + 1])
        low_ref[...] = gin.astype(BF16)
        lead = column_sum(g)
        vec[0:4] = vec_h[0:4]
        vec[4:10] = vec_f[0:6]
        vec[10:11] = column_sum(gin)
        vec[11:12] = lead
        vec[12:13] = column_sum(g * unit)
        vec[13:14] = column_sum(gmid_ref[...])
        vec[14:16] = stat_a[0:2]
        vec[16:19] = stat_b[0:3]
        vec[19:24] = jnp.zeros((5, D), F32)
        vec[24:32] = hot_ref[:, :1] * lead
        packed = []
        rows = shares[0].shape[1]
        cols = SUMS * D // rows
        for i in range(SUMS):
            packed += [vec[i : i + 1, at : at + min(cols, D)] for at in range(0, D, min(cols, D))]
        group = max(cols // D, 1)
        packed = [
            packed[i] if group == 1 else jnp.concatenate(packed[i : i + group], axis=1)
            for i in range(0, len(packed), group)
        ]
        put_sums(jnp.concatenate(packed, axis=0), shares)


def padded_rows(rows):
    return -(-rows // 16) * 16


def attend_back(place, gmid, wo, q, k, v, lse, bias, n1, mixed, sin, par, wqkv, vectors, n, stages, deps=()):
    tokens = gmid.shape[0]
    rows = padded_rows(D // n)
    outs = [shaped((tokens, D), BF16)] + share_shapes(n, stages, rows, D + sum_columns(rows, n // 2))
    return call(
        functools.partial(attend_back_kernel, n=n, stages=stages),
        (place, gmid, wo, q, k, v, lse, bias, n1, mixed, sin, par, wqkv, wqkv, wqkv, *vectors),
        [scalars(), fixed((tokens, D)), by_row(WIDTH, D)]
        + [by_column(tokens, WIDTH)] * 3
        + [pl.BlockSpec((PAIRS // GROUPS, 8, tokens), lambda j: (j, 0, 0)), fixed((tokens, LANES))]
        + [fixed((tokens, D))] * 3
        + [fixed(par.shape)]
        + [by_column(D, WIDTH, first) for first in (0, GROUPS, 2 * GROUPS)]
        + [fixed(v.shape) for v in vectors],
        outs,
        out_specs=[fixed(v.shape) for v in outs],
        grid=(GROUPS,),
        scratch=[
            VMEM((3, tokens, D), BF16),
            VMEM((tokens, D), BF16),
            VMEM((tokens, D), BF16),
            VMEM((D, D), F32),
            VMEM((n, rows, D), F32),
            VMEM((tokens, D), F32),
            VMEM((SUMS, D), F32),
        ],
        vmem=room(n) + 6,
        name="attend_back",
        us=19.0,
        deps=deps,
    )


STEPS = FF // D


def feed_kernel(
    smid_ref, bias_ref, par_ref, w1_ref, w2_ref, wh_ref, ho_ref,
    n2_ref, act_ref, slope_ref, sout_ref, n3_ref, blend_ref, stat_ref, feed,
):
    j = pl.program_id(0)

    @pl.when(j == 0)
    def _():
        unit, _ = unit_of(smid_ref[...])
        n2_ref[...] = (
            unit * par_ref[ROW_GAIN + 1 : ROW_GAIN + 2] + par_ref[ROW_SHIFT + 1 : ROW_SHIFT + 2]
        ).astype(BF16)
        feed[...] = jnp.broadcast_to(par_ref[ROW_CONTRACT : ROW_CONTRACT + 1], feed.shape)

    row = par_ref[ROW_EXPAND : ROW_EXPAND + 1]
    for i in range(1, STEPS):
        row = jnp.where(j == i, par_ref[ROW_EXPAND + i : ROW_EXPAND + i + 1], row)
    h = dot_nn(n2_ref[...], w1_ref[...]) + row
    sq = h * h
    t = jnp.tanh(h * (GELU_A + (GELU_A * GELU_B) * sq))
    side = 0.5 + 0.5 * t
    act_ref[...] = (h * side).astype(BF16)
    slope_ref[...] = (
        side + (h * (0.5 - 0.5 * t * t)) * (GELU_A + (3.0 * GELU_A * GELU_B) * sq)
    ).astype(BF16)
    feed[...] += dot_nn(act_ref[...], w2_ref[...])

    @pl.when(j == STEPS - 1)
    def _():
        feed_out = feed[...]
        sout = smid_ref[...] + feed_out
        sout_ref[...] = sout
        unit, _ = unit_of(sout)
        n3_ref[...] = (
            unit * par_ref[ROW_GAIN + 2 : ROW_GAIN + 3] + par_ref[ROW_SHIFT + 2 : ROW_SHIFT + 3]
        ).astype(BF16)
        vals = dot_nt(n3_ref[...], wh_ref[...]) + ho_ref[0:1]
        l = [vals[:, q * LANES : (q + 1) * LANES] for q in range(MODEL_TALLY)]
        top = jnp.maximum(jnp.maximum(l[0], l[1]), l[2])
        p = [jnp.exp(v - top) for v in l]
        total = p[0] + p[1] + p[2]
        for q in range(MODEL_TALLY):
            blend_ref[q] = p[q] / total
        blend_ref[MODEL_TALLY] = vals[:, MODEL_TALLY * LANES :]
        valid = (bias_ref[:, :1].astype(F32) == 0.0).astype(F32)
        stat_ref[0:1] = column_sum(feed_out * feed_out * valid)
        stat_ref[1:2] = column_sum(sout * sout * valid)
        stat_ref[2:3] = jnp.broadcast_to(column_sum(valid), (1, D)) * (1.0 / D)
        stat_ref[3:8] = jnp.zeros((5, D), F32)


def feed(smid, bias, par, w1, w2, wh, ho, deps=()):
    tokens = smid.shape[0]
    outs = [
        shaped((tokens, D), BF16),
        shaped((tokens, FF), BF16),
        shaped((tokens, FF), BF16),
        shaped((tokens, D), F32),
        shaped((tokens, D), BF16),
        shaped((4, tokens, LANES), F32),
        shaped((8, D), F32),
    ]
    out_specs = [fixed(v.shape) for v in outs]
    out_specs[1] = out_specs[2] = by_column(tokens, D)
    return call(
        feed_kernel,
        (smid, bias, par, w1, w2, wh, ho),
        [fixed((tokens, D)), fixed(bias.shape), fixed(par.shape), by_column(D, D), by_row(D, D)]
        + [fixed(wh.shape), fixed(ho.shape)],
        outs,
        out_specs=out_specs,
        grid=(STEPS,),
        scratch=[VMEM((tokens, D), F32)],
        vmem=VMEM_MIB,
        name="feed",
        us=12.0,
        deps=deps,
    )


def head_back_kernel(
    place_ref, blend_ref, gw_ref, gs_ref, wh_ref, sout_ref, par_ref, act_ref,
    hlow_ref, gout_ref, vec_ref, *rest, n, stages,
):
    shares, (flow, quarter, cgrad, blocks) = rest[:-4], rest[-4:]
    e, me = place_ref[0], place_ref[1]

    def by_token(v):
        tall = jnp.concatenate([v, jnp.zeros((LANES - HEAD_ROWS, v.shape[1]), F32)], axis=0)
        return jnp.transpose(tall)

    weights = [by_token(gw_ref[q]) for q in range(MODEL_TALLY)]
    inner = 0.0
    for q in range(MODEL_TALLY):
        inner = inner + blend_ref[q] * weights[q]
    vec_ref[...] = jnp.zeros_like(vec_ref)
    for q in range(MODEL_TALLY + 1):
        cols = slice(q * LANES, (q + 1) * LANES)
        g = by_token(gs_ref[...]) if q == MODEL_TALLY else blend_ref[q] * (weights[q] - inner)
        vec_ref[0:1, cols] = column_sum(g)
        hlow_ref[:, cols] = g.astype(BF16)
    gn3 = dot_nn(hlow_ref[...], wh_ref[...])
    unit, inverse = unit_of(sout_ref[...])
    g = norm_back(gn3, unit, inverse, par_ref[ROW_GAIN + 2 : ROW_GAIN + 3])
    gout_ref[...] = g
    flow[...] = g.astype(BF16)
    vec_ref[1:2] = column_sum(gn3 * unit)
    vec_ref[2:3] = column_sum(gn3)
    vec_ref[3:4] = column_sum(g)
    thin = D // 4
    for here in range(4):

        @pl.when(e == here)
        def _():
            quarter[...] = flow[:, here * thin : (here + 1) * thin]

    size, rows = FF // n, D // n
    clear_spare(blocks, rows)
    cgrad[...] = dot_tn(quarter[...], act_ref[...])
    for d in range(n):
        for i in range(n // 4):
            part = cgrad[i * rows : (i + 1) * rows, d * size : (d + 1) * size]
            blocks[d, :rows, i * size : (i + 1) * size] = part
    store_blocks(blocks, me, shares, stages, slice(None), D, 0)


def head_back(place, blend, gw, gs, wh, sout, par, act, n, stages, deps=()):
    tokens = sout.shape[0]
    return call(
        functools.partial(head_back_kernel, n=n, stages=stages),
        (place, blend, gw, gs, wh, sout, par, act),
        [scalars()] + [whole()] * 7,
        [shaped((tokens, 4 * LANES), BF16), shaped((tokens, D), F32), shaped((8, D), F32)]
        + share_shapes(n, stages, padded_rows(D // n), D),
        scratch=[
            VMEM((tokens, D), BF16),
            VMEM((tokens, D // 4), BF16),
            VMEM((D // 4, FF), F32),
            VMEM((n, padded_rows(D // n), D), F32),
        ],
        vmem=room(n),
        name="head_back",
        us=7,
        deps=deps,
    )


def feed_back_kernel(
    place_ref, hlow_ref, gout_ref, n3_ref, par_ref, slope_ref, n2_ref, smid_ref, w1_ref, w2_ref,
    gmid_ref, vec_ref, *rest, n, stages,
):
    shares, (flow, hid, mine, gn2, grad) = rest[:-5], rest[-5:]
    j = pl.program_id(0)
    e, me = place_ref[0], place_ref[1]

    @pl.when(j == 0)
    def _():
        flow[...] = gout_ref[...].astype(BF16)
        vec_ref[...] = jnp.zeros_like(vec_ref)
        gn2[...] = jnp.zeros_like(gn2)

    h = dot_nt(flow[...], w2_ref[...]) * slope_ref[...].astype(F32)
    sums = column_sum(h)
    for i in range(STEPS):

        @pl.when(j == i)
        def _():
            vec_ref[i : i + 1] = sums

    hid[...] = h.astype(BF16)

    @pl.when(j == e)
    def _():
        mine[...] = hid[...]

    gn2[...] += dot_nt(hid[...], w1_ref[...])

    @pl.when(j == STEPS - 1)
    def _():
        clear_spare(grad, D // n)
        put_blocks(grad, dot_tn(n2_ref[...], mine[...]), n)
        store_blocks(grad, me, shares, stages, slice(None), D, 0)
        put_blocks(grad, dot_tn(n3_ref[...], hlow_ref[:, pl.ds(pl.multiple_of(e * LANES, LANES), LANES)]), n)
        store_blocks(grad, me, shares, stages, slice(None), LANES, D)
        unit, inverse = unit_of(smid_ref[...])
        y = gn2[...]
        gmid_ref[...] = gout_ref[...] + norm_back(y, unit, inverse, par_ref[ROW_GAIN + 1 : ROW_GAIN + 2])
        vec_ref[4:5] = column_sum(y * unit)
        vec_ref[5:6] = column_sum(y)


def feed_back(place, hlow, gout, n3, par, slope, n2, smid, w1, w2, n, stages, deps=()):
    tokens = smid.shape[0]
    rows = padded_rows(D // n)
    outs = [shaped((tokens, D), F32), shaped((8, D), F32)] + share_shapes(n, stages, rows, D + LANES)
    return call(
        functools.partial(feed_back_kernel, n=n, stages=stages),
        (place, hlow, gout, n3, par, slope, n2, smid, w1, w2),
        [scalars()]
        + [fixed(v.shape) for v in (hlow, gout, n3, par)]
        + [by_column(tokens, D), fixed(n2.shape), fixed(smid.shape), by_column(D, D), by_row(D, D)],
        outs,
        out_specs=[fixed(v.shape) for v in outs],
        grid=(STEPS,),
        scratch=[
            VMEM((tokens, D), BF16),
            VMEM((tokens, D), BF16),
            VMEM((tokens, D), BF16),
            VMEM((tokens, D), F32),
            VMEM((n, rows, D), F32),
        ],
        vmem=room(n),
        name="feed_back",
        us=13.0,
        deps=deps,
    )


def fold_kernel(*refs, counts, parts, axis):
    outs = refs[sum(counts) :]
    ins, at = 0, 0
    for g, count in enumerate(counts):
        total = refs[ins][...].astype(F32)
        for i in range(1, count):
            total = total + refs[ins + i][...].astype(F32)
        ins += count
        size = total.shape[0] // parts
        for p in range(parts):
            piece = total[p * size : (p + 1) * size].astype(outs[p].dtype)
            if axis is None:
                outs[g * parts + p][...] = piece
            elif axis == 1:
                outs[p][:, at : at + piece.shape[1]] = piece
            else:
                outs[p][:, :, at : at + piece.shape[2]] = piece
        if axis is not None:
            at += total.shape[axis]


def fold(groups, parts, axis=None, deps=()):
    shapes = [g[0].shape for g in groups]
    dtype = groups[0][0].dtype
    size = shapes[0][0] // parts
    if axis is None:
        outs = [shaped((size,) + v[1:], dtype) for v in shapes for _ in range(parts)]
    else:
        full = list(shapes[0])
        full[0], full[axis] = size, sum(v[axis] for v in shapes)
        outs = [shaped(tuple(full), dtype)] * parts
    inputs = [v for g in groups for v in g]
    return call(
        functools.partial(fold_kernel, counts=[len(g) for g in groups], parts=parts, axis=axis),
        inputs,
        [whole()] * len(inputs),
        outs,
        name="fold",
        us=1.3,
        deps=deps,
    )


def fold_sums_kernel(*refs, first, parts):
    sums = refs[0:2]
    before = refs[2:4] if first else ()
    outs = refs[2 + len(before) :]
    count, rows, cols = sums[0].shape
    size = sum_columns(rows, count)
    vec = get_sums(sums[0][:, :, cols - size :]) + get_sums(sums[1][:, :, cols - size :])
    at = 0
    for pair in (before, sums):
        if pair:
            total = pair[0][...].astype(F32) + pair[1][...].astype(F32)
            wide = total.shape[2] - (size if pair is sums else 0)
            for p in range(parts):
                half = total[p * (count // parts) : (p + 1) * (count // parts), :, :wide]
                outs[p][:, :, at : at + wide] = half.astype(BF16)
            at += wide
    if parts == 1:
        outs[1][...] = vec
    else:
        put_sums(vec, outs[:parts])


def fold_sums(keep, got, parts, first=None, deps=()):
    count, rows, cols = keep.shape
    wide = cols - sum_columns(rows, count) + (first[0].shape[2] if first else 0)
    if parts == 1:
        outs = [shaped((1, rows, wide), BF16), shaped((rows, SUMS * D // rows), F32)]
    else:
        outs = [shaped((count // parts, rows, wide + sum_columns(rows, count // parts)), BF16)] * parts
    inputs = [keep, got] + (list(first) if first else [])
    return call(
        functools.partial(fold_sums_kernel, first=bool(first), parts=parts),
        inputs,
        [whole()] * len(inputs),
        outs,
        name="fold_sums",
        us=1.3,
        deps=deps,
    )


def assemble_kernel(place_ref, *refs, n):
    parts = refs[0:4]
    contract, expand, head, triple, result = refs[4:]
    e = place_ref[0]
    rows, size, thin, wide = D // n, FF // n, D // 4, 3 * D // 4
    last = 2 * D + LANES
    for here in range(4):

        @pl.when(e == here)
        def _():
            for i in range(4):
                part = parts[here ^ i]
                for j in range(n // 4):
                    block = jnp.transpose(part[0, :, j * size : (j + 1) * size].astype(F32))
                    contract[:, i * thin + j * rows : i * thin + (j + 1) * rows] = block[:, :rows]
                expand[:, i * D : (i + 1) * D] = part[0, :rows, D : 2 * D].astype(F32)
                head[:, i * CHANNELS : (i + 1) * CHANNELS] = part[0, :rows, 2 * D : 2 * D + CHANNELS].astype(F32)
                triple[:, i * wide : (i + 1) * wide] = part[0, :rows, last : last + wide].astype(F32)
                result[:, i * thin : (i + 1) * thin] = part[0, :rows, last + wide :].astype(F32)


def assemble(place, parts, n, deps=()):
    rows = D // n
    return call(
        functools.partial(assemble_kernel, n=n),
        (place, *parts),
        [scalars()] + [whole()] * 4,
        [
            shaped((FF // n, D), F32),
            shaped((rows, FF), F32),
            shaped((rows, 4 * CHANNELS), F32),
            shaped((rows, 3 * D), F32),
            shaped((rows, D), F32),
        ],
        name="assemble",
        us=2.5,
        deps=deps,
    )


def assemble_last_kernel(place_ref, p0, p1, p2, p3, lift, *, step, width):
    parts = (p0, p1, p2, p3)
    e = place_ref[0]
    for here in range(4):

        @pl.when(e == here)
        def _():
            for i in range(4):
                take = step if i < 3 else width
                lift[i * step : i * step + take] = parts[here ^ i][0, :take].astype(F32)


def assemble_last(place, parts, step, width, deps=()):
    return call(
        functools.partial(assemble_last_kernel, step=step, width=width),
        (place, *parts),
        [scalars()] + [whole()] * 4,
        shaped((3 * step + width, D), F32),
        name="assemble_last",
        us=2,
        deps=deps,
    )


THIRD = CHANNELS // 3


def channel_sums(pred_ref, adj_ref, first, channels, at, gw_ref, gs_ref):
    for i in range(channels):
        here = slice((first + i) * PIXELS, (first + i + 1) * PIXELS)
        adj = adj_ref[i * PIXELS : (i + 1) * PIXELS].astype(F32)
        gw_ref[first + i : first + i + 1, at] = column_sum(adj * pred_ref[here, at].astype(F32))
        gs_ref[first + i : first + i + 1, at] = column_sum(adj)


def weigh_near_kernel(place_ref, pred_ref, a0, a1, gw_ref, gs_ref):
    e = place_ref[0]
    rows = a0.shape[1]
    gw_ref[CHANNELS:] = jnp.zeros_like(gw_ref[CHANNELS:])
    gs_ref[CHANNELS:] = jnp.zeros_like(gs_ref[CHANNELS:])
    for k, a in enumerate((a0, a1)):
        at = pl.ds(pl.multiple_of((e ^ k) * rows, rows), rows)
        channel_sums(pred_ref, a, 0, CHANNELS, at, gw_ref, gs_ref)


def weigh_near(place, pred, adjoints, deps=()):
    tokens = pred.shape[1]
    return call(
        weigh_near_kernel,
        (place, pred, *adjoints),
        [scalars()] + [whole()] * 3,
        [shaped((HEAD_ROWS, tokens), F32)] * 2,
        name="weigh_near",
        us=3.6,
        deps=deps,
    )


def weigh_far_kernel(place_ref, pred_hbm, a2, a3, gw_in, gs_in, gw_ref, gs_ref, pred, sem):
    e = place_ref[0]
    rows = a2.shape[1]
    at = pl.ds(pl.multiple_of((e // 2) * 2 * rows, 2 * rows), 2 * rows)
    pair = pl.ds(pl.multiple_of((1 - e // 2) * 2 * rows, 2 * rows), 2 * rows)
    load = pltpu.make_async_copy(pred_hbm.at[:, pair], pred, sem)
    load.start()
    gw_ref[:, at] = gw_in[:, at]
    gs_ref[:, at] = gs_in[:, at]
    gw_ref[CHANNELS:, pair] = jnp.zeros((HEAD_ROWS - CHANNELS, 2 * rows), F32)
    gs_ref[CHANNELS:, pair] = jnp.zeros((HEAD_ROWS - CHANNELS, 2 * rows), F32)
    load.wait()
    for k, adj_ref in ((2, a2), (3, a3)):
        token = e ^ k
        own = pl.ds(pl.multiple_of(token * rows, rows), rows)
        inner = pl.ds(pl.multiple_of((token & 1) * rows, rows), rows)
        for i in range(CHANNELS):
            here = slice(i * PIXELS, (i + 1) * PIXELS)
            adj = adj_ref[here].astype(F32)
            gw_ref[i : i + 1, own] = column_sum(adj * pred[here, inner].astype(F32))
            gs_ref[i : i + 1, own] = column_sum(adj)


def weigh_far(place, pred, adjoints, gw, gs, deps=()):
    tokens = pred.shape[1]
    return call(
        weigh_far_kernel,
        (place, pred, *adjoints, gw, gs),
        [scalars(), in_hbm()] + [whole()] * 4,
        [shaped((HEAD_ROWS, tokens), F32)] * 2,
        scratch=[VMEM((TILE_ENTRIES, tokens // 2), BF16), pltpu.SemaphoreType.DMA],
        vmem=VMEM_MIB,
        name="weigh_far",
        us=2,
        deps=deps,
    )


def split_two(v, axis=0):
    hi = v.astype(BF16)
    return jnp.concatenate([hi, (v - hi.astype(F32)).astype(BF16)], axis=axis)


def by_rows(refs):
    pieces = [(0, refs[0], 0), (1, refs[1], 0)]
    for k in (2, 3):
        first = 0
        for ref in refs[2 + 3 * (k - 2) : 5 + 3 * (k - 2)]:
            pieces.append((k, ref, first))
            first += ref.shape[0]
    return pieces


def blend_kernel(place_ref, blend_ref, *rest):
    columns, spread_ref, outs, acc = rest[:8], rest[8], rest[9:13], rest[13]
    e = place_ref[0]
    rows = outs[0].shape[1]
    acc[...] = dot_nn(
        jnp.concatenate([spread_ref[...]] * 2, axis=1), split_two(jnp.transpose(blend_ref[MODEL_TALLY]))
    )
    for k, c, first in by_rows(columns):
        q = e ^ k

        @pl.when(q < MODEL_TALLY)
        def _():
            at = slice(first, first + c.shape[0])
            spread = jnp.concatenate([spread_ref[at]] * 2, axis=1)
            acc[at] += dot_nn(spread, split_two(jnp.transpose(blend_ref[q]))) * c[...].astype(F32)

    for k, o in enumerate(outs):
        at = pl.multiple_of((e ^ k) * rows, rows)
        o[...] = acc[:, pl.ds(at, rows)].astype(BF16)


def blend_columns(place, blend, columns, spread, deps=()):
    cols, tokens = columns[0].shape
    rows = tokens // 4
    return call(
        blend_kernel,
        (place, blend, *columns, spread),
        [scalars()] + [whole()] * 10,
        [shaped((cols, rows), BF16)] * 4,
        scratch=[VMEM((cols, tokens), F32)],
        name="blend",
        us=20,
        deps=deps,
    )


def lift_grad_kernel(place_ref, low_ref, masks_ref, *rest, n, stages, cut):
    columns, shares, grad = rest[:8], rest[8:-1], rest[-1]
    e, me = place_ref[0], place_ref[1]
    masks = jnp.transpose(masks_ref[...])
    low = low_ref[...].astype(F32)
    rows = grad.shape[1]
    grad[...] = jnp.zeros_like(grad)
    for k, c, first in by_rows(columns):

        @pl.when((e ^ k) < MODEL_TALLY)
        def _():
            part = dot_nn(c[...], (low * masks[:, k : k + 1]).astype(BF16))
            for i in range(c.shape[0] // rows):
                grad[first // rows + i] += part[i * rows : (i + 1) * rows]

    parts = len(shares) // 2
    store_blocks(grad, me, shares[:parts], stages, slice(0, cut), D, 0)
    store_blocks(grad, me, shares[parts:], stages, slice(cut, rows), D, 0)


def lift_grad(place, low, masks, columns, n, stages, deps=()):
    cols, tokens = columns[0].shape
    rows = cols // n
    cut = padded_rows(rows // 2)
    return call(
        functools.partial(lift_grad_kernel, n=n, stages=stages, cut=cut),
        (place, low, masks, *columns),
        [scalars()] + [whole()] * 10,
        share_shapes(n, stages, cut, D) + share_shapes(n, stages, rows - cut, D),
        scratch=[VMEM((n, rows, D), F32)],
        vmem=room(n),
        name="lift_grad",
        us=30,
        deps=deps,
    )


def slope_kernel(place_ref, low_ref, masks_ref, blend_ref, lift_ref, a0, a1, a2, a3, *rest, which):
    out_ref, acc = rest[-2], rest[-1]
    e = place_ref[0]
    rows = a0.shape[1]
    masks = jnp.transpose(masks_ref[...])
    low = (low_ref[...].astype(F32) * masks[:, :1]).astype(BF16)
    active = jnp.where(e < MODEL_TALLY, 1.0, 0.0)
    weights = jnp.transpose(blend_ref[jnp.minimum(e, MODEL_TALLY - 1)] * active)
    acc[...] = dot_nt(lift_ref[...], low)
    first = which * THIRD
    for k, a in enumerate((a0, a1, a2, a3)):
        for b in range(4):

            @pl.when((e ^ k) == b)
            def _():
                at = slice(b * rows, (b + 1) * rows)
                for i in range(THIRD):
                    here = slice(i * PIXELS, (i + 1) * PIXELS)
                    weight = weights[first + i : first + i + 1, at]
                    out_ref[here, at] = (acc[here, at] + weight * a[here].astype(F32)).astype(BF16)


def slope(which, before, place, low, masks, blend, lift, adjoints, deps=()):
    tokens = low.shape[0]
    rows = adjoints[0].shape[1]
    size = THIRD * PIXELS
    third = lambda cols: pl.BlockSpec((size, cols), lambda j: (which, 0))
    inputs = [place, low, masks, blend, lift, *adjoints]
    in_specs = [scalars(), fixed((tokens, D)), fixed(masks.shape), fixed(blend.shape), third(D)]
    in_specs += [third(rows)] * 4
    aliases = {}
    if before is not None:
        aliases = {len(inputs): 0}
        inputs.append(before)
        in_specs.append(in_hbm())
    return call(
        functools.partial(slope_kernel, which=which),
        inputs,
        in_specs,
        shaped((TILE_ENTRIES, tokens), BF16),
        grid=(1,),
        out_specs=third(tokens),
        scratch=[VMEM((size, tokens), F32)],
        aliases=aliases,
        name="slope",
        us=4.3,
        deps=deps,
    )


def expert_swap(v, k):
    size = lax.axis_size("expert")
    return lax.ppermute(v, "expert", [(i, i ^ k) for i in range(size)])


def frame_swap(v, k):
    size = lax.axis_size("dp")
    return lax.ppermute(v, "dp", [(i, i ^ k) for i in range(size)])


def gather_four(v):
    across = expert_swap(v, 2)
    return [v, expert_swap(v, 1), across, expert_swap(across, 1)]


def in_order(parts, e):
    odd = (e & 1) == 1
    high = (e & 2) == 2
    a, b, c, d = parts
    a, b, c, d = (
        jnp.where(odd, b, a),
        jnp.where(odd, a, b),
        jnp.where(odd, d, c),
        jnp.where(odd, c, d),
    )
    return [jnp.where(high, c, a), jnp.where(high, d, b), jnp.where(high, a, c), jnp.where(high, b, d)]


def local(
    model_predictions,
    member_tile_presence,
    piece_usable_flags,
    horizon_positions,
    result_adjoint,
    tile_lift_matrix,
    tile_lift_offset,
    horizon_lookup,
    normalizer_scales,
    normalizer_offsets,
    query_key_value_matrix,
    attend_result_matrix,
    attend_offset_vector,
    expand_matrix,
    expand_offset,
    contract_matrix,
    contract_offset,
    mixing_head_matrix,
    mixing_head_offset,
):
    n = lax.axis_size("dp")
    e = lax.axis_index("expert")
    place = jnp.stack([e, lax.axis_index("dp")]).astype(jnp.int32)
    core = e & 1
    active = (e < MODEL_TALLY).astype(F32)
    pred = jnp.transpose(model_predictions[0])
    tokens = pred.shape[1]
    block = TILE_ENTRIES // n
    step = block // 4 // 8 * 8 if block % 8 == 0 else block // 4
    width = block - 3 * step
    padded = padded_rows(width)

    adjoint = jnp.transpose(result_adjoint)
    near = expert_swap(adjoint, 1)
    far = expert_swap(adjoint, 2)

    mask = member_tile_presence.astype(F32) * active
    own_part, other_part, _ = embed(place, mask, pred, tile_lift_matrix)

    info = jnp.concatenate([mask, piece_usable_flags.astype(F32)[None]], axis=1)
    infos = [info] + [expert_swap(info, k) for k in (1, 2, 3)]
    masks = jnp.concatenate([v[:, :tokens] for v in infos] + [jnp.zeros((4, tokens), F32)], axis=0)
    valid = jnp.concatenate([v[0, tokens:] for v in in_order(infos, e)])
    first = jnp.arange(LANES) == 0
    bias = jnp.where((valid[:, None] == 0) & first[None, :], MASKED_SCORE, 0.0).astype(BF16)

    lead_hot = (jnp.arange(horizon_lookup.shape[0]) == horizon_positions[0]).astype(F32)
    lead_vector = jnp.sum(lead_hot[:, None] * horizon_lookup.astype(F32), axis=0)
    par = jnp.concatenate(
        [
            tile_lift_offset[None].astype(F32),
            normalizer_scales.astype(F32),
            normalizer_offsets.astype(F32),
            attend_offset_vector[None].astype(F32),
            contract_offset[None].astype(F32),
            expand_offset.reshape(FF // D, D).astype(F32),
            lead_vector[None],
            jnp.zeros((PARAM_ROWS - ROW_HEAD, D), F32),
        ],
        axis=0,
    )
    over = (0, LANES - CHANNELS)
    head = jnp.pad(jnp.transpose(mixing_head_matrix).reshape(4, CHANNELS, D), ((0, 0), over, (0, 0)))
    head = head.reshape(4 * LANES, D)
    head_row = jnp.pad(mixing_head_offset.astype(F32).reshape(1, 4, CHANNELS), ((0, 0), (0, 0), over))
    head_row = head_row.reshape(1, 4 * LANES)
    at = jnp.arange(n * padded)
    channel = ((at // padded) * block + e * step + at % padded) // PIXELS
    spread = (channel[:, None] == jnp.arange(LANES)[None, :]).astype(BF16)

    pair, done = fold([[own_part, expert_swap(other_part, 1)]], 1)
    other = expert_swap(own_part, 1)
    across = expert_swap(pair, 2)
    across_other = expert_swap(across, 1)

    mine, grad_shift, done = weigh_near(place, pred, [adjoint, near], deps=[done, par, bias, head, head_row, spread, masks])
    *pieces, far, done = pack(place, pred, far, n, step, width, padded, deps=[done, across])
    far_near = expert_swap(far, 1)
    adjoints = [adjoint, near, far, far_near]
    sin, n1, queries, keys, values, mixed, smid, lse, stat_a, done = attend(
        place, pair, other_part, other, across, across_other, bias, par, query_key_value_matrix, attend_result_matrix, deps=[done]
    )
    columns = [pieces[0], expert_swap(pieces[1], 1)] + [expert_swap(v, 2 + i // 3) for i, v in enumerate(pieces[2:])]
    mine, grad_shift, done = weigh_far(
        place, pred, adjoints[2:], mine, grad_shift, deps=[done, columns[1], columns[2], columns[5]]
    )
    all_mine = [mine] + [expert_swap(mine, k) for k in (1, 2, 3)]
    n2, act, gelu_slope, sout, n3, blend, stat_b, done = feed(
        smid, bias, par, expand_matrix, contract_matrix, head, head_row, deps=[done]
    )
    grad_weights = jnp.stack(in_order(all_mine, e)[:MODEL_TALLY])

    stages = stages_of(n)
    last_bit = len(stages) - 1

    def onward(keep, got, bit, deps):
        keep, send, done = fold([[keep, got]], 2, deps=deps)
        return keep, frame_swap(send, 1 << bit), done

    hlow, gout, vec_h, ckeep, csend, done = head_back(
        place, blend, grad_weights, grad_shift, head, sout, par, act, n, stages, deps=[done]
    )
    cgot = frame_swap(csend, 1)
    gmid, vec_f, tkeep, tsend, done = feed_back(
        place, hlow, gout, n3, par, gelu_slope, n2, smid, expand_matrix, contract_matrix, n, stages,
        deps=[done],
    )
    tgot = frame_swap(tsend, 1)
    hot = jnp.broadcast_to(lead_hot[:, None], (lead_hot.shape[0], LANES))
    low, qkeep, qsend, done = attend_back(
        place, gmid, attend_result_matrix, queries, keys, values, lse, bias, n1, mixed, sin, par,
        query_key_value_matrix, [vec_h, vec_f, stat_a, stat_b, hot], n, stages, deps=[done, cgot, columns[3], columns[6]],
    )
    qgot = frame_swap(qsend, 1)
    keep, send, done = fold([[ckeep, cgot], [tkeep, tgot]], 2, axis=2, deps=[done])
    got = frame_swap(send, 2)
    akeep, asend, bkeep, bsend, done = lift_grad(place, low, masks, columns, n, stages, deps=[done])
    agot = frame_swap(asend, 1)
    bgot = frame_swap(bsend, 1)
    slopes = [place, low, masks, blend, tile_lift_matrix, adjoints]
    *outgoing, done = blend_columns(place, blend, columns, spread, deps=[done])
    arrived = [outgoing[0]] + [expert_swap(outgoing[k], k) for k in (1, 2, 3)]
    qkeep, qsend, done = fold_sums(qkeep, qgot, 2, deps=[done])
    qgot = frame_swap(qsend, 2)
    part_slope, done = slope(0, None, *slopes, deps=[done])
    akeep, agot, done = onward(akeep, agot, 1, [done])
    keep, send, done = fold_sums(qkeep, qgot, 2, first=[keep, got], deps=[done])
    got = frame_swap(send, 4)
    combined, done = unpack(place, arrived, n, step, width, padded, deps=[done])
    combined_prediction = jnp.transpose(combined)
    part_slope, done = slope(1, part_slope, *slopes, deps=[done])
    bkeep, bgot, done = onward(bkeep, bgot, 1, [done])
    akeep, agot, done = onward(akeep, agot, 2, [done])
    part_slope, done = slope(2, part_slope, *slopes, deps=[done])
    bkeep, bgot, done = onward(bkeep, bgot, 2, [done])
    for bit in range(3, last_bit + 1):
        keep, send, done = fold_sums(keep, got, 2, deps=[done])
        got = frame_swap(send, 1 << bit)
    rows_one, packed, done = fold_sums(keep, got, 1, deps=[done])
    rows_one = gather_four(rows_one)
    packed = packed.reshape(SUMS, D)
    for bit in range(3, last_bit + 1):
        akeep, agot, done = onward(akeep, agot, bit, [done])
        bkeep, bgot, done = onward(bkeep, bgot, bit, [done])
    rows_two, done = fold([[akeep, agot], [bkeep, bgot]], 1, axis=1, deps=[done])
    rows_two = gather_four(rows_two)
    contract_slope, expand_slope, head_slope, triple_slope, result_slope, done = assemble(
        place, rows_one, n, deps=[done]
    )
    lift_slope, _ = assemble_last(place, rows_two, step, width, deps=[done])
    predictions_slope = jnp.transpose(part_slope)[None]

    head_off = packed[0, : 4 * LANES].reshape(4, LANES)[:, :CHANNELS].reshape(4 * CHANNELS)
    total = jnp.sum(packed[14:19], axis=1)
    magnitudes = jnp.sqrt(total[:4] / (total[4] * D) + SQUARE_EPSILON)
    gains = jnp.stack([packed[12], packed[8], packed[1]])
    shifts = jnp.stack([packed[11], packed[9], packed[2]])
    return (
        combined_prediction,
        predictions_slope,
        magnitudes,
        lift_slope,
        packed[10],
        packed[24:32],
        gains,
        shifts,
        triple_slope,
        result_slope,
        packed[13],
        expand_slope,
        packed[4:8].reshape(FF),
        contract_slope,
        packed[3],
        head_slope,
        head_off,
    )


def solution(mesh):
    rows = P(("dp", "expert"), None)
    placed = (
        P("expert", "dp", None),
        P("expert", "dp"),
        P(("dp", "expert")),
        P("dp"),
        rows,
    ) + (P(),) * 14
    given = (
        rows,
        P("expert", "dp", None),
        P(),
        P("dp", None),
        P(),
        P(),
        P(),
        P(),
        P("dp", None),
        P("dp", None),
        P(),
        P("dp", None),
        P(),
        P("dp", None),
        P(),
        P("dp", None),
        P(),
    )
    return jax.shard_map(local, mesh=mesh, in_specs=placed, out_specs=given, check_vma=False)
```

```python
import functools

import jax
import jax.numpy as jnp
from jax import lax
from jax.experimental import pallas as pl
from jax.experimental.pallas import tpu as pltpu
from jax.sharding import PartitionSpec as P

D = 768
HEADS = 12
HEAD_DIM = 64
FF = 3072
MODEL_TALLY = 3
CHANNELS = 69
PIXELS = 64
TILE_ENTRIES = 4416
LANES = 128
PAIRS = HEADS // 2

NORM_EPSILON = 1e-05
SQUARE_EPSILON = 1e-06
MASKED_SCORE = -1e30
GELU_A = 0.7978845608028654
GELU_B = 0.044715
F32 = jnp.float32
BF16 = jnp.bfloat16

ROW_LIFT, ROW_GAIN, ROW_SHIFT, ROW_ATTEND, ROW_CONTRACT, ROW_EXPAND, ROW_LEAD, ROW_HEAD = 0, 1, 4, 7, 8, 9, 13, 14
PARAM_ROWS = 16
HEAD_ROWS = 72
VMEM_MIB = 20
VMEM_SMALL = 12
SCALE = 1e8

VMEM = pltpu.VMEM
SMEM = pltpu.SMEM


def whole():
    return pl.BlockSpec(memory_space=VMEM)


def scalars():
    return pl.BlockSpec(memory_space=SMEM)


def in_hbm():
    return pl.BlockSpec(memory_space=pl.ANY)


def shaped(shape, dtype):
    return jax.ShapeDtypeStruct(shape, dtype)


def dot_nn(a, b):
    return jnp.dot(a, b, preferred_element_type=F32)


def dot_tn(a, b):
    return lax.dot_general(a, b, (((0,), (0,)), ((), ())), preferred_element_type=F32)


def dot_nt(a, b):
    return lax.dot_general(a, b, (((1,), (1,)), ((), ())), preferred_element_type=F32)


def unit_of(values):
    center = values - jnp.mean(values, axis=-1, keepdims=True)
    inverse = lax.rsqrt(jnp.mean(center * center, axis=-1, keepdims=True) + NORM_EPSILON)
    return center * inverse, inverse


def norm_back(grad_out, unit, inverse, gain):
    scaled = grad_out * gain
    return inverse * (
        scaled
        - jnp.mean(scaled, axis=-1, keepdims=True)
        - unit * jnp.mean(scaled * unit, axis=-1, keepdims=True)
    )


def column_sum(v):
    return jnp.sum(v, axis=0, keepdims=True)


def room(n):
    return VMEM_MIB if (D // n) % 16 == 0 else VMEM_MIB + 24


def fixed(shape):
    return pl.BlockSpec(shape, lambda *_: (0,) * len(shape))


def taking(us):
    return pl.CostEstimate(flops=int(us * SCALE), bytes_accessed=1000, transcendentals=0)


def call(
    body, inputs, in_specs, outs, scratch=(), vmem=VMEM_MIB, grid=None, out_specs=None, name=None, deps=(), us=1.0,
    aliases=None,
):
    kwargs = {}
    if grid is not None:
        kwargs["grid"] = grid
    if aliases:
        kwargs["input_output_aliases"] = aliases
    outs = list(outs) if isinstance(outs, (list, tuple)) else [outs]
    if out_specs is None:
        out_specs = [whole() for _ in outs]
    out_specs = list(out_specs) if isinstance(out_specs, (list, tuple)) else [out_specs]
    count = len(inputs)

    def kernel(*refs):
        given = count + len(deps)
        body(*refs[:count], *refs[given : given + len(outs)], *refs[given + len(outs) + 1 :])
        token = refs[given + len(outs)]
        token[...] = jnp.zeros_like(token)

    return pl.pallas_call(
        kernel,
        out_shape=outs + [shaped((8, LANES), F32)],
        in_specs=list(in_specs) + [in_hbm() for _ in deps],
        out_specs=out_specs + [whole() if grid is None else fixed((8, LANES))],
        scratch_shapes=list(scratch),
        compiler_params=pltpu.CompilerParams(vmem_limit_bytes=vmem * 1024 * 1024),
        cost_estimate=taking(us),
        name=name,
        **kwargs,
    )(*inputs, *deps)


def embed_kernel(place_ref, mask_ref, pred_hbm, lift_hbm, own_ref, other_ref, pred, lift, acc, sems, *, cuts):
    copies = []
    for i, (a, b) in enumerate(cuts):
        one = pltpu.make_async_copy(pred_hbm.at[a:b], pred.at[a:b], sems.at[0, i])
        two = pltpu.make_async_copy(lift_hbm.at[a:b], lift.at[a:b], sems.at[1, i])
        one.start()
        two.start()
        copies.append((one, two))
    for i, (a, b) in enumerate(cuts):
        for copy in copies[i]:
            copy.wait()
        part = dot_tn(pred[a:b], lift[a:b])
        if i == 0:
            acc[...] = part
        elif i < len(cuts) - 1:
            acc[...] += part
        else:
            mask = jnp.transpose(jnp.broadcast_to(mask_ref[...], (8, mask_ref.shape[1])))[:, :1]
            acc[...] = (acc[...] + part) * mask
            half = own_ref.shape[0]
            core = place_ref[0] & 1
            own_ref[...] = acc[pl.ds(pl.multiple_of(core * half, half), half)].astype(BF16)
            other_ref[...] = acc[pl.ds(pl.multiple_of((1 - core) * half, half), half)].astype(BF16)


def embed(place, mask, pred, lift):
    tokens = pred.shape[1]
    cuts = [(0, 768), (768, 1536), (1536, 2560), (2560, 3584), (3584, TILE_ENTRIES)]
    return call(
        functools.partial(embed_kernel, cuts=cuts),
        (place, mask, pred, lift),
        [scalars(), whole(), in_hbm(), in_hbm()],
        [shaped((tokens // 2, D), BF16)] * 2,
        scratch=[
            VMEM((TILE_ENTRIES, tokens), BF16),
            VMEM((TILE_ENTRIES, D), BF16),
            VMEM((tokens, D), F32),
            pltpu.SemaphoreType.DMA((2, len(cuts))),
        ],
        vmem=60,
        name="embed",
        us=7.5,
    )


def cuts_of(n):
    return [0, n // 4, n // 4 + 3 * n // 8, n]


def pack_kernel(place_ref, pred_ref, far_ref, *outs, n, step, width, padded):
    outs[-1][...] = far_ref[...]
    e = place_ref[0]
    tokens = pred_ref.shape[1]
    block = TILE_ENTRIES // n
    cuts = cuts_of(n)
    for here in range(4):

        @pl.when(e == here)
        def _():
            for k in range(4):
                q = here ^ k
                for d in range(n):
                    out, first = outs[min(k, 2)], 0
                    if k >= 2:
                        piece = max(i for i in range(3) if cuts[i] <= d)
                        out, first = outs[2 + 3 * (k - 2) + piece], cuts[piece]
                    at = (d - first) * padded
                    start = d * block + q * step
                    out[at : at + width] = pred_ref[start : start + width]
                    if padded > width:
                        out[at + width : at + padded] = jnp.zeros((padded - width, tokens), BF16)


def pack(place, pred, far, n, step, width, padded, deps=()):
    tokens = pred.shape[1]
    cuts = cuts_of(n)
    thirds = [shaped(((cuts[i + 1] - cuts[i]) * padded, tokens), BF16) for i in range(3)]
    return call(
        functools.partial(pack_kernel, n=n, step=step, width=width, padded=padded),
        (place, pred, far),
        [scalars(), whole(), whole()],
        [shaped((n * padded, tokens), BF16)] * 2 + thirds * 2 + [shaped(far.shape, BF16)],
        name="pack",
        us=2,
        deps=deps,
    )


def unpack_kernel(place_ref, *refs, n, step, width, padded):
    parts, out = refs[:4], refs[4]
    e = place_ref[0]
    block = TILE_ENTRIES // n
    for here in range(4):

        @pl.when(e == here)
        def _():
            for q in range(4):
                take = step if q < 3 else width
                for d in range(n):
                    start = d * block + q * step
                    out[start : start + take] = parts[here ^ q][d * padded : d * padded + take]


def unpack(place, parts, n, step, width, padded, deps=()):
    rows = parts[0].shape[1]
    return call(
        functools.partial(unpack_kernel, n=n, step=step, width=width, padded=padded),
        (place, *parts),
        [scalars()] + [whole()] * 4,
        shaped((TILE_ENTRIES, rows), BF16),
        name="unpack",
        us=2,
        deps=deps,
    )


def lane_side(shape):
    return lax.broadcasted_iota(jnp.int32, shape, 1) // HEAD_DIM


GROUPS = 3
WIDTH = D // GROUPS


def attend_kernel(
    place_ref, own_ref, mine_ref, other_ref, across_ref, across_other_ref, bias_ref, par_ref,
    wq_ref, wk_ref, wv_ref, wo_ref,
    sin_ref, n1_ref, q_ref, k_ref, v_ref, mixed_ref, smid_ref, lse_ref, stat_ref,
):
    j = pl.program_id(0)
    core = place_ref[0] & 1
    tokens = bias_ref.shape[0]
    half = tokens // 2

    @pl.when(j == 0)
    def _():
        gain = par_ref[ROW_GAIN : ROW_GAIN + 1]
        shift = par_ref[ROW_SHIFT : ROW_SHIFT + 1] + par_ref[ROW_LEAD : ROW_LEAD + 1]
        offset = par_ref[ROW_LIFT : ROW_LIFT + 1]
        other = (mine_ref[...].astype(F32) + other_ref[...].astype(F32)).astype(BF16)
        for side, near, far in ((core, own_ref[...], across_ref), (1 - core, other, across_other_ref)):
            rows = pl.ds(pl.multiple_of(side * half, half), half)
            s = near.astype(F32) + far[...].astype(F32) + offset
            sin_ref[rows] = s
            smid_ref[rows] = s + par_ref[ROW_ATTEND : ROW_ATTEND + 1]
            unit, _ = unit_of(s)
            n1_ref[rows] = (unit * gain + shift).astype(BF16)

    n1 = n1_ref[...]
    q_ref[...] = dot_nn(n1, wq_ref[...]).astype(BF16)
    k_ref[...] = dot_nn(n1, wk_ref[...]).astype(BF16)
    v_ref[...] = dot_nn(n1, wv_ref[...]).astype(BF16)
    side_of = lane_side((tokens, LANES))
    one = (lax.broadcasted_iota(jnp.int32, (tokens, LANES), 1) == 0).astype(BF16)
    bias = bias_ref[...]
    for pair in range(WIDTH // LANES):
        at = slice(pair * LANES, (pair + 1) * LANES)
        q = q_ref[:, at] * BF16(HEAD_DIM ** -0.5)
        keys = jnp.concatenate([k_ref[:, at], bias], axis=1)
        vt = jnp.transpose(v_ref[:, at])
        outs = []
        for a in range(2):
            qa = jnp.concatenate([jnp.where(side_of == a, q, BF16(0)), one], axis=1)
            s = dot_nt(keys, qa)
            top = jnp.max(s, axis=0, keepdims=True)
            p = jnp.exp(s - top)
            total = jnp.sum(p, axis=0, keepdims=True)
            lse_ref[pair, a : a + 1, :] = top + jnp.log(total)
            o = dot_nn(vt[a * HEAD_DIM : (a + 1) * HEAD_DIM], p.astype(BF16))
            outs.append(o * (1.0 / total))
        mixed_ref[:, at] = jnp.transpose(jnp.concatenate(outs, axis=0)).astype(BF16)
    smid_ref[...] += dot_nn(mixed_ref[...], wo_ref[...])

    @pl.when(j == GROUPS - 1)
    def _():
        s = sin_ref[...]
        attend_out = smid_ref[...] - s
        valid = (bias[:, :1].astype(F32) == 0.0).astype(F32)
        stat_ref[0:1] = column_sum(s * s * valid)
        stat_ref[1:2] = column_sum(attend_out * attend_out * valid)
        stat_ref[2:8] = jnp.zeros((6, D), F32)


def by_column(rows, cols, first=0):
    return pl.BlockSpec((rows, cols), lambda j: (0, first + j))


def by_row(rows, cols):
    return pl.BlockSpec((rows, cols), lambda j: (j, 0))


def attend(place, own, mine, other, across, across_other, bias, par, wqkv, wo, deps=()):
    tokens = bias.shape[0]
    half = tokens // 2
    return call(
        attend_kernel,
        (place, own, mine, other, across, across_other, bias, par, wqkv, wqkv, wqkv, wo),
        [scalars()] + [fixed((half, D))] * 5 + [fixed((tokens, LANES)), fixed(par.shape)]
        + [by_column(D, WIDTH, first) for first in (0, GROUPS, 2 * GROUPS)]
        + [by_row(WIDTH, D)],
        [shaped((tokens, D), F32)]
        + [shaped((tokens, D), BF16)] * 5
        + [shaped((tokens, D), F32), shaped((PAIRS, 8, tokens), F32), shaped((8, D), F32)],
        out_specs=[fixed((tokens, D)), fixed((tokens, D))]
        + [by_column(tokens, WIDTH)] * 4
        + [fixed((tokens, D)), pl.BlockSpec((PAIRS // GROUPS, 8, tokens), lambda j: (j, 0, 0)), fixed((8, D))],
        grid=(GROUPS,),
        vmem=VMEM_MIB,
        name="attend",
        us=14.0,
        deps=deps,
    )


def stages_of(n):
    return [[b] for b in range(n.bit_length() - 1)]


def bits_at(x, bits):
    place = 0
    for b in bits:
        place = place * 2 + ((x >> b) & 1)
    return place


def peer_of(part, bits):
    return sum(1 << b for j, b in enumerate(reversed(bits)) if (part >> j) & 1)


def store_blocks(g_ref, me, refs, stages, rows, cols, at):
    order = sum(stages, [])
    steps = len(order)
    for part, ref in enumerate(refs):
        for place in range(ref.shape[0]):
            value = part * ref.shape[0] + place
            apart = sum(((value >> (steps - 1 - i)) & 1) << b for i, b in enumerate(order))
            ref[place, :, at : at + cols] = g_ref[me ^ apart, rows, :cols].astype(BF16)


def put_blocks(g_ref, value, n):
    rows = value.shape[0] // n
    for d in range(n):
        g_ref[d, :rows, : value.shape[1]] = value[d * rows : (d + 1) * rows]


def share_shapes(n, stages, rows, cols):
    parts = 1 << len(stages[0])
    return [shaped((n // parts, rows, cols), BF16) for _ in range(parts)]


SUMS = 32


def put_sums(v, refs):
    both = split_two(v, 1)
    count = refs[0].shape[0]
    size = both.shape[1] // count
    for ref in refs:
        for i in range(count):
            ref[i, :, ref.shape[2] - size :] = both[:, i * size : (i + 1) * size]


def get_sums(values):
    both = jnp.concatenate([values[i] for i in range(values.shape[0])], axis=1).astype(F32)
    half = both.shape[1] // 2
    return both[:, :half] + both[:, half:]


def sum_columns(rows, count):
    return 2 * SUMS * D // rows // count


def clear_spare(ref, rows):
    if ref.shape[1] > rows:
        ref[...] = jnp.zeros_like(ref)


def attend_back_kernel(
    place_ref, gmid_ref, wo_ref, q_ref, k_ref, v_ref, lse_ref, bias_ref, n1_ref, mixed_ref, sin_ref, par_ref,
    wq_ref, wk_ref, wv_ref, vec_h, vec_f, stat_a, stat_b, hot_ref,
    low_ref, *rest, n, stages,
):
    shares, (gtri, alow, quarter, flat, grad, gn, vec) = rest[:-7], rest[-7:]
    j = pl.program_id(0)
    e, me = place_ref[0], place_ref[1]
    tokens = gmid_ref.shape[0]

    @pl.when(j == 0)
    def _():
        alow[...] = gmid_ref[...].astype(BF16)

    gmix = dot_nt(alow[...], wo_ref[...]).astype(BF16)
    side_of = lane_side((tokens, LANES))
    one = (lax.broadcasted_iota(jnp.int32, (tokens, LANES), 1) == 0).astype(BF16)
    bias = bias_ref[...]
    scale = HEAD_DIM ** -0.5
    for pair in range(WIDTH // LANES):
        at = slice(pair * LANES, (pair + 1) * LANES)
        q, k, v, do = q_ref[:, at], k_ref[:, at], v_ref[:, at], gmix[:, at]
        keys = jnp.concatenate([k, bias], axis=1)
        kt = jnp.transpose(k)
        dq, dk, dv = [], 0.0, 0.0
        for a in range(2):
            qm = jnp.where(side_of == a, q, BF16(0))
            dom = jnp.where(side_of == a, do, BF16(0))
            s = dot_nt(keys, jnp.concatenate([qm * BF16(scale), one], axis=1))
            p = jnp.exp(s - lse_ref[pair, a : a + 1, :])
            dv = dv + dot_nn(p.astype(BF16), dom)
            dp = dot_nt(v, dom)
            delta = jnp.sum(p * dp, axis=0, keepdims=True)
            ds = (p * (dp - delta) * scale).astype(BF16)
            dk = dk + dot_nn(ds, qm)
            dq.append(dot_nn(kt[a * HEAD_DIM : (a + 1) * HEAD_DIM], ds))
        here = pl.ds(pl.multiple_of(j * WIDTH + pair * LANES, LANES), LANES)
        gtri[0, :, here] = jnp.transpose(jnp.concatenate(dq, axis=0)).astype(BF16)
        gtri[1, :, here] = dk.astype(BF16)
        gtri[2, :, here] = dv.astype(BF16)
    here = pl.ds(pl.multiple_of(j * WIDTH, WIDTH), WIDTH)
    part = (
        dot_nt(gtri[0, :, here], wq_ref[...])
        + dot_nt(gtri[1, :, here], wk_ref[...])
        + dot_nt(gtri[2, :, here], wv_ref[...])
    )

    @pl.when(j == 0)
    def _():
        gn[...] = part

    @pl.when(j > 0)
    def _():
        gn[...] += part

    @pl.when(j == GROUPS - 1)
    def _():
        wide, thin = 3 * D // 4, D // 4
        for mine in range(4):

            @pl.when(e == mine)
            def _():
                at = 0
                for b in range(3):
                    first, last = max(mine * wide, b * D), min((mine + 1) * wide, (b + 1) * D)
                    if first < last:
                        quarter[:, at : at + last - first] = gtri[b, :, first - b * D : last - b * D]
                        at += last - first
                quarter[:, wide:] = alow[:, mine * thin : (mine + 1) * thin]

        flat[:, :wide] = dot_tn(n1_ref[...], quarter[:, :wide])
        flat[:, wide:] = dot_tn(mixed_ref[...], quarter[:, wide:])
        clear_spare(grad, D // n)
        put_blocks(grad, flat[...], n)
        store_blocks(grad, me, shares, stages, slice(None), D, 0)
        g = gn[...]
        unit, inverse = unit_of(sin_ref[...])
        gin = gmid_ref[...] + norm_back(g, unit, inverse, par_ref[ROW_GAIN : ROW_GAIN + 1])
        low_ref[...] = gin.astype(BF16)
        lead = column_sum(g)
        vec[0:4] = vec_h[0:4]
        vec[4:10] = vec_f[0:6]
        vec[10:11] = column_sum(gin)
        vec[11:12] = lead
        vec[12:13] = column_sum(g * unit)
        vec[13:14] = column_sum(gmid_ref[...])
        vec[14:16] = stat_a[0:2]
        vec[16:19] = stat_b[0:3]
        vec[19:24] = jnp.zeros((5, D), F32)
        vec[24:32] = hot_ref[:, :1] * lead
        packed = []
        rows = shares[0].shape[1]
        cols = SUMS * D // rows
        for i in range(SUMS):
            packed += [vec[i : i + 1, at : at + min(cols, D)] for at in range(0, D, min(cols, D))]
        group = max(cols // D, 1)
        packed = [
            packed[i] if group == 1 else jnp.concatenate(packed[i : i + group], axis=1)
            for i in range(0, len(packed), group)
        ]
        put_sums(jnp.concatenate(packed, axis=0), shares)


def padded_rows(rows):
    return -(-rows // 16) * 16


def attend_back(place, gmid, wo, q, k, v, lse, bias, n1, mixed, sin, par, wqkv, vectors, n, stages, deps=()):
    tokens = gmid.shape[0]
    rows = padded_rows(D // n)
    outs = [shaped((tokens, D), BF16)] + share_shapes(n, stages, rows, D + sum_columns(rows, n // 2))
    return call(
        functools.partial(attend_back_kernel, n=n, stages=stages),
        (place, gmid, wo, q, k, v, lse, bias, n1, mixed, sin, par, wqkv, wqkv, wqkv, *vectors),
        [scalars(), fixed((tokens, D)), by_row(WIDTH, D)]
        + [by_column(tokens, WIDTH)] * 3
        + [pl.BlockSpec((PAIRS // GROUPS, 8, tokens), lambda j: (j, 0, 0)), fixed((tokens, LANES))]
        + [fixed((tokens, D))] * 3
        + [fixed(par.shape)]
        + [by_column(D, WIDTH, first) for first in (0, GROUPS, 2 * GROUPS)]
        + [fixed(v.shape) for v in vectors],
        outs,
        out_specs=[fixed(v.shape) for v in outs],
        grid=(GROUPS,),
        scratch=[
            VMEM((3, tokens, D), BF16),
            VMEM((tokens, D), BF16),
            VMEM((tokens, D), BF16),
            VMEM((D, D), F32),
            VMEM((n, rows, D), F32),
            VMEM((tokens, D), F32),
            VMEM((SUMS, D), F32),
        ],
        vmem=room(n) + 6,
        name="attend_back",
        us=60.0,
        deps=deps,
    )


STEPS = FF // D


def feed_kernel(
    smid_ref, bias_ref, par_ref, w1_ref, w2_ref, wh_ref, ho_ref,
    n2_ref, act_ref, slope_ref, sout_ref, n3_ref, blend_ref, stat_ref, feed,
):
    j = pl.program_id(0)

    @pl.when(j == 0)
    def _():
        unit, _ = unit_of(smid_ref[...])
        n2_ref[...] = (
            unit * par_ref[ROW_GAIN + 1 : ROW_GAIN + 2] + par_ref[ROW_SHIFT + 1 : ROW_SHIFT + 2]
        ).astype(BF16)
        feed[...] = jnp.broadcast_to(par_ref[ROW_CONTRACT : ROW_CONTRACT + 1], feed.shape)

    row = par_ref[ROW_EXPAND : ROW_EXPAND + 1]
    for i in range(1, STEPS):
        row = jnp.where(j == i, par_ref[ROW_EXPAND + i : ROW_EXPAND + i + 1], row)
    h = dot_nn(n2_ref[...], w1_ref[...]) + row
    sq = h * h
    t = jnp.tanh(h * (GELU_A + (GELU_A * GELU_B) * sq))
    side = 0.5 + 0.5 * t
    act_ref[...] = (h * side).astype(BF16)
    slope_ref[...] = (
        side + (h * (0.5 - 0.5 * t * t)) * (GELU_A + (3.0 * GELU_A * GELU_B) * sq)
    ).astype(BF16)
    feed[...] += dot_nn(act_ref[...], w2_ref[...])

    @pl.when(j == STEPS - 1)
    def _():
        feed_out = feed[...]
        sout = smid_ref[...] + feed_out
        sout_ref[...] = sout
        unit, _ = unit_of(sout)
        n3_ref[...] = (
            unit * par_ref[ROW_GAIN + 2 : ROW_GAIN + 3] + par_ref[ROW_SHIFT + 2 : ROW_SHIFT + 3]
        ).astype(BF16)
        vals = dot_nt(n3_ref[...], wh_ref[...]) + ho_ref[0:1]
        l = [vals[:, q * LANES : (q + 1) * LANES] for q in range(MODEL_TALLY)]
        top = jnp.maximum(jnp.maximum(l[0], l[1]), l[2])
        p = [jnp.exp(v - top) for v in l]
        total = p[0] + p[1] + p[2]
        for q in range(MODEL_TALLY):
            blend_ref[q] = p[q] / total
        blend_ref[MODEL_TALLY] = vals[:, MODEL_TALLY * LANES :]
        valid = (bias_ref[:, :1].astype(F32) == 0.0).astype(F32)
        stat_ref[0:1] = column_sum(feed_out * feed_out * valid)
        stat_ref[1:2] = column_sum(sout * sout * valid)
        stat_ref[2:3] = jnp.broadcast_to(column_sum(valid), (1, D)) * (1.0 / D)
        stat_ref[3:8] = jnp.zeros((5, D), F32)


def feed(smid, bias, par, w1, w2, wh, ho, deps=()):
    tokens = smid.shape[0]
    outs = [
        shaped((tokens, D), BF16),
        shaped((tokens, FF), BF16),
        shaped((tokens, FF), BF16),
        shaped((tokens, D), F32),
        shaped((tokens, D), BF16),
        shaped((4, tokens, LANES), F32),
        shaped((8, D), F32),
    ]
    out_specs = [fixed(v.shape) for v in outs]
    out_specs[1] = out_specs[2] = by_column(tokens, D)
    return call(
        feed_kernel,
        (smid, bias, par, w1, w2, wh, ho),
        [fixed((tokens, D)), fixed(bias.shape), fixed(par.shape), by_column(D, D), by_row(D, D)]
        + [fixed(wh.shape), fixed(ho.shape)],
        outs,
        out_specs=out_specs,
        grid=(STEPS,),
        scratch=[VMEM((tokens, D), F32)],
        vmem=VMEM_MIB,
        name="feed",
        us=12.0,
        deps=deps,
    )


def head_back_kernel(
    place_ref, blend_ref, gw_ref, gs_ref, wh_ref, sout_ref, par_ref, act_ref,
    hlow_ref, gout_ref, vec_ref, *rest, n, stages,
):
    shares, (flow, quarter, cgrad, blocks) = rest[:-4], rest[-4:]
    e, me = place_ref[0], place_ref[1]

    def by_token(v):
        tall = jnp.concatenate([v, jnp.zeros((LANES - HEAD_ROWS, v.shape[1]), F32)], axis=0)
        return jnp.transpose(tall)

    weights = [by_token(gw_ref[q]) for q in range(MODEL_TALLY)]
    inner = 0.0
    for q in range(MODEL_TALLY):
        inner = inner + blend_ref[q] * weights[q]
    vec_ref[...] = jnp.zeros_like(vec_ref)
    for q in range(MODEL_TALLY + 1):
        cols = slice(q * LANES, (q + 1) * LANES)
        g = by_token(gs_ref[...]) if q == MODEL_TALLY else blend_ref[q] * (weights[q] - inner)
        vec_ref[0:1, cols] = column_sum(g)
        hlow_ref[:, cols] = g.astype(BF16)
    gn3 = dot_nn(hlow_ref[...], wh_ref[...])
    unit, inverse = unit_of(sout_ref[...])
    g = norm_back(gn3, unit, inverse, par_ref[ROW_GAIN + 2 : ROW_GAIN + 3])
    gout_ref[...] = g
    flow[...] = g.astype(BF16)
    vec_ref[1:2] = column_sum(gn3 * unit)
    vec_ref[2:3] = column_sum(gn3)
    vec_ref[3:4] = column_sum(g)
    thin = D // 4
    for here in range(4):

        @pl.when(e == here)
        def _():
            quarter[...] = flow[:, here * thin : (here + 1) * thin]

    size, rows = FF // n, D // n
    clear_spare(blocks, rows)
    cgrad[...] = dot_tn(quarter[...], act_ref[...])
    for d in range(n):
        for i in range(n // 4):
            part = cgrad[i * rows : (i + 1) * rows, d * size : (d + 1) * size]
            blocks[d, :rows, i * size : (i + 1) * size] = part
    store_blocks(blocks, me, shares, stages, slice(None), D, 0)


def head_back(place, blend, gw, gs, wh, sout, par, act, n, stages, deps=()):
    tokens = sout.shape[0]
    return call(
        functools.partial(head_back_kernel, n=n, stages=stages),
        (place, blend, gw, gs, wh, sout, par, act),
        [scalars()] + [whole()] * 7,
        [shaped((tokens, 4 * LANES), BF16), shaped((tokens, D), F32), shaped((8, D), F32)]
        + share_shapes(n, stages, padded_rows(D // n), D),
        scratch=[
            VMEM((tokens, D), BF16),
            VMEM((tokens, D // 4), BF16),
            VMEM((D // 4, FF), F32),
            VMEM((n, padded_rows(D // n), D), F32),
        ],
        vmem=room(n),
        name="head_back",
        us=7,
        deps=deps,
    )


def feed_back_kernel(
    place_ref, hlow_ref, gout_ref, n3_ref, par_ref, slope_ref, n2_ref, smid_ref, w1_ref, w2_ref,
    gmid_ref, vec_ref, *rest, n, stages,
):
    shares, (flow, hid, mine, gn2, grad) = rest[:-5], rest[-5:]
    j = pl.program_id(0)
    e, me = place_ref[0], place_ref[1]

    @pl.when(j == 0)
    def _():
        flow[...] = gout_ref[...].astype(BF16)
        vec_ref[...] = jnp.zeros_like(vec_ref)
        gn2[...] = jnp.zeros_like(gn2)

    h = dot_nt(flow[...], w2_ref[...]) * slope_ref[...].astype(F32)
    sums = column_sum(h)
    for i in range(STEPS):

        @pl.when(j == i)
        def _():
            vec_ref[i : i + 1] = sums

    hid[...] = h.astype(BF16)

    @pl.when(j == e)
    def _():
        mine[...] = hid[...]

    gn2[...] += dot_nt(hid[...], w1_ref[...])

    @pl.when(j == STEPS - 1)
    def _():
        clear_spare(grad, D // n)
        put_blocks(grad, dot_tn(n2_ref[...], mine[...]), n)
        store_blocks(grad, me, shares, stages, slice(None), D, 0)
        put_blocks(grad, dot_tn(n3_ref[...], hlow_ref[:, pl.ds(pl.multiple_of(e * LANES, LANES), LANES)]), n)
        store_blocks(grad, me, shares, stages, slice(None), LANES, D)
        unit, inverse = unit_of(smid_ref[...])
        y = gn2[...]
        gmid_ref[...] = gout_ref[...] + norm_back(y, unit, inverse, par_ref[ROW_GAIN + 1 : ROW_GAIN + 2])
        vec_ref[4:5] = column_sum(y * unit)
        vec_ref[5:6] = column_sum(y)


def feed_back(place, hlow, gout, n3, par, slope, n2, smid, w1, w2, n, stages, deps=()):
    tokens = smid.shape[0]
    rows = padded_rows(D // n)
    outs = [shaped((tokens, D), F32), shaped((8, D), F32)] + share_shapes(n, stages, rows, D + LANES)
    return call(
        functools.partial(feed_back_kernel, n=n, stages=stages),
        (place, hlow, gout, n3, par, slope, n2, smid, w1, w2),
        [scalars()]
        + [fixed(v.shape) for v in (hlow, gout, n3, par)]
        + [by_column(tokens, D), fixed(n2.shape), fixed(smid.shape), by_column(D, D), by_row(D, D)],
        outs,
        out_specs=[fixed(v.shape) for v in outs],
        grid=(STEPS,),
        scratch=[
            VMEM((tokens, D), BF16),
            VMEM((tokens, D), BF16),
            VMEM((tokens, D), BF16),
            VMEM((tokens, D), F32),
            VMEM((n, rows, D), F32),
        ],
        vmem=room(n),
        name="feed_back",
        us=13.0,
        deps=deps,
    )


def fold_kernel(*refs, counts, parts, axis):
    outs = refs[sum(counts) :]
    ins, at = 0, 0
    for g, count in enumerate(counts):
        total = refs[ins][...].astype(F32)
        for i in range(1, count):
            total = total + refs[ins + i][...].astype(F32)
        ins += count
        size = total.shape[0] // parts
        for p in range(parts):
            piece = total[p * size : (p + 1) * size].astype(outs[p].dtype)
            if axis is None:
                outs[g * parts + p][...] = piece
            elif axis == 1:
                outs[p][:, at : at + piece.shape[1]] = piece
            else:
                outs[p][:, :, at : at + piece.shape[2]] = piece
        if axis is not None:
            at += total.shape[axis]


def fold(groups, parts, axis=None, deps=()):
    shapes = [g[0].shape for g in groups]
    dtype = groups[0][0].dtype
    size = shapes[0][0] // parts
    if axis is None:
        outs = [shaped((size,) + v[1:], dtype) for v in shapes for _ in range(parts)]
    else:
        full = list(shapes[0])
        full[0], full[axis] = size, sum(v[axis] for v in shapes)
        outs = [shaped(tuple(full), dtype)] * parts
    inputs = [v for g in groups for v in g]
    return call(
        functools.partial(fold_kernel, counts=[len(g) for g in groups], parts=parts, axis=axis),
        inputs,
        [whole()] * len(inputs),
        outs,
        name="fold",
        us=1.3,
        deps=deps,
    )


def fold_sums_kernel(*refs, first, parts):
    sums = refs[0:2]
    before = refs[2:4] if first else ()
    outs = refs[2 + len(before) :]
    count, rows, cols = sums[0].shape
    size = sum_columns(rows, count)
    vec = get_sums(sums[0][:, :, cols - size :]) + get_sums(sums[1][:, :, cols - size :])
    at = 0
    for pair in (before, sums):
        if pair:
            total = pair[0][...].astype(F32) + pair[1][...].astype(F32)
            wide = total.shape[2] - (size if pair is sums else 0)
            for p in range(parts):
                half = total[p * (count // parts) : (p + 1) * (count // parts), :, :wide]
                outs[p][:, :, at : at + wide] = half.astype(BF16)
            at += wide
    if parts == 1:
        outs[1][...] = vec
    else:
        put_sums(vec, outs[:parts])


def fold_sums(keep, got, parts, first=None, deps=()):
    count, rows, cols = keep.shape
    wide = cols - sum_columns(rows, count) + (first[0].shape[2] if first else 0)
    if parts == 1:
        outs = [shaped((1, rows, wide), BF16), shaped((rows, SUMS * D // rows), F32)]
    else:
        outs = [shaped((count // parts, rows, wide + sum_columns(rows, count // parts)), BF16)] * parts
    inputs = [keep, got] + (list(first) if first else [])
    return call(
        functools.partial(fold_sums_kernel, first=bool(first), parts=parts),
        inputs,
        [whole()] * len(inputs),
        outs,
        name="fold_sums",
        us=1.3,
        deps=deps,
    )


def assemble_kernel(place_ref, *refs, n):
    parts = refs[0:4]
    contract, expand, head, triple, result = refs[4:]
    e = place_ref[0]
    rows, size, thin, wide = D // n, FF // n, D // 4, 3 * D // 4
    last = 2 * D + LANES
    for here in range(4):

        @pl.when(e == here)
        def _():
            for i in range(4):
                part = parts[here ^ i]
                for j in range(n // 4):
                    block = jnp.transpose(part[0, :, j * size : (j + 1) * size].astype(F32))
                    contract[:, i * thin + j * rows : i * thin + (j + 1) * rows] = block[:, :rows]
                expand[:, i * D : (i + 1) * D] = part[0, :rows, D : 2 * D].astype(F32)
                head[:, i * CHANNELS : (i + 1) * CHANNELS] = part[0, :rows, 2 * D : 2 * D + CHANNELS].astype(F32)
                triple[:, i * wide : (i + 1) * wide] = part[0, :rows, last : last + wide].astype(F32)
                result[:, i * thin : (i + 1) * thin] = part[0, :rows, last + wide :].astype(F32)


def assemble(place, parts, n, deps=()):
    rows = D // n
    return call(
        functools.partial(assemble_kernel, n=n),
        (place, *parts),
        [scalars()] + [whole()] * 4,
        [
            shaped((FF // n, D), F32),
            shaped((rows, FF), F32),
            shaped((rows, 4 * CHANNELS), F32),
            shaped((rows, 3 * D), F32),
            shaped((rows, D), F32),
        ],
        name="assemble",
        us=2.5,
        deps=deps,
    )


def assemble_last_kernel(place_ref, p0, p1, p2, p3, lift, *, step, width):
    parts = (p0, p1, p2, p3)
    e = place_ref[0]
    for here in range(4):

        @pl.when(e == here)
        def _():
            for i in range(4):
                take = step if i < 3 else width
                lift[i * step : i * step + take] = parts[here ^ i][0, :take].astype(F32)


def assemble_last(place, parts, step, width, deps=()):
    return call(
        functools.partial(assemble_last_kernel, step=step, width=width),
        (place, *parts),
        [scalars()] + [whole()] * 4,
        shaped((3 * step + width, D), F32),
        name="assemble_last",
        us=2,
        deps=deps,
    )


THIRD = CHANNELS // 3


def channel_sums(pred_ref, adj_ref, first, channels, at, gw_ref, gs_ref):
    for i in range(channels):
        here = slice((first + i) * PIXELS, (first + i + 1) * PIXELS)
        adj = adj_ref[i * PIXELS : (i + 1) * PIXELS].astype(F32)
        gw_ref[first + i : first + i + 1, at] = column_sum(adj * pred_ref[here, at].astype(F32))
        gs_ref[first + i : first + i + 1, at] = column_sum(adj)


def weigh_near_kernel(place_ref, pred_ref, a0, a1, gw_ref, gs_ref):
    e = place_ref[0]
    rows = a0.shape[1]
    gw_ref[CHANNELS:] = jnp.zeros_like(gw_ref[CHANNELS:])
    gs_ref[CHANNELS:] = jnp.zeros_like(gs_ref[CHANNELS:])
    for k, a in enumerate((a0, a1)):
        at = pl.ds(pl.multiple_of((e ^ k) * rows, rows), rows)
        channel_sums(pred_ref, a, 0, CHANNELS, at, gw_ref, gs_ref)


def weigh_near(place, pred, adjoints, deps=()):
    tokens = pred.shape[1]
    return call(
        weigh_near_kernel,
        (place, pred, *adjoints),
        [scalars()] + [whole()] * 3,
        [shaped((HEAD_ROWS, tokens), F32)] * 2,
        name="weigh_near",
        us=3.6,
        deps=deps,
    )


def weigh_far_kernel(place_ref, pred_hbm, a2, a3, gw_in, gs_in, gw_ref, gs_ref, pred, sem):
    e = place_ref[0]
    rows = a2.shape[1]
    at = pl.ds(pl.multiple_of((e // 2) * 2 * rows, 2 * rows), 2 * rows)
    pair = pl.ds(pl.multiple_of((1 - e // 2) * 2 * rows, 2 * rows), 2 * rows)
    load = pltpu.make_async_copy(pred_hbm.at[:, pair], pred, sem)
    load.start()
    gw_ref[:, at] = gw_in[:, at]
    gs_ref[:, at] = gs_in[:, at]
    gw_ref[CHANNELS:, pair] = jnp.zeros((HEAD_ROWS - CHANNELS, 2 * rows), F32)
    gs_ref[CHANNELS:, pair] = jnp.zeros((HEAD_ROWS - CHANNELS, 2 * rows), F32)
    load.wait()
    for k, adj_ref in ((2, a2), (3, a3)):
        token = e ^ k
        own = pl.ds(pl.multiple_of(token * rows, rows), rows)
        inner = pl.ds(pl.multiple_of((token & 1) * rows, rows), rows)
        for i in range(CHANNELS):
            here = slice(i * PIXELS, (i + 1) * PIXELS)
            adj = adj_ref[here].astype(F32)
            gw_ref[i : i + 1, own] = column_sum(adj * pred[here, inner].astype(F32))
            gs_ref[i : i + 1, own] = column_sum(adj)


def weigh_far(place, pred, adjoints, gw, gs, deps=()):
    tokens = pred.shape[1]
    return call(
        weigh_far_kernel,
        (place, pred, *adjoints, gw, gs),
        [scalars(), in_hbm()] + [whole()] * 4,
        [shaped((HEAD_ROWS, tokens), F32)] * 2,
        scratch=[VMEM((TILE_ENTRIES, tokens // 2), BF16), pltpu.SemaphoreType.DMA],
        vmem=VMEM_MIB,
        name="weigh_far",
        us=2,
        deps=deps,
    )


def split_two(v, axis=0):
    hi = v.astype(BF16)
    return jnp.concatenate([hi, (v - hi.astype(F32)).astype(BF16)], axis=axis)


def by_rows(refs):
    pieces = [(0, refs[0], 0), (1, refs[1], 0)]
    for k in (2, 3):
        first = 0
        for ref in refs[2 + 3 * (k - 2) : 5 + 3 * (k - 2)]:
            pieces.append((k, ref, first))
            first += ref.shape[0]
    return pieces


def blend_kernel(place_ref, blend_ref, *rest):
    columns, spread_ref, outs, acc = rest[:8], rest[8], rest[9:13], rest[13]
    e = place_ref[0]
    rows = outs[0].shape[1]
    acc[...] = dot_nn(
        jnp.concatenate([spread_ref[...]] * 2, axis=1), split_two(jnp.transpose(blend_ref[MODEL_TALLY]))
    )
    for k, c, first in by_rows(columns):
        q = e ^ k

        @pl.when(q < MODEL_TALLY)
        def _():
            at = slice(first, first + c.shape[0])
            spread = jnp.concatenate([spread_ref[at]] * 2, axis=1)
            acc[at] += dot_nn(spread, split_two(jnp.transpose(blend_ref[q]))) * c[...].astype(F32)

    for k, o in enumerate(outs):
        at = pl.multiple_of((e ^ k) * rows, rows)
        o[...] = acc[:, pl.ds(at, rows)].astype(BF16)


def blend_columns(place, blend, columns, spread, deps=()):
    cols, tokens = columns[0].shape
    rows = tokens // 4
    return call(
        blend_kernel,
        (place, blend, *columns, spread),
        [scalars()] + [whole()] * 10,
        [shaped((cols, rows), BF16)] * 4,
        scratch=[VMEM((cols, tokens), F32)],
        name="blend",
        us=5,
        deps=deps,
    )


def lift_grad_kernel(place_ref, low_ref, masks_ref, *rest, n, stages):
    columns, shares, grad = rest[:8], rest[8:-1], rest[-1]
    e, me = place_ref[0], place_ref[1]
    masks = jnp.transpose(masks_ref[...])
    low = low_ref[...].astype(F32)
    rows = grad.shape[1]
    grad[...] = jnp.zeros_like(grad)
    for k, c, first in by_rows(columns):

        @pl.when((e ^ k) < MODEL_TALLY)
        def _():
            part = dot_nn(c[...], (low * masks[:, k : k + 1]).astype(BF16))
            for i in range(c.shape[0] // rows):
                grad[first // rows + i] += part[i * rows : (i + 1) * rows]

    store_blocks(grad, me, shares, stages, slice(None), D, 0)


def lift_grad(place, low, masks, columns, n, stages, deps=()):
    cols, tokens = columns[0].shape
    rows = cols // n
    return call(
        functools.partial(lift_grad_kernel, n=n, stages=stages),
        (place, low, masks, *columns),
        [scalars()] + [whole()] * 10,
        share_shapes(n, stages, rows, D),
        scratch=[VMEM((n, rows, D), F32)],
        vmem=room(n),
        name="lift_grad",
        us=30,
        deps=deps,
    )


def slope_kernel(place_ref, low_ref, masks_ref, blend_ref, lift_ref, a0, a1, a2, a3, *rest, which):
    out_ref, acc = rest[-2], rest[-1]
    e = place_ref[0]
    rows = a0.shape[1]
    masks = jnp.transpose(masks_ref[...])
    low = (low_ref[...].astype(F32) * masks[:, :1]).astype(BF16)
    active = jnp.where(e < MODEL_TALLY, 1.0, 0.0)
    weights = jnp.transpose(blend_ref[jnp.minimum(e, MODEL_TALLY - 1)] * active)
    acc[...] = dot_nt(lift_ref[...], low)
    first = which * THIRD
    for k, a in enumerate((a0, a1, a2, a3)):
        for b in range(4):

            @pl.when((e ^ k) == b)
            def _():
                at = slice(b * rows, (b + 1) * rows)
                for i in range(THIRD):
                    here = slice(i * PIXELS, (i + 1) * PIXELS)
                    weight = weights[first + i : first + i + 1, at]
                    out_ref[here, at] = (acc[here, at] + weight * a[here].astype(F32)).astype(BF16)


def slope(which, before, place, low, masks, blend, lift, adjoints, deps=()):
    tokens = low.shape[0]
    rows = adjoints[0].shape[1]
    size = THIRD * PIXELS
    third = lambda cols: pl.BlockSpec((size, cols), lambda j: (which, 0))
    inputs = [place, low, masks, blend, lift, *adjoints]
    in_specs = [scalars(), fixed((tokens, D)), fixed(masks.shape), fixed(blend.shape), third(D)]
    in_specs += [third(rows)] * 4
    aliases = {}
    if before is not None:
        aliases = {len(inputs): 0}
        inputs.append(before)
        in_specs.append(in_hbm())
    return call(
        functools.partial(slope_kernel, which=which),
        inputs,
        in_specs,
        shaped((TILE_ENTRIES, tokens), BF16),
        grid=(1,),
        out_specs=third(tokens),
        scratch=[VMEM((size, tokens), F32)],
        aliases=aliases,
        name="slope",
        us=4.3,
        deps=deps,
    )


def expert_swap(v, k):
    size = lax.axis_size("expert")
    return lax.ppermute(v, "expert", [(i, i ^ k) for i in range(size)])


def frame_swap(v, k):
    size = lax.axis_size("dp")
    return lax.ppermute(v, "dp", [(i, i ^ k) for i in range(size)])


def gather_four(v):
    across = expert_swap(v, 2)
    return [v, expert_swap(v, 1), across, expert_swap(across, 1)]


def in_order(parts, e):
    odd = (e & 1) == 1
    high = (e & 2) == 2
    a, b, c, d = parts
    a, b, c, d = (
        jnp.where(odd, b, a),
        jnp.where(odd, a, b),
        jnp.where(odd, d, c),
        jnp.where(odd, c, d),
    )
    return [jnp.where(high, c, a), jnp.where(high, d, b), jnp.where(high, a, c), jnp.where(high, b, d)]


def local(
    model_predictions,
    member_tile_presence,
    piece_usable_flags,
    horizon_positions,
    result_adjoint,
    tile_lift_matrix,
    tile_lift_offset,
    horizon_lookup,
    normalizer_scales,
    normalizer_offsets,
    query_key_value_matrix,
    attend_result_matrix,
    attend_offset_vector,
    expand_matrix,
    expand_offset,
    contract_matrix,
    contract_offset,
    mixing_head_matrix,
    mixing_head_offset,
):
    n = lax.axis_size("dp")
    e = lax.axis_index("expert")
    place = jnp.stack([e, lax.axis_index("dp")]).astype(jnp.int32)
    core = e & 1
    active = (e < MODEL_TALLY).astype(F32)
    pred = jnp.transpose(model_predictions[0])
    tokens = pred.shape[1]
    block = TILE_ENTRIES // n
    step = block // 4 // 8 * 8 if block % 8 == 0 else block // 4
    width = block - 3 * step
    padded = padded_rows(width)

    adjoint = jnp.transpose(result_adjoint)
    near = expert_swap(adjoint, 1)
    far = expert_swap(adjoint, 2)

    mask = member_tile_presence.astype(F32) * active
    own_part, other_part, _ = embed(place, mask, pred, tile_lift_matrix)

    info = jnp.concatenate([mask, piece_usable_flags.astype(F32)[None]], axis=1)
    infos = [info] + [expert_swap(info, k) for k in (1, 2, 3)]
    masks = jnp.concatenate([v[:, :tokens] for v in infos] + [jnp.zeros((4, tokens), F32)], axis=0)
    valid = jnp.concatenate([v[0, tokens:] for v in in_order(infos, e)])
    first = jnp.arange(LANES) == 0
    bias = jnp.where((valid[:, None] == 0) & first[None, :], MASKED_SCORE, 0.0).astype(BF16)

    lead_hot = (jnp.arange(horizon_lookup.shape[0]) == horizon_positions[0]).astype(F32)
    lead_vector = jnp.sum(lead_hot[:, None] * horizon_lookup.astype(F32), axis=0)
    par = jnp.concatenate(
        [
            tile_lift_offset[None].astype(F32),
            normalizer_scales.astype(F32),
            normalizer_offsets.astype(F32),
            attend_offset_vector[None].astype(F32),
            contract_offset[None].astype(F32),
            expand_offset.reshape(FF // D, D).astype(F32),
            lead_vector[None],
            jnp.zeros((PARAM_ROWS - ROW_HEAD, D), F32),
        ],
        axis=0,
    )
    over = (0, LANES - CHANNELS)
    head = jnp.pad(jnp.transpose(mixing_head_matrix).reshape(4, CHANNELS, D), ((0, 0), over, (0, 0)))
    head = head.reshape(4 * LANES, D)
    head_row = jnp.pad(mixing_head_offset.astype(F32).reshape(1, 4, CHANNELS), ((0, 0), (0, 0), over))
    head_row = head_row.reshape(1, 4 * LANES)
    at = jnp.arange(n * padded)
    channel = ((at // padded) * block + e * step + at % padded) // PIXELS
    spread = (channel[:, None] == jnp.arange(LANES)[None, :]).astype(BF16)

    pair, done = fold([[own_part, expert_swap(other_part, 1)]], 1)
    other = expert_swap(own_part, 1)
    across = expert_swap(pair, 2)
    across_other = expert_swap(across, 1)

    mine, grad_shift, done = weigh_near(place, pred, [adjoint, near], deps=[done, par, bias, head, head_row, spread, masks])
    *pieces, far, done = pack(place, pred, far, n, step, width, padded, deps=[done, across])
    far_near = expert_swap(far, 1)
    adjoints = [adjoint, near, far, far_near]
    sin, n1, queries, keys, values, mixed, smid, lse, stat_a, done = attend(
        place, pair, other_part, other, across, across_other, bias, par, query_key_value_matrix, attend_result_matrix, deps=[done]
    )
    columns = [pieces[0], expert_swap(pieces[1], 1)] + [expert_swap(v, 2 + i // 3) for i, v in enumerate(pieces[2:])]
    mine, grad_shift, done = weigh_far(
        place, pred, adjoints[2:], mine, grad_shift, deps=[done, columns[1], columns[2], columns[5]]
    )
    all_mine = [mine] + [expert_swap(mine, k) for k in (1, 2, 3)]
    n2, act, gelu_slope, sout, n3, blend, stat_b, done = feed(
        smid, bias, par, expand_matrix, contract_matrix, head, head_row, deps=[done]
    )
    grad_weights = jnp.stack(in_order(all_mine, e)[:MODEL_TALLY])

    stages = stages_of(n)
    last_bit = len(stages) - 1

    def onward(keep, got, bit, deps):
        keep, send, done = fold([[keep, got]], 2, deps=deps)
        return keep, frame_swap(send, 1 << bit), done

    hlow, gout, vec_h, ckeep, csend, done = head_back(
        place, blend, grad_weights, grad_shift, head, sout, par, act, n, stages, deps=[done]
    )
    cgot = frame_swap(csend, 1)
    gmid, vec_f, tkeep, tsend, done = feed_back(
        place, hlow, gout, n3, par, gelu_slope, n2, smid, expand_matrix, contract_matrix, n, stages,
        deps=[done, columns[3]],
    )
    tgot = frame_swap(tsend, 1)
    hot = jnp.broadcast_to(lead_hot[:, None], (lead_hot.shape[0], LANES))
    low, qkeep, qsend, done = attend_back(
        place, gmid, attend_result_matrix, queries, keys, values, lse, bias, n1, mixed, sin, par,
        query_key_value_matrix, [vec_h, vec_f, stat_a, stat_b, hot], n, stages, deps=[done, cgot, columns[6]],
    )
    qgot = frame_swap(qsend, 1)
    keep, send, done = fold([[ckeep, cgot], [tkeep, tgot]], 2, axis=2, deps=[done])
    got = frame_swap(send, 2)
    akeep, asend, done = lift_grad(place, low, masks, columns, n, stages, deps=[done])
    agot = frame_swap(asend, 1)
    slopes = [place, low, masks, blend, tile_lift_matrix, adjoints]
    *outgoing, done = blend_columns(place, blend, columns, spread, deps=[done])
    arrived = [outgoing[0]] + [expert_swap(outgoing[k], k) for k in (1, 2, 3)]
    part_slope, done = slope(0, None, *slopes, deps=[done])
    keep, got, done = onward(keep, got, 2, [done])
    qkeep, qsend, done = fold_sums(qkeep, qgot, 2, deps=[done])
    qgot = frame_swap(qsend, 2)
    part_slope, done = slope(1, part_slope, *slopes, deps=[done])
    combined, done = unpack(place, arrived, n, step, width, padded, deps=[done])
    combined_prediction = jnp.transpose(combined)
    qkeep, qsend, done = fold_sums(qkeep, qgot, 2, deps=[done])
    qgot = frame_swap(qsend, 4)
    akeep, agot, done = onward(akeep, agot, 1, [done])
    part_slope, done = slope(2, part_slope, *slopes, deps=[done])
    for bit in range(3, last_bit + 1):
        keep, got, done = onward(keep, got, bit, [done])
        qkeep, qsend, done = fold_sums(qkeep, qgot, 2, deps=[done])
        qgot = frame_swap(qsend, 1 << bit)
    rows_one, packed, done = fold_sums(qkeep, qgot, 1, first=[keep, got], deps=[done])
    rows_one = gather_four(rows_one)
    packed = packed.reshape(SUMS, D)
    for bit in range(2, last_bit + 1):
        akeep, agot, done = onward(akeep, agot, bit, [done])
    contract_slope, expand_slope, head_slope, triple_slope, result_slope, done = assemble(
        place, rows_one, n, deps=[done]
    )
    rows_two, done = fold([[akeep, agot]], 1, deps=[done])
    lift_slope, _ = assemble_last(place, gather_four(rows_two), step, width, deps=[done])
    predictions_slope = jnp.transpose(part_slope)[None]

    head_off = packed[0, : 4 * LANES].reshape(4, LANES)[:, :CHANNELS].reshape(4 * CHANNELS)
    total = jnp.sum(packed[14:19], axis=1)
    magnitudes = jnp.sqrt(total[:4] / (total[4] * D) + SQUARE_EPSILON)
    gains = jnp.stack([packed[12], packed[8], packed[1]])
    shifts = jnp.stack([packed[11], packed[9], packed[2]])
    return (
        combined_prediction,
        predictions_slope,
        magnitudes,
        lift_slope,
        packed[10],
        packed[24:32],
        gains,
        shifts,
        triple_slope,
        result_slope,
        packed[13],
        expand_slope,
        packed[4:8].reshape(FF),
        contract_slope,
        packed[3],
        head_slope,
        head_off,
    )


def solution(mesh):
    rows = P(("dp", "expert"), None)
    placed = (
        P("expert", "dp", None),
        P("expert", "dp"),
        P(("dp", "expert")),
        P("dp"),
        rows,
    ) + (P(),) * 14
    given = (
        rows,
        P("expert", "dp", None),
        P(),
        P("dp", None),
        P(),
        P(),
        P(),
        P(),
        P("dp", None),
        P("dp", None),
        P(),
        P("dp", None),
        P(),
        P("dp", None),
        P(),
        P("dp", None),
        P(),
    )
    return jax.shard_map(local, mesh=mesh, in_specs=placed, out_specs=given, check_vma=False)
```

```python
import functools

import jax
import jax.numpy as jnp
from jax import lax
from jax.experimental import pallas as pl
from jax.experimental.pallas import tpu as pltpu
from jax.sharding import PartitionSpec as P

D = 768
HEADS = 12
HEAD_DIM = 64
FF = 3072
MODEL_TALLY = 3
CHANNELS = 69
PIXELS = 64
TILE_ENTRIES = 4416
LANES = 128
PAIRS = HEADS // 2

NORM_EPSILON = 1e-05
SQUARE_EPSILON = 1e-06
MASKED_SCORE = -1e30
GELU_A = 0.7978845608028654
GELU_B = 0.044715
F32 = jnp.float32
BF16 = jnp.bfloat16

ROW_LIFT, ROW_GAIN, ROW_SHIFT, ROW_ATTEND, ROW_CONTRACT, ROW_EXPAND, ROW_LEAD, ROW_HEAD = 0, 1, 4, 7, 8, 9, 13, 14
PARAM_ROWS = 16
HEAD_ROWS = 72
VMEM_MIB = 20
VMEM_SMALL = 12
SCALE = 1e8

VMEM = pltpu.VMEM
SMEM = pltpu.SMEM


def whole():
    return pl.BlockSpec(memory_space=VMEM)


def scalars():
    return pl.BlockSpec(memory_space=SMEM)


def in_hbm():
    return pl.BlockSpec(memory_space=pl.ANY)


def shaped(shape, dtype):
    return jax.ShapeDtypeStruct(shape, dtype)


def dot_nn(a, b):
    return jnp.dot(a, b, preferred_element_type=F32)


def dot_tn(a, b):
    return lax.dot_general(a, b, (((0,), (0,)), ((), ())), preferred_element_type=F32)


def dot_nt(a, b):
    return lax.dot_general(a, b, (((1,), (1,)), ((), ())), preferred_element_type=F32)


def unit_of(values):
    center = values - jnp.mean(values, axis=-1, keepdims=True)
    inverse = lax.rsqrt(jnp.mean(center * center, axis=-1, keepdims=True) + NORM_EPSILON)
    return center * inverse, inverse


def norm_back(grad_out, unit, inverse, gain):
    scaled = grad_out * gain
    return inverse * (
        scaled
        - jnp.mean(scaled, axis=-1, keepdims=True)
        - unit * jnp.mean(scaled * unit, axis=-1, keepdims=True)
    )


def column_sum(v):
    return jnp.sum(v, axis=0, keepdims=True)


def room(n):
    return VMEM_MIB if (D // n) % 16 == 0 else VMEM_MIB + 24


def fixed(shape):
    return pl.BlockSpec(shape, lambda *_: (0,) * len(shape))


def taking(us):
    return pl.CostEstimate(flops=int(us * SCALE), bytes_accessed=1000, transcendentals=0)


def call(
    body, inputs, in_specs, outs, scratch=(), vmem=VMEM_MIB, grid=None, out_specs=None, name=None, deps=(), us=1.0,
    aliases=None,
):
    kwargs = {}
    if grid is not None:
        kwargs["grid"] = grid
    if aliases:
        kwargs["input_output_aliases"] = aliases
    outs = list(outs) if isinstance(outs, (list, tuple)) else [outs]
    if out_specs is None:
        out_specs = [whole() for _ in outs]
    out_specs = list(out_specs) if isinstance(out_specs, (list, tuple)) else [out_specs]
    count = len(inputs)

    def kernel(*refs):
        given = count + len(deps)
        body(*refs[:count], *refs[given : given + len(outs)], *refs[given + len(outs) + 1 :])
        token = refs[given + len(outs)]
        token[...] = jnp.zeros_like(token)

    return pl.pallas_call(
        kernel,
        out_shape=outs + [shaped((8, LANES), F32)],
        in_specs=list(in_specs) + [in_hbm() for _ in deps],
        out_specs=out_specs + [whole() if grid is None else fixed((8, LANES))],
        scratch_shapes=list(scratch),
        compiler_params=pltpu.CompilerParams(vmem_limit_bytes=vmem * 1024 * 1024),
        cost_estimate=taking(us),
        name=name,
        **kwargs,
    )(*inputs, *deps)


def embed_kernel(place_ref, mask_ref, pred_hbm, lift_hbm, own_ref, other_ref, pred, lift, acc, sems, *, cuts):
    copies = []
    for i, (a, b) in enumerate(cuts):
        one = pltpu.make_async_copy(pred_hbm.at[a:b], pred.at[a:b], sems.at[0, i])
        two = pltpu.make_async_copy(lift_hbm.at[a:b], lift.at[a:b], sems.at[1, i])
        one.start()
        two.start()
        copies.append((one, two))
    for i, (a, b) in enumerate(cuts):
        for copy in copies[i]:
            copy.wait()
        part = dot_tn(pred[a:b], lift[a:b])
        if i == 0:
            acc[...] = part
        elif i < len(cuts) - 1:
            acc[...] += part
        else:
            mask = jnp.transpose(jnp.broadcast_to(mask_ref[...], (8, mask_ref.shape[1])))[:, :1]
            acc[...] = (acc[...] + part) * mask
            half = own_ref.shape[0]
            core = place_ref[0] & 1
            own_ref[...] = acc[pl.ds(pl.multiple_of(core * half, half), half)].astype(BF16)
            other_ref[...] = acc[pl.ds(pl.multiple_of((1 - core) * half, half), half)].astype(BF16)


def embed(place, mask, pred, lift):
    tokens = pred.shape[1]
    cuts = [(0, 768), (768, 1536), (1536, 2560), (2560, 3584), (3584, TILE_ENTRIES)]
    return call(
        functools.partial(embed_kernel, cuts=cuts),
        (place, mask, pred, lift),
        [scalars(), whole(), in_hbm(), in_hbm()],
        [shaped((tokens // 2, D), BF16)] * 2,
        scratch=[
            VMEM((TILE_ENTRIES, tokens), BF16),
            VMEM((TILE_ENTRIES, D), BF16),
            VMEM((tokens, D), F32),
            pltpu.SemaphoreType.DMA((2, len(cuts))),
        ],
        vmem=60,
        name="embed",
        us=7.5,
    )


def cuts_of(n):
    return [0, n // 4, n // 4 + 3 * n // 8, n]


def pack_kernel(place_ref, pred_ref, far_ref, *outs, n, step, width, padded):
    outs[-1][...] = far_ref[...]
    e = place_ref[0]
    tokens = pred_ref.shape[1]
    block = TILE_ENTRIES // n
    cuts = cuts_of(n)
    for here in range(4):

        @pl.when(e == here)
        def _():
            for k in range(4):
                q = here ^ k
                for d in range(n):
                    out, first = outs[min(k, 2)], 0
                    if k >= 2:
                        piece = max(i for i in range(3) if cuts[i] <= d)
                        out, first = outs[2 + 3 * (k - 2) + piece], cuts[piece]
                    at = (d - first) * padded
                    start = d * block + q * step
                    out[at : at + width] = pred_ref[start : start + width]
                    if padded > width:
                        out[at + width : at + padded] = jnp.zeros((padded - width, tokens), BF16)


def pack(place, pred, far, n, step, width, padded, deps=()):
    tokens = pred.shape[1]
    cuts = cuts_of(n)
    thirds = [shaped(((cuts[i + 1] - cuts[i]) * padded, tokens), BF16) for i in range(3)]
    return call(
        functools.partial(pack_kernel, n=n, step=step, width=width, padded=padded),
        (place, pred, far),
        [scalars(), whole(), whole()],
        [shaped((n * padded, tokens), BF16)] * 2 + thirds * 2 + [shaped(far.shape, BF16)],
        name="pack",
        us=2,
        deps=deps,
    )


def unpack_kernel(place_ref, *refs, n, step, width, padded):
    parts, out = refs[:4], refs[4]
    e = place_ref[0]
    block = TILE_ENTRIES // n
    for here in range(4):

        @pl.when(e == here)
        def _():
            for q in range(4):
                take = step if q < 3 else width
                for d in range(n):
                    start = d * block + q * step
                    out[start : start + take] = parts[here ^ q][d * padded : d * padded + take]


def unpack(place, parts, n, step, width, padded, deps=()):
    rows = parts[0].shape[1]
    return call(
        functools.partial(unpack_kernel, n=n, step=step, width=width, padded=padded),
        (place, *parts),
        [scalars()] + [whole()] * 4,
        shaped((TILE_ENTRIES, rows), BF16),
        name="unpack",
        us=2,
        deps=deps,
    )


def lane_side(shape):
    return lax.broadcasted_iota(jnp.int32, shape, 1) // HEAD_DIM


GROUPS = 3
WIDTH = D // GROUPS


def attend_kernel(
    place_ref, own_ref, mine_ref, other_ref, across_ref, across_other_ref, bias_ref, par_ref,
    wq_ref, wk_ref, wv_ref, wo_ref,
    sin_ref, n1_ref, q_ref, k_ref, v_ref, mixed_ref, smid_ref, lse_ref, stat_ref,
):
    j = pl.program_id(0)
    core = place_ref[0] & 1
    tokens = bias_ref.shape[0]
    half = tokens // 2

    @pl.when(j == 0)
    def _():
        gain = par_ref[ROW_GAIN : ROW_GAIN + 1]
        shift = par_ref[ROW_SHIFT : ROW_SHIFT + 1] + par_ref[ROW_LEAD : ROW_LEAD + 1]
        offset = par_ref[ROW_LIFT : ROW_LIFT + 1]
        other = (mine_ref[...].astype(F32) + other_ref[...].astype(F32)).astype(BF16)
        for side, near, far in ((core, own_ref[...], across_ref), (1 - core, other, across_other_ref)):
            rows = pl.ds(pl.multiple_of(side * half, half), half)
            s = near.astype(F32) + far[...].astype(F32) + offset
            sin_ref[rows] = s
            smid_ref[rows] = s + par_ref[ROW_ATTEND : ROW_ATTEND + 1]
            unit, _ = unit_of(s)
            n1_ref[rows] = (unit * gain + shift).astype(BF16)

    n1 = n1_ref[...]
    q_ref[...] = dot_nn(n1, wq_ref[...]).astype(BF16)
    k_ref[...] = dot_nn(n1, wk_ref[...]).astype(BF16)
    v_ref[...] = dot_nn(n1, wv_ref[...]).astype(BF16)
    side_of = lane_side((tokens, LANES))
    one = (lax.broadcasted_iota(jnp.int32, (tokens, LANES), 1) == 0).astype(BF16)
    bias = bias_ref[...]
    for pair in range(WIDTH // LANES):
        at = slice(pair * LANES, (pair + 1) * LANES)
        q = q_ref[:, at] * BF16(HEAD_DIM ** -0.5)
        keys = jnp.concatenate([k_ref[:, at], bias], axis=1)
        vt = jnp.transpose(v_ref[:, at])
        outs = []
        for a in range(2):
            qa = jnp.concatenate([jnp.where(side_of == a, q, BF16(0)), one], axis=1)
            s = dot_nt(keys, qa)
            top = jnp.max(s, axis=0, keepdims=True)
            p = jnp.exp(s - top)
            total = jnp.sum(p, axis=0, keepdims=True)
            lse_ref[pair, a : a + 1, :] = top + jnp.log(total)
            o = dot_nn(vt[a * HEAD_DIM : (a + 1) * HEAD_DIM], p.astype(BF16))
            outs.append(o * (1.0 / total))
        mixed_ref[:, at] = jnp.transpose(jnp.concatenate(outs, axis=0)).astype(BF16)
    smid_ref[...] += dot_nn(mixed_ref[...], wo_ref[...])

    @pl.when(j == GROUPS - 1)
    def _():
        s = sin_ref[...]
        attend_out = smid_ref[...] - s
        valid = (bias[:, :1].astype(F32) == 0.0).astype(F32)
        stat_ref[0:1] = column_sum(s * s * valid)
        stat_ref[1:2] = column_sum(attend_out * attend_out * valid)
        stat_ref[2:8] = jnp.zeros((6, D), F32)


def by_column(rows, cols, first=0):
    return pl.BlockSpec((rows, cols), lambda j: (0, first + j))


def by_row(rows, cols):
    return pl.BlockSpec((rows, cols), lambda j: (j, 0))


def attend(place, own, mine, other, across, across_other, bias, par, wqkv, wo, deps=()):
    tokens = bias.shape[0]
    half = tokens // 2
    return call(
        attend_kernel,
        (place, own, mine, other, across, across_other, bias, par, wqkv, wqkv, wqkv, wo),
        [scalars()] + [fixed((half, D))] * 5 + [fixed((tokens, LANES)), fixed(par.shape)]
        + [by_column(D, WIDTH, first) for first in (0, GROUPS, 2 * GROUPS)]
        + [by_row(WIDTH, D)],
        [shaped((tokens, D), F32)]
        + [shaped((tokens, D), BF16)] * 5
        + [shaped((tokens, D), F32), shaped((PAIRS, 8, tokens), F32), shaped((8, D), F32)],
        out_specs=[fixed((tokens, D)), fixed((tokens, D))]
        + [by_column(tokens, WIDTH)] * 4
        + [fixed((tokens, D)), pl.BlockSpec((PAIRS // GROUPS, 8, tokens), lambda j: (j, 0, 0)), fixed((8, D))],
        grid=(GROUPS,),
        vmem=VMEM_MIB,
        name="attend",
        us=14.0,
        deps=deps,
    )


def stages_of(n):
    return [[b] for b in range(n.bit_length() - 1)]


def bits_at(x, bits):
    place = 0
    for b in bits:
        place = place * 2 + ((x >> b) & 1)
    return place


def peer_of(part, bits):
    return sum(1 << b for j, b in enumerate(reversed(bits)) if (part >> j) & 1)


def store_blocks(g_ref, me, refs, stages, rows, cols, at):
    order = sum(stages, [])
    steps = len(order)
    for part, ref in enumerate(refs):
        for place in range(ref.shape[0]):
            value = part * ref.shape[0] + place
            apart = sum(((value >> (steps - 1 - i)) & 1) << b for i, b in enumerate(order))
            ref[place, :, at : at + cols] = g_ref[me ^ apart, rows, :cols].astype(BF16)


def put_blocks(g_ref, value, n):
    rows = value.shape[0] // n
    for d in range(n):
        g_ref[d, :rows, : value.shape[1]] = value[d * rows : (d + 1) * rows]


def share_shapes(n, stages, rows, cols):
    parts = 1 << len(stages[0])
    return [shaped((n // parts, rows, cols), BF16) for _ in range(parts)]


SUMS = 32


def put_sums(v, refs):
    both = split_two(v, 1)
    count = refs[0].shape[0]
    size = both.shape[1] // count
    for ref in refs:
        for i in range(count):
            ref[i, :, ref.shape[2] - size :] = both[:, i * size : (i + 1) * size]


def get_sums(values):
    both = jnp.concatenate([values[i] for i in range(values.shape[0])], axis=1).astype(F32)
    half = both.shape[1] // 2
    return both[:, :half] + both[:, half:]


def sum_columns(rows, count):
    return 2 * SUMS * D // rows // count


def clear_spare(ref, rows):
    if ref.shape[1] > rows:
        ref[...] = jnp.zeros_like(ref)


def attend_back_kernel(
    place_ref, gmid_ref, wo_ref, q_ref, k_ref, v_ref, lse_ref, bias_ref, n1_ref, mixed_ref, sin_ref, par_ref,
    wq_ref, wk_ref, wv_ref, vec_h, vec_f, stat_a, stat_b, hot_ref,
    low_ref, *rest, n, stages,
):
    shares, (gtri, alow, quarter, flat, grad, gn, vec) = rest[:-7], rest[-7:]
    j = pl.program_id(0)
    e, me = place_ref[0], place_ref[1]
    tokens = gmid_ref.shape[0]

    @pl.when(j == 0)
    def _():
        alow[...] = gmid_ref[...].astype(BF16)

    gmix = dot_nt(alow[...], wo_ref[...]).astype(BF16)
    side_of = lane_side((tokens, LANES))
    one = (lax.broadcasted_iota(jnp.int32, (tokens, LANES), 1) == 0).astype(BF16)
    bias = bias_ref[...]
    scale = HEAD_DIM ** -0.5
    for pair in range(WIDTH // LANES):
        at = slice(pair * LANES, (pair + 1) * LANES)
        q, k, v, do = q_ref[:, at], k_ref[:, at], v_ref[:, at], gmix[:, at]
        keys = jnp.concatenate([k, bias], axis=1)
        kt = jnp.transpose(k)
        dq, dk, dv = [], 0.0, 0.0
        for a in range(2):
            qm = jnp.where(side_of == a, q, BF16(0))
            dom = jnp.where(side_of == a, do, BF16(0))
            s = dot_nt(keys, jnp.concatenate([qm * BF16(scale), one], axis=1))
            p = jnp.exp(s - lse_ref[pair, a : a + 1, :])
            dv = dv + dot_nn(p.astype(BF16), dom)
            dp = dot_nt(v, dom)
            delta = jnp.sum(p * dp, axis=0, keepdims=True)
            ds = (p * (dp - delta) * scale).astype(BF16)
            dk = dk + dot_nn(ds, qm)
            dq.append(dot_nn(kt[a * HEAD_DIM : (a + 1) * HEAD_DIM], ds))
        here = pl.ds(pl.multiple_of(j * WIDTH + pair * LANES, LANES), LANES)
        gtri[0, :, here] = jnp.transpose(jnp.concatenate(dq, axis=0)).astype(BF16)
        gtri[1, :, here] = dk.astype(BF16)
        gtri[2, :, here] = dv.astype(BF16)
    here = pl.ds(pl.multiple_of(j * WIDTH, WIDTH), WIDTH)
    part = (
        dot_nt(gtri[0, :, here], wq_ref[...])
        + dot_nt(gtri[1, :, here], wk_ref[...])
        + dot_nt(gtri[2, :, here], wv_ref[...])
    )

    @pl.when(j == 0)
    def _():
        gn[...] = part

    @pl.when(j > 0)
    def _():
        gn[...] += part

    @pl.when(j == GROUPS - 1)
    def _():
        wide, thin = 3 * D // 4, D // 4
        for mine in range(4):

            @pl.when(e == mine)
            def _():
                at = 0
                for b in range(3):
                    first, last = max(mine * wide, b * D), min((mine + 1) * wide, (b + 1) * D)
                    if first < last:
                        quarter[:, at : at + last - first] = gtri[b, :, first - b * D : last - b * D]
                        at += last - first
                quarter[:, wide:] = alow[:, mine * thin : (mine + 1) * thin]

        flat[:, :wide] = dot_tn(n1_ref[...], quarter[:, :wide])
        flat[:, wide:] = dot_tn(mixed_ref[...], quarter[:, wide:])
        clear_spare(grad, D // n)
        put_blocks(grad, flat[...], n)
        store_blocks(grad, me, shares, stages, slice(None), D, 0)
        g = gn[...]
        unit, inverse = unit_of(sin_ref[...])
        gin = gmid_ref[...] + norm_back(g, unit, inverse, par_ref[ROW_GAIN : ROW_GAIN + 1])
        low_ref[...] = gin.astype(BF16)
        lead = column_sum(g)
        vec[0:4] = vec_h[0:4]
        vec[4:10] = vec_f[0:6]
        vec[10:11] = column_sum(gin)
        vec[11:12] = lead
        vec[12:13] = column_sum(g * unit)
        vec[13:14] = column_sum(gmid_ref[...])
        vec[14:16] = stat_a[0:2]
        vec[16:19] = stat_b[0:3]
        vec[19:24] = jnp.zeros((5, D), F32)
        vec[24:32] = hot_ref[:, :1] * lead
        packed = []
        rows = shares[0].shape[1]
        cols = SUMS * D // rows
        for i in range(SUMS):
            packed += [vec[i : i + 1, at : at + min(cols, D)] for at in range(0, D, min(cols, D))]
        group = max(cols // D, 1)
        packed = [
            packed[i] if group == 1 else jnp.concatenate(packed[i : i + group], axis=1)
            for i in range(0, len(packed), group)
        ]
        put_sums(jnp.concatenate(packed, axis=0), shares)


def padded_rows(rows):
    return -(-rows // 16) * 16


def attend_back(place, gmid, wo, q, k, v, lse, bias, n1, mixed, sin, par, wqkv, vectors, n, stages, deps=()):
    tokens = gmid.shape[0]
    rows = padded_rows(D // n)
    outs = [shaped((tokens, D), BF16)] + share_shapes(n, stages, rows, D + sum_columns(rows, n // 2))
    return call(
        functools.partial(attend_back_kernel, n=n, stages=stages),
        (place, gmid, wo, q, k, v, lse, bias, n1, mixed, sin, par, wqkv, wqkv, wqkv, *vectors),
        [scalars(), fixed((tokens, D)), by_row(WIDTH, D)]
        + [by_column(tokens, WIDTH)] * 3
        + [pl.BlockSpec((PAIRS // GROUPS, 8, tokens), lambda j: (j, 0, 0)), fixed((tokens, LANES))]
        + [fixed((tokens, D))] * 3
        + [fixed(par.shape)]
        + [by_column(D, WIDTH, first) for first in (0, GROUPS, 2 * GROUPS)]
        + [fixed(v.shape) for v in vectors],
        outs,
        out_specs=[fixed(v.shape) for v in outs],
        grid=(GROUPS,),
        scratch=[
            VMEM((3, tokens, D), BF16),
            VMEM((tokens, D), BF16),
            VMEM((tokens, D), BF16),
            VMEM((D, D), F32),
            VMEM((n, rows, D), F32),
            VMEM((tokens, D), F32),
            VMEM((SUMS, D), F32),
        ],
        vmem=room(n) + 6,
        name="attend_back",
        us=60.0,
        deps=deps,
    )


STEPS = FF // D


def feed_kernel(
    smid_ref, bias_ref, par_ref, w1_ref, w2_ref, wh_ref, ho_ref,
    n2_ref, act_ref, slope_ref, sout_ref, n3_ref, blend_ref, stat_ref, feed,
):
    j = pl.program_id(0)

    @pl.when(j == 0)
    def _():
        unit, _ = unit_of(smid_ref[...])
        n2_ref[...] = (
            unit * par_ref[ROW_GAIN + 1 : ROW_GAIN + 2] + par_ref[ROW_SHIFT + 1 : ROW_SHIFT + 2]
        ).astype(BF16)
        feed[...] = jnp.broadcast_to(par_ref[ROW_CONTRACT : ROW_CONTRACT + 1], feed.shape)

    row = par_ref[ROW_EXPAND : ROW_EXPAND + 1]
    for i in range(1, STEPS):
        row = jnp.where(j == i, par_ref[ROW_EXPAND + i : ROW_EXPAND + i + 1], row)
    h = dot_nn(n2_ref[...], w1_ref[...]) + row
    sq = h * h
    t = jnp.tanh(h * (GELU_A + (GELU_A * GELU_B) * sq))
    side = 0.5 + 0.5 * t
    act_ref[...] = (h * side).astype(BF16)
    slope_ref[...] = (
        side + (h * (0.5 - 0.5 * t * t)) * (GELU_A + (3.0 * GELU_A * GELU_B) * sq)
    ).astype(BF16)
    feed[...] += dot_nn(act_ref[...], w2_ref[...])

    @pl.when(j == STEPS - 1)
    def _():
        feed_out = feed[...]
        sout = smid_ref[...] + feed_out
        sout_ref[...] = sout
        unit, _ = unit_of(sout)
        n3_ref[...] = (
            unit * par_ref[ROW_GAIN + 2 : ROW_GAIN + 3] + par_ref[ROW_SHIFT + 2 : ROW_SHIFT + 3]
        ).astype(BF16)
        vals = dot_nt(n3_ref[...], wh_ref[...]) + ho_ref[0:1]
        l = [vals[:, q * LANES : (q + 1) * LANES] for q in range(MODEL_TALLY)]
        top = jnp.maximum(jnp.maximum(l[0], l[1]), l[2])
        p = [jnp.exp(v - top) for v in l]
        total = p[0] + p[1] + p[2]
        for q in range(MODEL_TALLY):
            blend_ref[q] = p[q] / total
        blend_ref[MODEL_TALLY] = vals[:, MODEL_TALLY * LANES :]
        valid = (bias_ref[:, :1].astype(F32) == 0.0).astype(F32)
        stat_ref[0:1] = column_sum(feed_out * feed_out * valid)
        stat_ref[1:2] = column_sum(sout * sout * valid)
        stat_ref[2:3] = jnp.broadcast_to(column_sum(valid), (1, D)) * (1.0 / D)
        stat_ref[3:8] = jnp.zeros((5, D), F32)


def feed(smid, bias, par, w1, w2, wh, ho, deps=()):
    tokens = smid.shape[0]
    outs = [
        shaped((tokens, D), BF16),
        shaped((tokens, FF), BF16),
        shaped((tokens, FF), BF16),
        shaped((tokens, D), F32),
        shaped((tokens, D), BF16),
        shaped((4, tokens, LANES), F32),
        shaped((8, D), F32),
    ]
    out_specs = [fixed(v.shape) for v in outs]
    out_specs[1] = out_specs[2] = by_column(tokens, D)
    return call(
        feed_kernel,
        (smid, bias, par, w1, w2, wh, ho),
        [fixed((tokens, D)), fixed(bias.shape), fixed(par.shape), by_column(D, D), by_row(D, D)]
        + [fixed(wh.shape), fixed(ho.shape)],
        outs,
        out_specs=out_specs,
        grid=(STEPS,),
        scratch=[VMEM((tokens, D), F32)],
        vmem=VMEM_MIB,
        name="feed",
        us=12.0,
        deps=deps,
    )


def head_back_kernel(
    place_ref, blend_ref, gw_ref, gs_ref, wh_ref, sout_ref, par_ref, act_ref,
    hlow_ref, gout_ref, vec_ref, *rest, n, stages,
):
    shares, (flow, quarter, cgrad, blocks) = rest[:-4], rest[-4:]
    e, me = place_ref[0], place_ref[1]

    def by_token(v):
        tall = jnp.concatenate([v, jnp.zeros((LANES - HEAD_ROWS, v.shape[1]), F32)], axis=0)
        return jnp.transpose(tall)

    weights = [by_token(gw_ref[q]) for q in range(MODEL_TALLY)]
    inner = 0.0
    for q in range(MODEL_TALLY):
        inner = inner + blend_ref[q] * weights[q]
    vec_ref[...] = jnp.zeros_like(vec_ref)
    for q in range(MODEL_TALLY + 1):
        cols = slice(q * LANES, (q + 1) * LANES)
        g = by_token(gs_ref[...]) if q == MODEL_TALLY else blend_ref[q] * (weights[q] - inner)
        vec_ref[0:1, cols] = column_sum(g)
        hlow_ref[:, cols] = g.astype(BF16)
    gn3 = dot_nn(hlow_ref[...], wh_ref[...])
    unit, inverse = unit_of(sout_ref[...])
    g = norm_back(gn3, unit, inverse, par_ref[ROW_GAIN + 2 : ROW_GAIN + 3])
    gout_ref[...] = g
    flow[...] = g.astype(BF16)
    vec_ref[1:2] = column_sum(gn3 * unit)
    vec_ref[2:3] = column_sum(gn3)
    vec_ref[3:4] = column_sum(g)
    thin = D // 4
    for here in range(4):

        @pl.when(e == here)
        def _():
            quarter[...] = flow[:, here * thin : (here + 1) * thin]

    size, rows = FF // n, D // n
    clear_spare(blocks, rows)
    cgrad[...] = dot_tn(quarter[...], act_ref[...])
    for d in range(n):
        for i in range(n // 4):
            part = cgrad[i * rows : (i + 1) * rows, d * size : (d + 1) * size]
            blocks[d, :rows, i * size : (i + 1) * size] = part
    store_blocks(blocks, me, shares, stages, slice(None), D, 0)


def head_back(place, blend, gw, gs, wh, sout, par, act, n, stages, deps=()):
    tokens = sout.shape[0]
    return call(
        functools.partial(head_back_kernel, n=n, stages=stages),
        (place, blend, gw, gs, wh, sout, par, act),
        [scalars()] + [whole()] * 7,
        [shaped((tokens, 4 * LANES), BF16), shaped((tokens, D), F32), shaped((8, D), F32)]
        + share_shapes(n, stages, padded_rows(D // n), D),
        scratch=[
            VMEM((tokens, D), BF16),
            VMEM((tokens, D // 4), BF16),
            VMEM((D // 4, FF), F32),
            VMEM((n, padded_rows(D // n), D), F32),
        ],
        vmem=room(n),
        name="head_back",
        us=7,
        deps=deps,
    )


def feed_back_kernel(
    place_ref, hlow_ref, gout_ref, n3_ref, par_ref, slope_ref, n2_ref, smid_ref, w1_ref, w2_ref,
    gmid_ref, vec_ref, *rest, n, stages,
):
    shares, (flow, hid, mine, gn2, grad) = rest[:-5], rest[-5:]
    j = pl.program_id(0)
    e, me = place_ref[0], place_ref[1]

    @pl.when(j == 0)
    def _():
        flow[...] = gout_ref[...].astype(BF16)
        vec_ref[...] = jnp.zeros_like(vec_ref)
        gn2[...] = jnp.zeros_like(gn2)

    h = dot_nt(flow[...], w2_ref[...]) * slope_ref[...].astype(F32)
    sums = column_sum(h)
    for i in range(STEPS):

        @pl.when(j == i)
        def _():
            vec_ref[i : i + 1] = sums

    hid[...] = h.astype(BF16)

    @pl.when(j == e)
    def _():
        mine[...] = hid[...]

    gn2[...] += dot_nt(hid[...], w1_ref[...])

    @pl.when(j == STEPS - 1)
    def _():
        clear_spare(grad, D // n)
        put_blocks(grad, dot_tn(n2_ref[...], mine[...]), n)
        store_blocks(grad, me, shares, stages, slice(None), D, 0)
        put_blocks(grad, dot_tn(n3_ref[...], hlow_ref[:, pl.ds(pl.multiple_of(e * LANES, LANES), LANES)]), n)
        store_blocks(grad, me, shares, stages, slice(None), LANES, D)
        unit, inverse = unit_of(smid_ref[...])
        y = gn2[...]
        gmid_ref[...] = gout_ref[...] + norm_back(y, unit, inverse, par_ref[ROW_GAIN + 1 : ROW_GAIN + 2])
        vec_ref[4:5] = column_sum(y * unit)
        vec_ref[5:6] = column_sum(y)


def feed_back(place, hlow, gout, n3, par, slope, n2, smid, w1, w2, n, stages, deps=()):
    tokens = smid.shape[0]
    rows = padded_rows(D // n)
    outs = [shaped((tokens, D), F32), shaped((8, D), F32)] + share_shapes(n, stages, rows, D + LANES)
    return call(
        functools.partial(feed_back_kernel, n=n, stages=stages),
        (place, hlow, gout, n3, par, slope, n2, smid, w1, w2),
        [scalars()]
        + [fixed(v.shape) for v in (hlow, gout, n3, par)]
        + [by_column(tokens, D), fixed(n2.shape), fixed(smid.shape), by_column(D, D), by_row(D, D)],
        outs,
        out_specs=[fixed(v.shape) for v in outs],
        grid=(STEPS,),
        scratch=[
            VMEM((tokens, D), BF16),
            VMEM((tokens, D), BF16),
            VMEM((tokens, D), BF16),
            VMEM((tokens, D), F32),
            VMEM((n, rows, D), F32),
        ],
        vmem=room(n),
        name="feed_back",
        us=13.0,
        deps=deps,
    )


def fold_kernel(*refs, counts, parts, axis):
    outs = refs[sum(counts) :]
    ins, at = 0, 0
    for g, count in enumerate(counts):
        total = refs[ins][...].astype(F32)
        for i in range(1, count):
            total = total + refs[ins + i][...].astype(F32)
        ins += count
        size = total.shape[0] // parts
        for p in range(parts):
            piece = total[p * size : (p + 1) * size].astype(outs[p].dtype)
            if axis is None:
                outs[g * parts + p][...] = piece
            elif axis == 1:
                outs[p][:, at : at + piece.shape[1]] = piece
            else:
                outs[p][:, :, at : at + piece.shape[2]] = piece
        if axis is not None:
            at += total.shape[axis]


def fold(groups, parts, axis=None, deps=()):
    shapes = [g[0].shape for g in groups]
    dtype = groups[0][0].dtype
    size = shapes[0][0] // parts
    if axis is None:
        outs = [shaped((size,) + v[1:], dtype) for v in shapes for _ in range(parts)]
    else:
        full = list(shapes[0])
        full[0], full[axis] = size, sum(v[axis] for v in shapes)
        outs = [shaped(tuple(full), dtype)] * parts
    inputs = [v for g in groups for v in g]
    return call(
        functools.partial(fold_kernel, counts=[len(g) for g in groups], parts=parts, axis=axis),
        inputs,
        [whole()] * len(inputs),
        outs,
        name="fold",
        us=1.3,
        deps=deps,
    )


def fold_sums_kernel(*refs, first, parts):
    sums = refs[0:2]
    before = refs[2:4] if first else ()
    outs = refs[2 + len(before) :]
    count, rows, cols = sums[0].shape
    size = sum_columns(rows, count)
    vec = get_sums(sums[0][:, :, cols - size :]) + get_sums(sums[1][:, :, cols - size :])
    at = 0
    for pair in (before, sums):
        if pair:
            total = pair[0][...].astype(F32) + pair[1][...].astype(F32)
            wide = total.shape[2] - (size if pair is sums else 0)
            for p in range(parts):
                half = total[p * (count // parts) : (p + 1) * (count // parts), :, :wide]
                outs[p][:, :, at : at + wide] = half.astype(BF16)
            at += wide
    if parts == 1:
        outs[1][...] = vec
    else:
        put_sums(vec, outs[:parts])


def fold_sums(keep, got, parts, first=None, deps=()):
    count, rows, cols = keep.shape
    wide = cols - sum_columns(rows, count) + (first[0].shape[2] if first else 0)
    if parts == 1:
        outs = [shaped((1, rows, wide), BF16), shaped((rows, SUMS * D // rows), F32)]
    else:
        outs = [shaped((count // parts, rows, wide + sum_columns(rows, count // parts)), BF16)] * parts
    inputs = [keep, got] + (list(first) if first else [])
    return call(
        functools.partial(fold_sums_kernel, first=bool(first), parts=parts),
        inputs,
        [whole()] * len(inputs),
        outs,
        name="fold_sums",
        us=1.3,
        deps=deps,
    )


def assemble_kernel(place_ref, *refs, n):
    parts = refs[0:4]
    contract, expand, head, triple, result = refs[4:]
    e = place_ref[0]
    rows, size, thin, wide = D // n, FF // n, D // 4, 3 * D // 4
    last = 2 * D + LANES
    for here in range(4):

        @pl.when(e == here)
        def _():
            for i in range(4):
                part = parts[here ^ i]
                for j in range(n // 4):
                    block = jnp.transpose(part[0, :, j * size : (j + 1) * size].astype(F32))
                    contract[:, i * thin + j * rows : i * thin + (j + 1) * rows] = block[:, :rows]
                expand[:, i * D : (i + 1) * D] = part[0, :rows, D : 2 * D].astype(F32)
                head[:, i * CHANNELS : (i + 1) * CHANNELS] = part[0, :rows, 2 * D : 2 * D + CHANNELS].astype(F32)
                triple[:, i * wide : (i + 1) * wide] = part[0, :rows, last : last + wide].astype(F32)
                result[:, i * thin : (i + 1) * thin] = part[0, :rows, last + wide :].astype(F32)


def assemble(place, parts, n, deps=()):
    rows = D // n
    return call(
        functools.partial(assemble_kernel, n=n),
        (place, *parts),
        [scalars()] + [whole()] * 4,
        [
            shaped((FF // n, D), F32),
            shaped((rows, FF), F32),
            shaped((rows, 4 * CHANNELS), F32),
            shaped((rows, 3 * D), F32),
            shaped((rows, D), F32),
        ],
        name="assemble",
        us=2.5,
        deps=deps,
    )


def assemble_last_kernel(place_ref, p0, p1, p2, p3, lift, *, step, width):
    parts = (p0, p1, p2, p3)
    e = place_ref[0]
    for here in range(4):

        @pl.when(e == here)
        def _():
            for i in range(4):
                take = step if i < 3 else width
                lift[i * step : i * step + take] = parts[here ^ i][0, :take].astype(F32)


def assemble_last(place, parts, step, width, deps=()):
    return call(
        functools.partial(assemble_last_kernel, step=step, width=width),
        (place, *parts),
        [scalars()] + [whole()] * 4,
        shaped((3 * step + width, D), F32),
        name="assemble_last",
        us=2,
        deps=deps,
    )


THIRD = CHANNELS // 3


def channel_sums(pred_ref, adj_ref, first, channels, at, gw_ref, gs_ref):
    for i in range(channels):
        here = slice((first + i) * PIXELS, (first + i + 1) * PIXELS)
        adj = adj_ref[i * PIXELS : (i + 1) * PIXELS].astype(F32)
        gw_ref[first + i : first + i + 1, at] = column_sum(adj * pred_ref[here, at].astype(F32))
        gs_ref[first + i : first + i + 1, at] = column_sum(adj)


def weigh_near_kernel(place_ref, pred_ref, a0, a1, gw_ref, gs_ref):
    e = place_ref[0]
    rows = a0.shape[1]
    gw_ref[CHANNELS:] = jnp.zeros_like(gw_ref[CHANNELS:])
    gs_ref[CHANNELS:] = jnp.zeros_like(gs_ref[CHANNELS:])
    for k, a in enumerate((a0, a1)):
        at = pl.ds(pl.multiple_of((e ^ k) * rows, rows), rows)
        channel_sums(pred_ref, a, 0, CHANNELS, at, gw_ref, gs_ref)


def weigh_near(place, pred, adjoints, deps=()):
    tokens = pred.shape[1]
    return call(
        weigh_near_kernel,
        (place, pred, *adjoints),
        [scalars()] + [whole()] * 3,
        [shaped((HEAD_ROWS, tokens), F32)] * 2,
        name="weigh_near",
        us=3.6,
        deps=deps,
    )


def weigh_far_kernel(place_ref, pred_hbm, a2, a3, gw_in, gs_in, gw_ref, gs_ref, pred, sem):
    e = place_ref[0]
    rows = a2.shape[1]
    at = pl.ds(pl.multiple_of((e // 2) * 2 * rows, 2 * rows), 2 * rows)
    pair = pl.ds(pl.multiple_of((1 - e // 2) * 2 * rows, 2 * rows), 2 * rows)
    load = pltpu.make_async_copy(pred_hbm.at[:, pair], pred, sem)
    load.start()
    gw_ref[:, at] = gw_in[:, at]
    gs_ref[:, at] = gs_in[:, at]
    gw_ref[CHANNELS:, pair] = jnp.zeros((HEAD_ROWS - CHANNELS, 2 * rows), F32)
    gs_ref[CHANNELS:, pair] = jnp.zeros((HEAD_ROWS - CHANNELS, 2 * rows), F32)
    load.wait()
    for k, adj_ref in ((2, a2), (3, a3)):
        token = e ^ k
        own = pl.ds(pl.multiple_of(token * rows, rows), rows)
        inner = pl.ds(pl.multiple_of((token & 1) * rows, rows), rows)
        for i in range(CHANNELS):
            here = slice(i * PIXELS, (i + 1) * PIXELS)
            adj = adj_ref[here].astype(F32)
            gw_ref[i : i + 1, own] = column_sum(adj * pred[here, inner].astype(F32))
            gs_ref[i : i + 1, own] = column_sum(adj)


def weigh_far(place, pred, adjoints, gw, gs, deps=()):
    tokens = pred.shape[1]
    return call(
        weigh_far_kernel,
        (place, pred, *adjoints, gw, gs),
        [scalars(), in_hbm()] + [whole()] * 4,
        [shaped((HEAD_ROWS, tokens), F32)] * 2,
        scratch=[VMEM((TILE_ENTRIES, tokens // 2), BF16), pltpu.SemaphoreType.DMA],
        vmem=VMEM_MIB,
        name="weigh_far",
        us=2,
        deps=deps,
    )


def split_two(v, axis=0):
    hi = v.astype(BF16)
    return jnp.concatenate([hi, (v - hi.astype(F32)).astype(BF16)], axis=axis)


def by_rows(refs):
    pieces = [(0, refs[0], 0), (1, refs[1], 0)]
    for k in (2, 3):
        first = 0
        for ref in refs[2 + 3 * (k - 2) : 5 + 3 * (k - 2)]:
            pieces.append((k, ref, first))
            first += ref.shape[0]
    return pieces


def blend_kernel(place_ref, blend_ref, *rest):
    columns, spread_ref, outs, acc = rest[:8], rest[8], rest[9:13], rest[13]
    e = place_ref[0]
    rows = outs[0].shape[1]
    acc[...] = dot_nn(
        jnp.concatenate([spread_ref[...]] * 2, axis=1), split_two(jnp.transpose(blend_ref[MODEL_TALLY]))
    )
    for k, c, first in by_rows(columns):
        q = e ^ k

        @pl.when(q < MODEL_TALLY)
        def _():
            at = slice(first, first + c.shape[0])
            spread = jnp.concatenate([spread_ref[at]] * 2, axis=1)
            acc[at] += dot_nn(spread, split_two(jnp.transpose(blend_ref[q]))) * c[...].astype(F32)

    for k, o in enumerate(outs):
        at = pl.multiple_of((e ^ k) * rows, rows)
        o[...] = acc[:, pl.ds(at, rows)].astype(BF16)


def blend_columns(place, blend, columns, spread, deps=()):
    cols, tokens = columns[0].shape
    rows = tokens // 4
    return call(
        blend_kernel,
        (place, blend, *columns, spread),
        [scalars()] + [whole()] * 10,
        [shaped((cols, rows), BF16)] * 4,
        scratch=[VMEM((cols, tokens), F32)],
        name="blend",
        us=5,
        deps=deps,
    )


def lift_grad_kernel(place_ref, low_ref, masks_ref, *rest, n, stages):
    columns, shares, grad = rest[:8], rest[8:-1], rest[-1]
    e, me = place_ref[0], place_ref[1]
    masks = jnp.transpose(masks_ref[...])
    low = low_ref[...].astype(F32)
    rows = grad.shape[1]
    grad[...] = jnp.zeros_like(grad)
    for k, c, first in by_rows(columns):

        @pl.when((e ^ k) < MODEL_TALLY)
        def _():
            part = dot_nn(c[...], (low * masks[:, k : k + 1]).astype(BF16))
            for i in range(c.shape[0] // rows):
                grad[first // rows + i] += part[i * rows : (i + 1) * rows]

    store_blocks(grad, me, shares, stages, slice(None), D, 0)


def lift_grad(place, low, masks, columns, n, stages, deps=()):
    cols, tokens = columns[0].shape
    rows = cols // n
    return call(
        functools.partial(lift_grad_kernel, n=n, stages=stages),
        (place, low, masks, *columns),
        [scalars()] + [whole()] * 10,
        share_shapes(n, stages, rows, D),
        scratch=[VMEM((n, rows, D), F32)],
        vmem=room(n),
        name="lift_grad",
        us=30,
        deps=deps,
    )


def slope_kernel(place_ref, low_ref, masks_ref, blend_ref, lift_ref, a0, a1, a2, a3, *rest, which):
    out_ref, acc = rest[-2], rest[-1]
    e = place_ref[0]
    rows = a0.shape[1]
    masks = jnp.transpose(masks_ref[...])
    low = (low_ref[...].astype(F32) * masks[:, :1]).astype(BF16)
    active = jnp.where(e < MODEL_TALLY, 1.0, 0.0)
    weights = jnp.transpose(blend_ref[jnp.minimum(e, MODEL_TALLY - 1)] * active)
    acc[...] = dot_nt(lift_ref[...], low)
    first = which * THIRD
    for k, a in enumerate((a0, a1, a2, a3)):
        for b in range(4):

            @pl.when((e ^ k) == b)
            def _():
                at = slice(b * rows, (b + 1) * rows)
                for i in range(THIRD):
                    here = slice(i * PIXELS, (i + 1) * PIXELS)
                    weight = weights[first + i : first + i + 1, at]
                    out_ref[here, at] = (acc[here, at] + weight * a[here].astype(F32)).astype(BF16)


def slope(which, before, place, low, masks, blend, lift, adjoints, deps=()):
    tokens = low.shape[0]
    rows = adjoints[0].shape[1]
    size = THIRD * PIXELS
    third = lambda cols: pl.BlockSpec((size, cols), lambda j: (which, 0))
    inputs = [place, low, masks, blend, lift, *adjoints]
    in_specs = [scalars(), fixed((tokens, D)), fixed(masks.shape), fixed(blend.shape), third(D)]
    in_specs += [third(rows)] * 4
    aliases = {}
    if before is not None:
        aliases = {len(inputs): 0}
        inputs.append(before)
        in_specs.append(in_hbm())
    return call(
        functools.partial(slope_kernel, which=which),
        inputs,
        in_specs,
        shaped((TILE_ENTRIES, tokens), BF16),
        grid=(1,),
        out_specs=third(tokens),
        scratch=[VMEM((size, tokens), F32)],
        aliases=aliases,
        name="slope",
        us=4.3,
        deps=deps,
    )


def expert_swap(v, k):
    size = lax.axis_size("expert")
    return lax.ppermute(v, "expert", [(i, i ^ k) for i in range(size)])


def frame_swap(v, k):
    size = lax.axis_size("dp")
    return lax.ppermute(v, "dp", [(i, i ^ k) for i in range(size)])


def gather_four(v):
    across = expert_swap(v, 2)
    return [v, expert_swap(v, 1), across, expert_swap(across, 1)]


def in_order(parts, e):
    odd = (e & 1) == 1
    high = (e & 2) == 2
    a, b, c, d = parts
    a, b, c, d = (
        jnp.where(odd, b, a),
        jnp.where(odd, a, b),
        jnp.where(odd, d, c),
        jnp.where(odd, c, d),
    )
    return [jnp.where(high, c, a), jnp.where(high, d, b), jnp.where(high, a, c), jnp.where(high, b, d)]


def local(
    model_predictions,
    member_tile_presence,
    piece_usable_flags,
    horizon_positions,
    result_adjoint,
    tile_lift_matrix,
    tile_lift_offset,
    horizon_lookup,
    normalizer_scales,
    normalizer_offsets,
    query_key_value_matrix,
    attend_result_matrix,
    attend_offset_vector,
    expand_matrix,
    expand_offset,
    contract_matrix,
    contract_offset,
    mixing_head_matrix,
    mixing_head_offset,
):
    n = lax.axis_size("dp")
    e = lax.axis_index("expert")
    place = jnp.stack([e, lax.axis_index("dp")]).astype(jnp.int32)
    core = e & 1
    active = (e < MODEL_TALLY).astype(F32)
    pred = jnp.transpose(model_predictions[0])
    tokens = pred.shape[1]
    block = TILE_ENTRIES // n
    step = block // 4 // 8 * 8 if block % 8 == 0 else block // 4
    width = block - 3 * step
    padded = padded_rows(width)

    adjoint = jnp.transpose(result_adjoint)
    near = expert_swap(adjoint, 1)
    far = expert_swap(adjoint, 2)

    mask = member_tile_presence.astype(F32) * active
    own_part, other_part, _ = embed(place, mask, pred, tile_lift_matrix)

    info = jnp.concatenate([mask, piece_usable_flags.astype(F32)[None]], axis=1)
    infos = [info] + [expert_swap(info, k) for k in (1, 2, 3)]
    masks = jnp.concatenate([v[:, :tokens] for v in infos] + [jnp.zeros((4, tokens), F32)], axis=0)
    valid = jnp.concatenate([v[0, tokens:] for v in in_order(infos, e)])
    first = jnp.arange(LANES) == 0
    bias = jnp.where((valid[:, None] == 0) & first[None, :], MASKED_SCORE, 0.0).astype(BF16)

    lead_hot = (jnp.arange(horizon_lookup.shape[0]) == horizon_positions[0]).astype(F32)
    lead_vector = jnp.sum(lead_hot[:, None] * horizon_lookup.astype(F32), axis=0)
    par = jnp.concatenate(
        [
            tile_lift_offset[None].astype(F32),
            normalizer_scales.astype(F32),
            normalizer_offsets.astype(F32),
            attend_offset_vector[None].astype(F32),
            contract_offset[None].astype(F32),
            expand_offset.reshape(FF // D, D).astype(F32),
            lead_vector[None],
            jnp.zeros((PARAM_ROWS - ROW_HEAD, D), F32),
        ],
        axis=0,
    )
    over = (0, LANES - CHANNELS)
    head = jnp.pad(jnp.transpose(mixing_head_matrix).reshape(4, CHANNELS, D), ((0, 0), over, (0, 0)))
    head = head.reshape(4 * LANES, D)
    head_row = jnp.pad(mixing_head_offset.astype(F32).reshape(1, 4, CHANNELS), ((0, 0), (0, 0), over))
    head_row = head_row.reshape(1, 4 * LANES)
    at = jnp.arange(n * padded)
    channel = ((at // padded) * block + e * step + at % padded) // PIXELS
    spread = (channel[:, None] == jnp.arange(LANES)[None, :]).astype(BF16)

    pair, done = fold([[own_part, expert_swap(other_part, 1)]], 1)
    other = expert_swap(own_part, 1)
    across = expert_swap(pair, 2)
    across_other = expert_swap(across, 1)

    mine, grad_shift, done = weigh_near(place, pred, [adjoint, near], deps=[done, par, bias, head, head_row, spread, masks])
    *pieces, far, done = pack(place, pred, far, n, step, width, padded, deps=[done, across])
    far_near = expert_swap(far, 1)
    adjoints = [adjoint, near, far, far_near]
    sin, n1, queries, keys, values, mixed, smid, lse, stat_a, done = attend(
        place, pair, other_part, other, across, across_other, bias, par, query_key_value_matrix, attend_result_matrix, deps=[done]
    )
    columns = [pieces[0], expert_swap(pieces[1], 1)] + [expert_swap(v, 2 + i // 3) for i, v in enumerate(pieces[2:])]
    mine, grad_shift, done = weigh_far(
        place, pred, adjoints[2:], mine, grad_shift, deps=[done, columns[1], columns[2], columns[5]]
    )
    all_mine = [mine] + [expert_swap(mine, k) for k in (1, 2, 3)]
    n2, act, gelu_slope, sout, n3, blend, stat_b, done = feed(
        smid, bias, par, expand_matrix, contract_matrix, head, head_row, deps=[done]
    )
    grad_weights = jnp.stack(in_order(all_mine, e)[:MODEL_TALLY])

    stages = stages_of(n)
    last_bit = len(stages) - 1

    def onward(keep, got, bit, deps):
        keep, send, done = fold([[keep, got]], 2, deps=deps)
        return keep, frame_swap(send, 1 << bit), done

    hlow, gout, vec_h, ckeep, csend, done = head_back(
        place, blend, grad_weights, grad_shift, head, sout, par, act, n, stages, deps=[done]
    )
    cgot = frame_swap(csend, 1)
    gmid, vec_f, tkeep, tsend, done = feed_back(
        place, hlow, gout, n3, par, gelu_slope, n2, smid, expand_matrix, contract_matrix, n, stages,
        deps=[done, columns[3]],
    )
    tgot = frame_swap(tsend, 1)
    hot = jnp.broadcast_to(lead_hot[:, None], (lead_hot.shape[0], LANES))
    low, qkeep, qsend, done = attend_back(
        place, gmid, attend_result_matrix, queries, keys, values, lse, bias, n1, mixed, sin, par,
        query_key_value_matrix, [vec_h, vec_f, stat_a, stat_b, hot], n, stages, deps=[done, cgot, columns[6]],
    )
    qgot = frame_swap(qsend, 1)
    keep, send, done = fold([[ckeep, cgot], [tkeep, tgot]], 2, axis=2, deps=[done])
    got = frame_swap(send, 2)
    akeep, asend, done = lift_grad(place, low, masks, columns, n, stages, deps=[done])
    agot = frame_swap(asend, 1)
    slopes = [place, low, masks, blend, tile_lift_matrix, adjoints]
    *outgoing, done = blend_columns(place, blend, columns, spread, deps=[done])
    arrived = [outgoing[0]] + [expert_swap(outgoing[k], k) for k in (1, 2, 3)]
    part_slope, done = slope(0, None, *slopes, deps=[done])
    keep, got, done = onward(keep, got, 2, [done])
    qkeep, qsend, done = fold_sums(qkeep, qgot, 2, deps=[done])
    qgot = frame_swap(qsend, 2)
    part_slope, done = slope(1, part_slope, *slopes, deps=[done])
    combined, done = unpack(place, arrived, n, step, width, padded, deps=[done])
    combined_prediction = jnp.transpose(combined)
    qkeep, qsend, done = fold_sums(qkeep, qgot, 2, deps=[done])
    qgot = frame_swap(qsend, 4)
    akeep, agot, done = onward(akeep, agot, 1, [done])
    part_slope, done = slope(2, part_slope, *slopes, deps=[done])
    for bit in range(3, last_bit + 1):
        keep, got, done = onward(keep, got, bit, [done])
        qkeep, qsend, done = fold_sums(qkeep, qgot, 2, deps=[done])
        qgot = frame_swap(qsend, 1 << bit)
    rows_one, packed, done = fold_sums(qkeep, qgot, 1, first=[keep, got], deps=[done])
    rows_across = expert_swap(rows_one, 2)
    rows_near = expert_swap(rows_one, 1)
    packed = packed.reshape(SUMS, D)
    for bit in range(2, last_bit + 1):
        akeep, agot, done = onward(akeep, agot, bit, [done])
    rows_across, done = fold([[rows_across]], 1, deps=[done])
    rows_one = [rows_one, rows_near, rows_across, expert_swap(rows_across, 1)]
    contract_slope, expand_slope, head_slope, triple_slope, result_slope, done = assemble(
        place, rows_one, n, deps=[done]
    )
    rows_two, done = fold([[akeep, agot]], 1, deps=[done])
    lift_slope, _ = assemble_last(place, gather_four(rows_two), step, width, deps=[done])
    predictions_slope = jnp.transpose(part_slope)[None]

    head_off = packed[0, : 4 * LANES].reshape(4, LANES)[:, :CHANNELS].reshape(4 * CHANNELS)
    total = jnp.sum(packed[14:19], axis=1)
    magnitudes = jnp.sqrt(total[:4] / (total[4] * D) + SQUARE_EPSILON)
    gains = jnp.stack([packed[12], packed[8], packed[1]])
    shifts = jnp.stack([packed[11], packed[9], packed[2]])
    return (
        combined_prediction,
        predictions_slope,
        magnitudes,
        lift_slope,
        packed[10],
        packed[24:32],
        gains,
        shifts,
        triple_slope,
        result_slope,
        packed[13],
        expand_slope,
        packed[4:8].reshape(FF),
        contract_slope,
        packed[3],
        head_slope,
        head_off,
    )


def solution(mesh):
    rows = P(("dp", "expert"), None)
    placed = (
        P("expert", "dp", None),
        P("expert", "dp"),
        P(("dp", "expert")),
        P("dp"),
        rows,
    ) + (P(),) * 14
    given = (
        rows,
        P("expert", "dp", None),
        P(),
        P("dp", None),
        P(),
        P(),
        P(),
        P(),
        P("dp", None),
        P("dp", None),
        P(),
        P("dp", None),
        P(),
        P("dp", None),
        P(),
        P("dp", None),
        P(),
    )
    return jax.shard_map(local, mesh=mesh, in_specs=placed, out_specs=given, check_vma=False)
```
